32 devices in a mesh: rows: 4 (over x, core), state: 8 (over z, y).
Axes of the slice: x: 2, y: 2, z: 4, core: 2. Of those that a mesh axis runs over, the one named last changes fastest.
Arguments:
- hidden_in: bfloat16 [16384, 2048], P('rows'), may hold values from -64 to 64
- starts: int32 [16384], P('rows'), may hold values 0 or 1
- cotangent: bfloat16 [16384, 2048], P('rows', 'state'), may hold values from -6 to 6
- norm_gain: float32 [2048], replicated, may hold values from 0.1 to 1.9
- w_zx: bfloat16 [2048, 2, 4096], P(None, None, 'state'), may hold values from -3 to 3
- w_dt: bfloat16 [2048, 64], P(None, 'state'), may hold values from -0.125 to 0.125
- w_bc: bfloat16 [2048, 2, 128], P(None, None, 'state'), may hold values from -0.125 to 0.125
- conv_x_w: float32 [4, 4096], P(None, 'state'), may hold values from -3 to 3
- conv_x_b: float32 [4096], P('state'), may hold values from -0.5 to 0.5
- conv_bc_w: float32 [4, 2, 128], P(None, None, 'state'), may hold values from -3 to 3
- conv_bc_b: float32 [2, 128], P(None, 'state'), may hold values from -0.5 to 0.5
- dt_bias: float32 [64], P('state'), may hold values from -7 to -1
- a_log: float32 [64], P('state'), may hold values from 0 to 2.7
- d_skip: float32 [64], P('state'), may hold values from 0.5 to 1.5
- gnorm_w: float32 [4096], P('state'), may hold values from 0.1 to 1.9
- w_out: bfloat16 [4096, 2048], P('state'), may hold values from -0.09375 to 0.09375
Outputs:
- output: bfloat16 [16384, 2048], P('rows', 'state')
- grad_input: float32 [16384, 2048], P('rows', 'state')
- grad_norm_gain: float32 [2048], P('state')
- grad_w_zx: float32 [2048, 2, 4096], P(None, None, 'state')
- grad_w_dt: float32 [2048, 64], P(None, 'state')
- grad_w_bc: float32 [2048, 2, 128], P(None, None, 'state')
- grad_conv_x_w: float32 [4, 4096], P(None, 'state')
- grad_conv_x_b: float32 [4096], P('state')
- grad_conv_bc_w: float32 [4, 2, 128], P(None, None, 'state')
- grad_conv_bc_b: float32 [2, 128], P(None, 'state')
- grad_dt_bias: float32 [64], P('state')
- grad_a_log: float32 [64], P('state')
- grad_d_skip: float32 [64], P('state')
- grad_gnorm_w: float32 [4096], P('state')
- grad_w_out: float32 [4096, 2048], P('state')
The draws below stay inside these ranges and needn't reach their ends.
All inputs are finite; a program needn't handle non-finite values. No bound on the sum of `starts` on one device may be relied on, other than what follows from the above.
Results may differ from the reference program's by a relative error of at most 0.009.
Values may be sent and summed in bfloat16 or wider, within the bound.
No kernel may reach another device: no remote copies, remote signals or barrier semaphores. Data moves between devices by JAX's collectives and lax.ppermute only.
A program may use at most 384 MiB of HBM per device.

```python
import math
import jax
import jax.numpy as jnp
from jax import lax

D = 2048
NH = 64
HD = 64
DI = 4096
NS = 128
KCONV = 4
BLOCK = 256
LEN = 2048
TOKENS = 16384


def draw_hidden_in(key, part):
    key = jax.random.fold_in(key, 11)
    subkeys = jax.random.split(key, 3)
    position = jnp.arange(D, dtype=jnp.float32) / (D - 1)
    column_scale = 10.0 ** (0.5 * position + 0.5 * jax.random.uniform(subkeys[0], (D,))) / 3.2
    pattern = jnp.clip(jax.random.normal(subkeys[1], (TOKENS, D)), -6.0, 6.0)
    row_scale = jnp.exp(jax.random.uniform(subkeys[2], (TOKENS, 1), minval=math.log(0.3), maxval=math.log(3.0)))
    values = pattern * column_scale * row_scale
    return values.astype(jnp.bfloat16)


def draw_w_zx(key, part):
    key = jax.random.fold_in(key, 12)
    subkeys = jax.random.split(key, 2)
    position = jnp.arange(NH, dtype=jnp.float32) / (NH - 1)
    head_scale = 10.0 ** (0.5 * position + 0.5 * jax.random.uniform(subkeys[0], (NH,))) / 3.2
    lane_scale = jnp.stack([jnp.ones((NH * HD,), jnp.float32), jnp.repeat(head_scale, HD)])
    pattern = jnp.clip(jax.random.normal(subkeys[1], (D, 2, NH * HD)), -6.0, 6.0)
    return (pattern * lane_scale / math.sqrt(D)).astype(jnp.bfloat16)


def touch_ends(array, stream_key, least, largest):
    extent = array.shape
    place = [jax.random.randint(jax.random.fold_in(stream_key, axis), (), 0, extent[axis]) for axis in range(len(extent))]
    array = array.at[tuple(place)].set(least)
    longest = extent.index(max(extent))
    place[longest] = (place[longest] + 1) % extent[longest]
    return array.at[tuple(place)].set(largest)


def block_scale(own_key, shape, shards, least, high):
    def one(dim, blocks):
        draws = jax.random.uniform(jax.random.fold_in(jax.random.fold_in(own_key, 6), dim), (blocks,), jnp.float32, least / len(shards), high / len(shards))
        return jnp.repeat(jnp.exp(draws), shape[dim] // blocks).reshape((-1,) + (1,) * (len(shape) - dim - 1))

    factor_of = one(*shards[0])
    for cut in shards[1:]:
        factor_of = factor_of * one(*cut)
    return factor_of


def normal_values(own_key, shape, scale, bound, shards=(), kind=jnp.bfloat16):
    loudness = block_scale(own_key, shape, shards, -0.22, 0.18) if shards else 1.0
    drawn = jax.random.normal(own_key, shape, jnp.float32) * scale * loudness
    return jnp.minimum(jnp.maximum(drawn, -bound), bound).astype(kind)


def setup_inputs(seed: int = 0) -> dict:
    splits = jax.random.split(jax.random.key(seed), 17)
    return {
        "hidden_in": draw_hidden_in(jax.random.fold_in(splits[16], 71), 0),
        "starts": touch_ends((jax.random.randint(splits[1], (TOKENS,), 0, 300) < 1).astype(jnp.int32), jax.random.fold_in(splits[1], 1), 0, 1),
        "cotangent": normal_values(splits[2], (TOKENS, D), 1.0, 6.0, ((0, 4), (1, 8))),
        "norm_gain": jnp.clip(1.0 + 0.18 * jax.random.normal(splits[3], (D,), jnp.float32), 0.1, 1.9),
        "w_zx": draw_w_zx(jax.random.fold_in(splits[16], 71), 0),
        "w_dt": normal_values(splits[5], (D, NH), D ** -0.5, 0.125, ((1, 8),)),
        "w_bc": normal_values(splits[6], (D, 2, NS), D ** -0.5, 0.125, ((2, 8),)),
        "conv_x_w": normal_values(splits[7], (KCONV, DI), KCONV ** -0.5, 3.0, ((1, 8),), jnp.float32),
        "conv_x_b": jnp.clip(jax.random.uniform(splits[8], (DI,), jnp.float32, -0.5, 0.5) * block_scale(splits[8], (DI,), ((0, 8),), -0.4, 0.0), -0.5, 0.5),
        "conv_bc_w": normal_values(splits[9], (KCONV, 2, NS), KCONV ** -0.5, 3.0, ((2, 8),), jnp.float32),
        "conv_bc_b": jnp.clip(jax.random.uniform(splits[10], (2, NS), jnp.float32, -0.5, 0.5) * block_scale(splits[10], (2, NS), ((1, 8),), -0.4, 0.0), -0.5, 0.5),
        "dt_bias": jnp.clip(-7.0 + 6.0 * jax.random.uniform(splits[11], (NH,), jnp.float32) ** block_scale(splits[11], (NH,), ((0, 8),), -0.2, 0.2), -7.0, -1.0),
        "a_log": jnp.clip(2.7 * jax.random.uniform(splits[12], (NH,), jnp.float32) ** block_scale(splits[12], (NH,), ((0, 8),), -0.2, 0.2), 0.0, 2.7),
        "d_skip": jnp.clip(0.5 + 1.0 * jax.random.uniform(splits[13], (NH,), jnp.float32) ** block_scale(splits[13], (NH,), ((0, 8),), -0.2, 0.2), 0.5, 1.5),
        "gnorm_w": jnp.clip(1.0 + 0.18 * jax.random.normal(splits[14], (DI,), jnp.float32), 0.1, 1.9),
        "w_out": normal_values(splits[15], (DI, D), DI ** -0.5, 0.09375, ((0, 8),)),
    }


HIGHEST = lax.Precision.HIGHEST
EPSILON = 1e-05

@jax.custom_vjp
def low(v):
    return lax.optimization_barrier(v.astype(jnp.bfloat16)).astype(jnp.float32)

@jax.custom_vjp
def low_back(v):
    return v

def low_keep(v):
    return (low(v), None)

def low_pass(kept, grad):
    return (grad,)

def back_keep(v):
    return (v, None)

def back_low(kept, grad):
    return (low(grad),)
low.defvjp(low_keep, low_pass)
low_back.defvjp(back_keep, back_low)

def causal_conv(values, kernel, offset, doc_ids):
    taps = kernel.shape[0]
    summed = offset + kernel[taps - 1] * values
    ones_tail = (1,) * (values.ndim - 2)
    for lag_steps in range(1, taps):
        lagged = jnp.concatenate([jnp.zeros_like(values[:, :lag_steps]), values[:, :-lag_steps]], axis=1)
        lag_ids = jnp.concatenate([jnp.full_like(doc_ids[:, :lag_steps], -1), doc_ids[:, :-lag_steps]], axis=1)
        same_doc = (lag_ids == doc_ids).astype(values.dtype).reshape(doc_ids.shape + ones_tail)
        summed = summed + kernel[taps - 1 - lag_steps] * lagged * same_doc
    return summed

def block_step(carry_state, block):
    inflow, log_rate, b_rows, c_rows, doc_ids, start_rows = block
    block_len = log_rate.shape[1]
    running = jnp.cumsum(log_rate, axis=1)
    places = jnp.arange(block_len)
    within = (doc_ids[:, :, None] == doc_ids[:, None, :]) & (places[:, None] >= places[None, :])[None]
    within_mask = within.astype(log_rate.dtype)[..., None]
    gaps = running[:, :, None, :] - running[:, None, :, :]
    decays = jnp.exp(jnp.where(within[..., None], gaps, 0.0)) * within_mask
    intersection = jnp.einsum('sin,sjn->sij', c_rows, b_rows, precision=HIGHEST)
    mixing = decays * intersection[..., None]
    inside = jnp.einsum('sijh,sjhp->sihp', mixing, inflow, precision=HIGHEST)
    opened = (jnp.cumsum(start_rows, axis=1) == 0).astype(log_rate.dtype)
    leading = jnp.exp(running) * opened[..., None]
    carried = jnp.einsum('sin,shnp->sihp', c_rows, carry_state, precision=HIGHEST) * leading[..., None]
    trailing = jnp.exp(running[:, -1:, :] - running) * (doc_ids == doc_ids[:, -1:]).astype(log_rate.dtype)[..., None]
    gained = jnp.einsum('sjn,sjh,sjhp->shnp', b_rows, trailing, inflow, precision=HIGHEST)
    retain = jnp.exp(running[:, -1, :]) * opened[:, -1:]
    carry_state = carry_state * retain[:, :, None, None] + gained
    return (carry_state, inside + carried)

def state_space(xvals, dt_raw, dt_bias, a_log, b_rows, c_rows, d_skip, doc_ids, start_rows, seqs, block_len):
    tok_count, head_count, head_dim = xvals.shape
    step_size = jax.nn.softplus(dt_raw + dt_bias)
    log_rate = -jnp.exp(a_log) * step_size
    inflow = xvals * step_size[..., None]
    blocks = tok_count // (seqs * block_len)

    def split(values):
        values = values.reshape((seqs, blocks, block_len) + values.shape[1:])
        return jnp.moveaxis(values, 1, 0)
    initial = jnp.zeros((seqs, head_count, b_rows.shape[1], head_dim), xvals.dtype)
    final_state, pieces = lax.scan(jax.checkpoint(block_step), initial, (split(inflow), split(log_rate), split(b_rows), split(c_rows), split(doc_ids), split(start_rows)))
    pieces = jnp.moveaxis(pieces, 0, 1).reshape(tok_count, head_count, head_dim)
    return pieces + d_skip[:, None] * xvals

def layer_forward(params, hidden, start_rows):
    norm_gain, w_zx, w_dt, w_bc, conv_x_w, conv_x_b, conv_bc_w, conv_bc_b, dt_bias, a_log, d_skip, gnorm_w, w_out = params
    seq_len = hidden.shape[0]
    scale_rows = lax.rsqrt(lax.optimization_barrier(jnp.mean(hidden * hidden, axis=-1, keepdims=True)) + EPSILON)
    normed = low(hidden * scale_rows * norm_gain)
    gate_value = low_back(jnp.einsum('td,dkc->tkc', normed, w_zx, precision=HIGHEST))
    dt_raw = low_back(jnp.dot(normed, w_dt, precision=HIGHEST))
    state_proj = low_back(jnp.einsum('td,dkn->tkn', normed, w_bc, precision=HIGHEST))
    doc_ids = jnp.cumsum(start_rows).astype(jnp.int32)[None]
    mixed_x = low(jax.nn.silu(causal_conv(gate_value[None, :, 1], conv_x_w, conv_x_b, doc_ids)[0]))
    state_rows = low(jax.nn.silu(causal_conv(state_proj[None], conv_bc_w, conv_bc_b, doc_ids)[0]))
    head_count = dt_bias.shape[0]
    xvals = mixed_x.reshape(seq_len, head_count, -1)
    scanned = state_space(xvals, dt_raw, dt_bias, a_log, state_rows[:, 0], state_rows[:, 1], d_skip, doc_ids[0], start_rows, 1, BLOCK)
    gated = scanned.reshape(seq_len, -1) * jax.nn.silu(gate_value[:, 0])
    gate_scale = lax.rsqrt(lax.optimization_barrier(jnp.mean(gated * gated, axis=-1, keepdims=True)) + EPSILON)
    normed_out = low(gated * gate_scale * gnorm_w)
    return hidden + jnp.dot(normed_out, w_out, precision=HIGHEST)

def reference(hidden_in, starts, cotangent, norm_gain, w_zx, w_dt, w_bc, conv_x_w, conv_x_b, conv_bc_w, conv_bc_b, dt_bias, a_log, d_skip, gnorm_w, w_out):
    params = tuple((item.astype(jnp.float32) for item in (norm_gain, w_zx, w_dt, w_bc, conv_x_w, conv_x_b, conv_bc_w, conv_bc_b, dt_bias, a_log, d_skip, gnorm_w, w_out)))
    seq_count = hidden_in.shape[0] // LEN
    model_dim = hidden_in.shape[1]
    hidden = hidden_in.astype(jnp.float32).reshape(seq_count, LEN, model_dim)
    cot_rows = cotangent.astype(jnp.float32).reshape(seq_count, LEN, model_dim)
    start_all = starts.reshape(seq_count, LEN)

    def per_sequence(totals, item):
        hidden_seq, start_seq, cot_seq = item
        result, pullback = jax.vjp(lambda weights, tokens: layer_forward(weights, tokens, start_seq), params, hidden_seq)
        weight_grads, token_grads = pullback(cot_seq)
        totals = jax.tree.map(jnp.add, totals, weight_grads)
        return (totals, (result.astype(jnp.bfloat16), token_grads))
    zeroed = jax.tree.map(jnp.zeros_like, params)
    totals, (outputs, token_grads) = lax.scan(per_sequence, zeroed, (hidden, start_all, cot_rows))
    return (outputs.reshape(-1, model_dim), token_grads.reshape(-1, model_dim), totals[0], totals[1], totals[2], totals[3], totals[4], totals[5], totals[6], totals[7], totals[8], totals[9], totals[10], totals[11], totals[12])
```

```python
import functools

import jax
import jax.numpy as jnp
from jax import lax
from jax.experimental import pallas as pl
from jax.experimental.pallas import tpu as pltpu
from jax.sharding import PartitionSpec as P

LEN = 2048
BLK = 256
NBLK = LEN // BLK
CHUNKS = 4
CT = LEN // CHUNKS
CB = CT // BLK
HD = 64
NS = 128
EPSILON = 1e-05
HIGHEST = lax.Precision.HIGHEST
f32 = jnp.float32
bf16 = jnp.bfloat16
VMEM_LIMIT = 56 * 1024 * 1024


def nn(a, b, **kw):
    return lax.dot_general(a, b, (((1,), (0,)), ((), ())), preferred_element_type=f32, **kw)


def nt(a, b):
    return lax.dot_general(a, b, (((1,), (1,)), ((), ())), preferred_element_type=f32)


def tn(a, b):
    return lax.dot_general(a, b, (((0,), (0,)), ((), ())), preferred_element_type=f32)


def iota(shape, dim):
    return lax.broadcasted_iota(jnp.int32, shape, dim)


def sigmoid(v):
    return 1.0 / (1.0 + jnp.exp(-v))


def fold(v):
    return v.reshape(v.shape[0] // 8, 8, v.shape[1]).sum(axis=0)


def expand(cols, off, heads):
    low = iota((cols.shape[0], 128), 1) < HD
    pieces = []
    for p in range(heads // 2):
        a = cols[:, off + 2 * p : off + 2 * p + 1]
        b = cols[:, off + 2 * p + 1 : off + 2 * p + 2]
        pieces.append(jnp.where(low, a, b))
    return jnp.concatenate(pieces, axis=1)


def quad_masks(rows):
    head = iota((rows, 4 * HD), 1) // HD
    return [head == h for h in range(4)]


def stacked(v, masks):
    zero = jnp.zeros_like(v)
    return jnp.concatenate([jnp.where(m, v, zero) for m in masks], axis=0)


def segment_sums(v, off):
    n = v.shape[1]
    pick = (iota((n, 128), 1) == iota((n, 128), 0) // HD + off).astype(bf16)
    high = v.astype(bf16)
    rest = (v - high.astype(f32)).astype(bf16)
    return nn(high, pick) + nn(rest, pick)


def conv_tile(step, x1, kern, msk, buf):
    @pl.when(step == 0)
    def _():
        buf[0:8, :] = jnp.zeros((8, buf.shape[1]), f32)

    buf[8 : 8 + BLK, :] = x1
    acc = kern[4:5, :] + kern[3:4, :] * x1
    for k in range(1, 4):
        acc = acc + kern[3 - k : 4 - k, :] * (buf[8 - k : 8 - k + BLK, :] * msk[:, k : k + 1])
    buf[0:8, :] = x1[BLK - 8 :, :]
    return acc


def project_tile(n, w, kern, msk, z, xp, a, xs, buf):
    lanes = w.shape[1] // 2
    p = nn(n, w[...])
    z[...] = p[:, :lanes]
    x1 = p[:, lanes:]
    xp[...] = x1
    acc = conv_tile(pl.program_id(0), x1, kern, msk, buf)
    a[...] = acc
    xs[...] = (acc * sigmoid(acc)).astype(bf16)


def first_kernel(which, hid, gain, w, kern, msk, normed, r, z, xp, a, xs, buf):
    x = hid[...].astype(f32)
    rr = lax.rsqrt(jnp.mean(x * x, axis=1, keepdims=True) + EPSILON)
    n = (x * rr * gain[...]).astype(bf16)
    normed[...] = n
    r[...] = jnp.broadcast_to(rr, (BLK, 128))
    project_tile(n, w, kern, msk, z, xp, a, xs, buf)


def second_kernel(normed, w, kern, msk, z, xp, a, xs, buf):
    project_tile(normed[...], w, kern, msk, z, xp, a, xs, buf)


def states_kernel(docl, normed, ws, kern, dtp, msk, bcp, bca, bc, dtr, dt, cum, cumt, buf):
    q = nt(normed[...], ws[...])
    x1 = q[:, : 2 * NS]
    bcp[...] = x1
    acc = conv_tile(pl.program_id(0), x1, kern, msk, buf)
    bca[...] = acc
    bc[...] = (acc * sigmoid(acc)).astype(bf16)
    d = q[:, 2 * NS :]
    dtr[...] = d
    v = d + dtp[0:1, :]
    e = jnp.exp(-jnp.abs(v))
    small = e * (1.0 - e * (0.5 - e * (1.0 / 3.0 - 0.25 * e)))
    step = jnp.maximum(v, 0.0) + jnp.where(e < 0.01, small, jnp.log(1.0 + e))
    lane = iota((BLK, 128), 1)
    step = jnp.where(lane < docl, step, 0.0)
    dt[...] = step
    ext = jnp.where(lane == docl, msk[:, 0:1], step * dtp[1:2, :])
    tri = (iota((BLK, BLK), 0) >= iota((BLK, BLK), 1)).astype(f32)
    c = nn(tri, ext, precision=HIGHEST)
    cum[...] = c
    cumt[...] = c.T


def block_scalars(docl, cum):
    lane = iota((BLK, 128), 1)
    doc = cum[:, docl : docl + 1]
    doc_last = cum[BLK - 1 : BLK, docl : docl + 1]
    rates = jnp.where(lane < docl, cum, 0.0)
    last = rates[BLK - 1 : BLK, :]
    lead = jnp.exp(rates) * (doc == 0.0).astype(f32)
    trail = jnp.exp(last - rates) * (doc == doc_last).astype(f32)
    retain = jnp.exp(last) * (doc_last == 0.0).astype(f32)
    return lead, trail, retain


def scan_kernel(docl, off, xs, z, bc, dt, cum, cumt, prm, y, gw, sin, pw, state):
    lanes = xs.shape[1]
    heads = lanes // HD

    @pl.when(pl.program_id(0) == 0)
    def _():
        state[...] = jnp.zeros_like(state)

    s_in = state[...]
    sin[0] = s_in
    b = bc[:, :NS]
    c = bc[:, NS:]
    cumv = cum[...]
    lead, trail, retain = block_scalars(docl, cumv)
    within = (cumv[:, docl : docl + 1] == cumt[docl : docl + 1, :]) & (
        iota((BLK, BLK), 0) >= iota((BLK, BLK), 1)
    )
    bias = jnp.where(within, 0.0, -1e30)
    g = nt(c, b)
    xf = xs[...].astype(f32)
    u = xf * expand(dt[...], off, heads)
    ub = u.astype(bf16)
    masks = quad_masks(BLK)
    parts = []
    for q in range(heads // 4):
        mixes = []
        for h in range(off + 4 * q, off + 4 * q + 4):
            decay = jnp.exp((cumv[:, h : h + 1] - cumt[h : h + 1, :]) + bias)
            mixes.append((decay * g).astype(bf16))
        uq = ub[:, q * 256 : q * 256 + 256]
        parts.append(nn(jnp.concatenate(mixes, axis=1), stacked(uq, masks)))
    yv = jnp.concatenate(parts, axis=1)
    yv = yv + nn(c, s_in.astype(bf16)) * expand(lead, off, heads) + prm[6:7, :] * xf
    y[...] = yv
    ut = (u * expand(trail, off, heads)).astype(bf16)
    state[...] = s_in * expand(retain, off, heads) + tn(b, ut)
    zz = z[...]
    gated = yv * zz * sigmoid(zz)
    gw[...] = (gated * prm[5:6, :]).astype(bf16)
    pw[...] = jnp.broadcast_to(jnp.sum(gated * gated, axis=1, keepdims=True), (BLK, 128))


def out_kernel(ga, gb, wa, wb, o):
    o[...] = (nn(ga[...], wa[...]) + nn(gb[...], wb[...])).astype(bf16)


def dyn_kernel(c, wa, wb, ga, gb, da, db, qs):
    cv = c[...]
    a = nt(cv, wa[...])
    b = nt(cv, wb[...])
    da[...] = a.astype(bf16)
    db[...] = b.astype(bf16)
    q = jnp.sum(a * ga[...].astype(f32), axis=1, keepdims=True)
    q = q + jnp.sum(b * gb[...].astype(f32), axis=1, keepdims=True)
    qs[...] = jnp.broadcast_to(q, (BLK, 128))


def gate_kernel(sq, da, db, ya, yb, za, zb, prma, prmb, dz, dy, yn, mt, gg):
    lanes = da.shape[1]
    s = sq[:, 0:1]
    kq = sq[:, 1:2]

    @pl.when(pl.program_id(0) == 0)
    def _():
        gg[...] = jnp.zeros_like(gg)

    total = jnp.zeros((BLK, 1), f32)
    for half, (dref, yref, zref, prm) in enumerate(((da, ya, za, prma), (db, yb, zb, prmb))):
        at = slice(half * lanes, half * lanes + lanes)
        dn = dref[...].astype(f32)
        y = yref[...]
        z = zref[...]
        gn = prm[5:6, :]
        sg = sigmoid(z)
        act = z * sg
        g = y * act
        gs = g * s
        yn[:, at] = (gs * gn).astype(bf16)
        gg[:, at] += fold(dn * gs)
        dg = s * (dn * gn) - g * kq
        dy[:, at] = (dg * act).astype(bf16)
        low = (dg * y * (sg * (1.0 + z * (1.0 - sg)))).astype(bf16)
        dz[:, at] = low
        total = total + jnp.sum(low.astype(f32) * z, axis=1, keepdims=True)
    mt[...] = jnp.broadcast_to(total, (BLK, 128))


def conv_back(da, xp, kern, buf, mbuf):
    dx = kern[3:4, :] * da
    taps = [None, None, None, fold(xp * da)]
    for k in range(1, 4):
        sh = buf[k : k + BLK, :] * mbuf[k : k + BLK, k : k + 1]
        dx = dx + kern[3 - k : 4 - k, :] * sh
        taps[3 - k] = fold(xp * sh)
    return dx, taps


def back_kernel(
    docl,
    dy, bc, dt, cum, cumt, dtr, msk, dtp,
    ya, yb, xsa, xsb, aa, ab, xpa, xpb, sia, sib, prma, prmb,
    ds_in, cda_in, cm_in,
    dxp, ddt, dbc, mt, acc, accs, ds, cda, cm,
    buf, mbuf,
):
    lanes = xsa.shape[1]
    heads = lanes // HD
    step = pl.program_id(0)

    @pl.when(step == 0)
    def _():
        ds[...] = ds_in[...]
        buf[:, 0:8, :] = cda_in[...]
        mbuf[0:8, :] = cm_in[...]
        acc[...] = jnp.zeros_like(acc)
        accs[...] = jnp.zeros_like(accs)

    mbuf[BLK : BLK + 8, :] = mbuf[0:8, :]
    mbuf[0:BLK, :] = msk[...]
    b = bc[:, :NS]
    c = bc[:, NS:]
    cumv = cum[...]
    lead, trail, retain = block_scalars(docl, cumv)
    within = (cumv[:, docl : docl + 1] == cumt[docl : docl + 1, :]) & (
        iota((BLK, BLK), 0) <= iota((BLK, BLK), 1)
    )
    bias = jnp.where(within, 0.0, -1e30)
    gt = nt(b, c)
    masks = quad_masks(BLK)
    dgt = jnp.zeros((BLK, BLK), f32)
    d_c = jnp.zeros((BLK, NS), f32)
    d_b = jnp.zeros((BLK, NS), f32)
    r1 = jnp.zeros((BLK, 128), f32)
    r2 = jnp.zeros((BLK, 128), f32)
    r3 = jnp.zeros((BLK, 128), f32)
    held = jnp.zeros((8, 128), f32)
    total = jnp.zeros((BLK, 1), f32)
    refs = ((ya, xsa, aa, xpa, sia, prma), (yb, xsb, ab, xpb, sib, prmb))
    for half, (yr, xsr, ar, xpr, sir, prm) in enumerate(refs):
        off = half * heads
        at = slice(half * lanes, half * lanes + lanes)
        dyb = dy[:, at]
        dyf = dyb.astype(f32)
        skip = prm[6:7, :]
        xf = xsr[...].astype(f32)
        dte = expand(dt[...], off, heads)
        u = xf * dte
        ub = u.astype(bf16)
        ubf = ub.astype(f32)
        s_in = sir[0]
        d_state = ds[half]
        dsb = d_state.astype(bf16)
        te = expand(trail, off, heads)
        tb = te * nn(b, dsb)
        parts = []
        for q in range(heads // 4):
            uq = ub[:, q * 256 : q * 256 + 256]
            dq = dyb[:, q * 256 : q * 256 + 256]
            dmt = nt(stacked(uq, masks), dq)
            mixes = []
            for i in range(4):
                h = off + 4 * q + i
                decay = jnp.exp((cumt[h : h + 1, :] - cumv[:, h : h + 1]) + bias)
                mixes.append((decay * gt).astype(bf16))
                dgt = dgt + dmt[i * BLK : i * BLK + BLK, :] * decay
            parts.append(nn(jnp.concatenate(mixes, axis=1), stacked(dq, masks)))
        du = jnp.concatenate(parts, axis=1) + tb
        ldy = (expand(lead, off, heads) * dyf).astype(bf16)
        d_c = d_c + nt(ldy, s_in.astype(bf16))
        d_b = d_b + nt((te * u).astype(bf16), dsb)
        ds[half] = d_state * expand(retain, off, heads) + tn(c, ldy)
        r1 = r1 + segment_sums(dyf * (yr[...] - skip * xf) - ubf * du, off)
        r2 = r2 + segment_sums(ubf * tb, off)
        r3 = r3 + segment_sums(xf * du, off)
        held = held + segment_sums(fold(d_state * s_in), off)
        a = ar[...]
        sa = sigmoid(a)
        da = (dte * du + skip * dyf) * (sa * (1.0 + a * (1.0 - sa)))
        buf[half, BLK : BLK + 8, :] = buf[half, 0:8, :]
        buf[half, 0:BLK, :] = da
        xp = xpr[...]
        dx, taps = conv_back(da, xp, prm, buf.at[half], mbuf)
        low = dx.astype(bf16)
        dxp[:, at] = low
        total = total + jnp.sum(low.astype(f32) * xp, axis=1, keepdims=True)
        for k in range(4):
            acc[half, 8 * k : 8 * k + 8, :] += taps[k]
        acc[half, 32:40, :] += fold(da)
        acc[half, 40:48, :] += fold(dyf * xf)
    dgb = dgt.astype(bf16)
    dbc[:, :NS] = (d_b + nn(dgb, c)).astype(bf16)
    dbc[:, NS:] = (d_c + tn(dgb, b)).astype(bf16)
    at_last = jnp.sum(r2, axis=0, keepdims=True) + retain * jnp.sum(held, axis=0, keepdims=True)
    dcum = r1 + jnp.where(iota((BLK, 128), 0) == BLK - 1, at_last, 0.0)
    later = (iota((BLK, BLK), 1) >= iota((BLK, BLK), 0)).astype(f32)
    drate = nn(later, dcum, precision=HIGHEST)
    rate = dtp[1:2, :]
    lane = iota((BLK, 128), 1)
    draw = jnp.where(lane < docl, (r3 + rate * drate) * sigmoid(dtr[...] + dtp[0:1, :]), 0.0)
    low = draw.astype(bf16)
    ddt[...] = low
    accs[0:8, :] += fold(drate * dt[...]) * rate
    accs[8:16, :] += fold(draw)
    total = total + jnp.sum(low.astype(f32) * dtr[...], axis=1, keepdims=True)
    mt[...] = jnp.broadcast_to(total, (BLK, 128))
    cda[...] = buf[:, 0:8, :]
    cm[...] = mbuf[0:8, :]


def states_back_kernel(dbc, bca, bcp, msk, kern, cda_in, cm_in, dsp, mt, acc, cda, cm, buf, mbuf):
    @pl.when(pl.program_id(0) == 0)
    def _():
        buf[0:8, :] = cda_in[...]
        mbuf[0:8, :] = cm_in[...]
        acc[...] = jnp.zeros_like(acc)

    mbuf[BLK : BLK + 8, :] = mbuf[0:8, :]
    mbuf[0:BLK, :] = msk[...]
    a = bca[...]
    sa = sigmoid(a)
    da = dbc[...] * (sa * (1.0 + a * (1.0 - sa)))
    buf[BLK : BLK + 8, :] = buf[0:8, :]
    buf[0:BLK, :] = da
    xp = bcp[...]
    dx, taps = conv_back(da, xp, kern, buf, mbuf)
    low = dx.astype(bf16)
    dsp[...] = low
    mt[...] = jnp.broadcast_to(jnp.sum(low.astype(f32) * xp, axis=1, keepdims=True), (BLK, 128))
    for k in range(4):
        acc[8 * k : 8 * k + 8, :] += taps[k]
    acc[32:40, :] += fold(da)
    cda[...] = buf[0:8, :]
    cm[...] = mbuf[0:8, :]


def dn_kernel(dz, dxp, ddt, wa, wb, wdt, o):
    n = wa.shape[1] // 2
    v = nt(dz[:, :n], wa[:, :n]) + nt(dxp[:, :n], wa[:, n:])
    v = v + nt(dz[:, n:], wb[:, :n]) + nt(dxp[:, n:], wb[:, n:])
    o[...] = (v + nt(ddt[...], wdt[...])).astype(bf16)


def tile(width, first=0):
    return pl.BlockSpec((BLK, width), lambda i, *_: (first + i, 0))


def back_tile(width, last):
    return pl.BlockSpec((BLK, width), lambda i, *_: (last - i, 0))


def whole(*shape):
    zeros = (0,) * len(shape)
    return pl.BlockSpec(shape, lambda i, *_: zeros)


def sds(shape, dtype):
    return jax.ShapeDtypeStruct(shape, dtype)


def call(kernel, grid, in_specs, out_specs, out_shape, scratch=(), flops=0, moved=0, prefetch=0):
    return pl.pallas_call(
        kernel,
        grid_spec=pltpu.PrefetchScalarGridSpec(
            num_scalar_prefetch=prefetch,
            grid=(grid,),
            in_specs=in_specs,
            out_specs=out_specs,
            scratch_shapes=list(scratch),
        ),
        out_shape=out_shape,
        compiler_params=pltpu.CompilerParams(
            dimension_semantics=("arbitrary",), vmem_limit_bytes=VMEM_LIMIT
        ),
        cost_estimate=pl.CostEstimate(flops=flops, bytes_accessed=moved, transcendentals=0),
    )


def shards(
    hidden_in, starts, cotangent, norm_gain, w_zx, w_dt, w_bc, conv_x_w, conv_x_b,
    conv_bc_w, conv_bc_b, dt_bias, a_log, d_skip, gnorm_w, w_out,
):
    parts = lax.axis_size("state")
    nrows = lax.axis_size("rows")
    groups = parts // 2
    me = lax.axis_index("state")
    mine = me % 2
    zpos = me // 2
    core = lax.axis_index("rows") % 2
    dim = hidden_in.shape[1]
    local_dim = cotangent.shape[1]
    lanes = w_zx.shape[2]
    heads = w_dt.shape[1]
    inner = lanes * parts
    docl = 2 * heads
    wide = dim // groups

    pair = [(i, i ^ 1) for i in range(parts)]

    def swap(v):
        return lax.ppermute(v, "state", pair)

    def cross(v, bit):
        return lax.ppermute(v, "rows", [(i, i ^ bit) for i in range(nrows)])

    def line_sum(v):
        bit = 2
        while bit < parts:
            v = v + lax.ppermute(v, "state", [(i, i ^ bit) for i in range(parts)])
            bit *= 2
        return v

    def rows_of(v, start, size):
        return lax.dynamic_slice_in_dim(v, start, size, 0)

    def fetch(own):
        half = own.shape[0] // 2
        got = swap(rows_of(own, core * half, half))
        other = cross(got, 1)
        first = core == 0
        return jnp.concatenate([jnp.where(first, got, other), jnp.where(first, other, got)], axis=0)

    w_a = w_zx.reshape(dim, 2 * lanes)
    w_b = fetch(w_a)
    o_a = w_out
    o_b = fetch(w_out)
    small = jnp.stack([dt_bias, a_log, d_skip]).reshape(-1)
    prm_a = jnp.concatenate(
        [
            conv_x_w,
            conv_x_b[None],
            gnorm_w[None],
            jnp.repeat(d_skip, HD)[None],
            jnp.pad(small, (0, lanes - small.shape[0]))[None],
        ],
        axis=0,
    )
    prm_b = swap(prm_a)
    small_b = prm_b[7, : 3 * heads].reshape(3, heads)
    wdt_a = w_dt.T
    wdt_b = swap(wdt_a)
    bias_all = jnp.concatenate([dt_bias, small_b[0]])
    rate_all = -jnp.exp(jnp.concatenate([a_log, small_b[1]]))
    dtp = jnp.pad(jnp.stack([bias_all, rate_all]), ((0, 6), (0, 128 - docl)))
    wbc = lax.all_gather(w_bc.transpose(1, 2, 0), "state", axis=1, tiled=True)
    wbc = wbc.reshape(2 * NS, dim)
    wdt = jnp.concatenate([wdt_a, wdt_b, jnp.zeros((128 - docl, dim), bf16)], axis=0)
    wst = jnp.concatenate([wbc, wdt], axis=0)
    kern_bc = jnp.concatenate([conv_bc_w, conv_bc_b[None]], axis=0)
    kern_bc = lax.all_gather(kern_bc, "state", axis=2, tiled=True).reshape(5, 2 * NS)
    kern_bc = jnp.pad(kern_bc, ((0, 3), (0, 0)))

    st = rows_of(starts, mine * LEN, LEN).astype(f32)
    open1 = jnp.where(jnp.arange(LEN) == 0, 0.0, 1.0 - st)
    open2 = open1 * jnp.concatenate([jnp.zeros((1,), f32), open1[:-1]])
    open3 = open2 * jnp.concatenate([jnp.zeros((2,), f32), open1[:-2]])
    msk = jnp.pad(jnp.stack([st, open1, open2, open3], axis=1), ((0, 0), (0, 124)))
    which = mine.astype(jnp.int32).reshape(1)

    tl = (BLK, lanes)
    proj_out = [tile(lanes), tile(lanes), tile(lanes), tile(lanes)]
    proj_shape = [sds((LEN, lanes), f32)] * 3 + [sds((LEN, lanes), bf16)]
    pf = 2 * LEN * dim * 2 * lanes
    normed, r_wide, z_a, xp_a, a_a, xs_a = call(
        first_kernel,
        NBLK,
        [
            pl.BlockSpec((BLK, dim), lambda i, which: (which[0] * NBLK + i, 0)),
            whole(1, dim),
            whole(dim, 2 * lanes),
            whole(8, lanes),
            tile(128),
        ],
        [tile(dim), tile(128)] + proj_out,
        [sds((LEN, dim), bf16), sds((LEN, 128), f32)] + proj_shape,
        [pltpu.VMEM((BLK + 8, lanes), f32)],
        flops=pf,
        moved=40 << 20,
        prefetch=1,
    )(which, hidden_in, norm_gain.reshape(1, dim), w_a, prm_a, msk)
    bcp, bca, bc, dtr, dt, cum, cumt = call(
        functools.partial(states_kernel, docl),
        NBLK,
        [tile(dim), whole(2 * NS + 128, dim), whole(8, 2 * NS), whole(8, 128), tile(128)],
        [tile(2 * NS)] * 3 + [tile(128)] * 3 + [pl.BlockSpec((128, BLK), lambda i: (0, i))],
        [sds((LEN, 2 * NS), f32)] * 2
        + [sds((LEN, 2 * NS), bf16)]
        + [sds((LEN, 128), f32)] * 3
        + [sds((128, LEN), f32)],
        [pltpu.VMEM((BLK + 8, 2 * NS), f32)],
        flops=2 * LEN * dim * 512,
        moved=18 << 20,
    )(normed, wst, kern_bc, dtp, msk)

    def scan(off, xs, z, prm):
        return call(
            functools.partial(scan_kernel, docl, off),
            NBLK,
            [
                tile(lanes), tile(lanes), tile(2 * NS), tile(128), tile(128),
                pl.BlockSpec((128, BLK), lambda i: (0, i)), whole(8, lanes),
            ],
            [tile(lanes), tile(lanes), pl.BlockSpec((1, NS, lanes), lambda i: (i, 0, 0)), tile(128)],
            [
                sds((LEN, lanes), f32),
                sds((LEN, lanes), bf16),
                sds((NBLK, NS, lanes), f32),
                sds((LEN, 128), f32),
            ],
            [pltpu.VMEM((NS, lanes), f32)],
            flops=10 << 30,
            moved=20 << 20,
        )(xs, z, bc, dt, cum, cumt, prm)

    y_a, gw_a, sin_a, pw_a = scan(0, xs_a, z_a, prm_a)
    z_b, xp_b, a_b, xs_b = call(
        second_kernel,
        NBLK,
        [tile(dim), whole(dim, 2 * lanes), whole(8, lanes), tile(128)],
        proj_out,
        proj_shape,
        [pltpu.VMEM((BLK + 8, lanes), f32)],
        flops=pf,
        moved=28 << 20,
    )(normed, w_b, prm_b, msk)
    y_b, gw_b, sin_b, pw_b = scan(heads, xs_b, z_b, prm_b)

    c_mine = rows_of(cotangent, mine * LEN, LEN)
    c_got = swap(rows_of(cotangent, (1 - mine) * LEN, LEN))
    is0 = mine == 0
    c_pair = jnp.concatenate([jnp.where(is0, c_mine, c_got), jnp.where(is0, c_got, c_mine)], axis=1)

    def right(k):
        return [(i, i + 2) for i in range(parts - 2) if i // 2 >= k - 1]

    def left(k):
        return [(i, i - 2) for i in range(2, parts) if i // 2 <= groups - k]

    def gather_line(v):
        up, down = {}, {}
        cur_u = cur_d = v
        for k in range(1, groups):
            cur_u = lax.ppermute(cur_u, "state", right(k))
            cur_d = lax.ppermute(cur_d, "state", left(k))
            up[k], down[k] = cur_u, cur_d
        pieces = [v]
        for k in range(1, groups):
            pieces.append(jnp.where(zpos >= k, up[k], down[groups - k]))
        return jnp.concatenate(pieces, axis=1)

    def relative(w):
        return jnp.concatenate(
            [
                lax.dynamic_slice_in_dim(w, (zpos + groups - k) % groups * wide, wide, 1)
                for k in range(groups)
            ],
            axis=1,
        )

    def scatter_line(v):
        def own(j):
            return lax.dynamic_slice_in_dim(v, jnp.clip(j, 0, groups - 1) * wide, wide, 1)

        up = down = None
        for d in range(groups - 1, 0, -1):
            send_u, send_d = own(zpos + d), own(zpos - d)
            if up is not None:
                send_u = (send_u.astype(f32) + up.astype(f32)).astype(bf16)
                send_d = (send_d.astype(f32) + down.astype(f32)).astype(bf16)
            up = lax.ppermute(
                send_u, "state", [(i, i + 2) for i in range(parts - 2) if i // 2 + d < groups]
            )
            down = lax.ppermute(
                send_d, "state", [(i, i - 2) for i in range(2, parts) if i // 2 - d >= 0]
            )
        return own(zpos).astype(f32) + up.astype(f32) + down.astype(f32)

    c_rel = [None] * CHUNKS
    for j in reversed(range(CHUNKS)):
        c_rel[j] = gather_line(c_pair[j * CT : (j + 1) * CT])
    or_a, or_b = relative(o_a), relative(o_b)

    partial_out = call(
        out_kernel,
        NBLK,
        [tile(lanes), tile(lanes), whole(lanes, dim), whole(lanes, dim)],
        tile(dim),
        sds((LEN, dim), bf16),
        flops=4 * LEN * lanes * dim,
        moved=14 << 20,
    )(gw_a, gw_b, o_a, o_b)
    mixer = scatter_line(partial_out)

    def dyn_call(j):
        return call(
            dyn_kernel,
            CB,
            [tile(dim), whole(lanes, dim), whole(lanes, dim), tile(lanes, j * CB), tile(lanes, j * CB)],
            [tile(lanes), tile(lanes), tile(128)],
            [sds((CT, lanes), bf16)] * 2 + [sds((CT, 128), f32)],
            flops=4 * CT * lanes * dim,
            moved=10 << 20,
        )(c_rel[j], or_a, or_b, gw_a, gw_b)

    power = pw_a[:, 0] + pw_b[:, 0]
    dz, dy, yn, mtg, ggs, scales = ([None] * CHUNKS for _ in range(6))
    for j in reversed(range(CHUNKS)):
        d_a, d_b, qs = dyn_call(j)
        sums = line_sum(jnp.concatenate([power[j * CT : (j + 1) * CT], qs[:, 0]]))
        s = lax.rsqrt(sums[:CT] / inner + EPSILON)
        kq = s * s * s * (sums[CT:] / inner)
        scales[j] = s
        sq = jnp.pad(jnp.stack([s, kq], axis=1), ((0, 0), (0, 126)))
        dz[j], dy[j], yn[j], mtg[j], gg = call(
            gate_kernel,
            CB,
            [tile(128)]
            + [tile(lanes)] * 2
            + [tile(lanes, j * CB)] * 4
            + [whole(8, lanes)] * 2,
            [tile(2 * lanes)] * 3 + [tile(128), whole(8, 2 * lanes)],
            [sds((CT, 2 * lanes), bf16)] * 3 + [sds((CT, 128), f32), sds((8, 2 * lanes), f32)],
            flops=100 * CT * lanes,
            moved=12 << 20,
        )(sq, d_a, d_b, y_a, y_b, z_a, z_b, prm_a, prm_b)
        ggs[j] = gg.sum(axis=0)

    wdt_t = wdt.T
    wbc_near = lax.dynamic_slice_in_dim(wbc, zpos * wide, wide, 1)
    ds = jnp.zeros((2, NS, lanes), f32)
    cda = jnp.zeros((2, 8, lanes), f32)
    cm = jnp.zeros((8, 128), f32)
    sda = jnp.zeros((8, 2 * NS), f32)
    scm = cm
    dxp, ddt, dsp, mts, near, far = ([None] * CHUNKS for _ in range(6))
    accs, accs_dt, accs_bc = [], [], []
    for j in reversed(range(CHUNKS)):
        last = j * CB + CB - 1

        def bt(width, last=last):
            return back_tile(width, last)

        def loc(width):
            return back_tile(width, CB - 1)

        cols = pl.BlockSpec((128, BLK), lambda i, last=last: (0, last - i))
        sins = pl.BlockSpec((1, NS, lanes), lambda i, last=last: (last - i, 0, 0))
        dxp[j], ddt[j], dbc, mtb, acc, acc_dt, ds, cda, cm = call(
            functools.partial(back_kernel, docl),
            CB,
            [
                loc(2 * lanes), bt(2 * NS), bt(128), bt(128), cols, bt(128), bt(128), whole(8, 128),
                bt(lanes), bt(lanes), bt(lanes), bt(lanes), bt(lanes), bt(lanes), bt(lanes), bt(lanes),
                sins, sins, whole(8, lanes), whole(8, lanes),
                whole(2, NS, lanes), whole(2, 8, lanes), whole(8, 128),
            ],
            [
                loc(2 * lanes), loc(128), loc(2 * NS), loc(128), whole(2, 48, lanes), whole(16, 128),
                whole(2, NS, lanes), whole(2, 8, lanes), whole(8, 128),
            ],
            [
                sds((CT, 2 * lanes), bf16), sds((CT, 128), bf16), sds((CT, 2 * NS), bf16),
                sds((CT, 128), f32), sds((2, 48, lanes), f32), sds((16, 128), f32),
                sds((2, NS, lanes), f32), sds((2, 8, lanes), f32), sds((8, 128), f32),
            ],
            [pltpu.VMEM((2, BLK + 8, lanes), f32), pltpu.VMEM((BLK + 8, 128), f32)],
            flops=24 << 30,
            moved=20 << 20,
        )(
            dy[j], bc, dt, cum, cumt, dtr, msk, dtp,
            y_a, y_b, xs_a, xs_b, a_a, a_b, xp_a, xp_b, sin_a, sin_b, prm_a, prm_b,
            ds, cda, cm,
        )
        accs.append(acc)
        accs_dt.append(acc_dt)

        whole_dbc = dbc
        bit = 2
        while bit < parts:
            got = lax.ppermute(
                whole_dbc.astype(bf16), "state", [(i, i ^ bit) for i in range(parts)]
            )
            whole_dbc = whole_dbc.astype(f32) + got.astype(f32)
            bit *= 2
        dsp[j], mtc, acc_bc, sda, scm = call(
            states_back_kernel,
            CB,
            [loc(2 * NS), bt(2 * NS), bt(2 * NS), bt(128), whole(8, 2 * NS), whole(8, 2 * NS), whole(8, 128)],
            [loc(2 * NS), loc(128), whole(40, 2 * NS), whole(8, 2 * NS), whole(8, 128)],
            [
                sds((CT, 2 * NS), bf16), sds((CT, 128), f32), sds((40, 2 * NS), f32),
                sds((8, 2 * NS), f32), sds((8, 128), f32),
            ],
            [pltpu.VMEM((BLK + 8, 2 * NS), f32), pltpu.VMEM((BLK + 8, 128), f32)],
            flops=100 * CT * 2 * NS,
            moved=3 << 20,
        )(whole_dbc, bca, bcp, msk, kern_bc, sda, scm)
        accs_bc.append(acc_bc)

        dn = call(
            dn_kernel,
            4,
            [
                whole(CT, 2 * lanes), whole(CT, 2 * lanes), whole(CT, 128),
                pl.BlockSpec((dim // 4, 2 * lanes), lambda i: (i, 0)),
                pl.BlockSpec((dim // 4, 2 * lanes), lambda i: (i, 0)),
                pl.BlockSpec((dim // 4, 128), lambda i: (i, 0)),
            ],
            pl.BlockSpec((CT, dim // 4), lambda i: (0, i)),
            sds((CT, dim), bf16),
            flops=8 * CT * lanes * dim,
            moved=14 << 20,
        )(dz[j], dxp[j], ddt[j], w_a, w_b, wdt_t)
        near_sum = scatter_line(dn) + jnp.dot(dsp[j], wbc_near, preferred_element_type=f32)
        near[j] = lax.dynamic_slice_in_dim(near_sum, mine * local_dim, local_dim, 1)
        far[j] = swap(
            lax.dynamic_slice_in_dim(near_sum, (1 - mine) * local_dim, local_dim, 1).astype(bf16)
        )
        mts[j] = line_sum(mtg[j][:, 0] + mtb[:, 0]) + mtc[:, 0]

    def halves(v, bit):
        size = v.shape[-2] // 2
        up = (lax.axis_index("rows") // bit) % 2
        keep = lax.dynamic_slice_in_dim(v, up * size, size, v.ndim - 2)
        give = lax.dynamic_slice_in_dim(v, (1 - up) * size, size, v.ndim - 2)
        return keep, give

    def reduce_pair(v):
        keep, give = halves(v, 1)
        v = keep + cross(give, 1)
        v = v[0] + swap(v[1].astype(bf16)).astype(f32)
        bit = 2
        while bit < nrows:
            keep, give = halves(v, bit)
            v = keep + cross(give.astype(bf16), bit).astype(f32)
            bit *= 2
        while bit > 1:
            bit //= 2
            got = cross(v, bit)
            low = (lax.axis_index("rows") // bit) % 2 == 0
            v = jnp.concatenate([jnp.where(low, v, got), jnp.where(low, got, v)], axis=0)
        return v

    def weight_grad(a, b):
        return jnp.einsum("ta,tb->ab", a, b, preferred_element_type=f32)

    c_all = jnp.concatenate(c_rel, axis=0)
    yn_all = jnp.concatenate(yn, axis=0)
    g_out = reduce_pair(weight_grad(yn_all, c_all).reshape(2, lanes, dim))
    back = [(zpos + groups - q) % groups for q in range(groups)]
    grad_w_out = jnp.concatenate(
        [lax.dynamic_slice_in_dim(g_out, k * wide, wide, 1) for k in back], axis=1
    )

    def zx_grad(v):
        v = jnp.concatenate(v, axis=0)
        return reduce_pair(
            jnp.stack([weight_grad(normed, v[:, :lanes]), weight_grad(normed, v[:, lanes:])])
        )

    grad_w_zx = jnp.stack([zx_grad(dz), zx_grad(dxp)], axis=1)
    cols = w_bc.shape[2]
    dsp_all = jnp.concatenate(dsp, axis=0).reshape(LEN, 2, NS)
    dsp_near = lax.dynamic_slice_in_dim(dsp_all, zpos * 2 * cols, 2 * cols, 2)
    dsp_near = dsp_near.reshape(LEN, 2, 2, cols)
    ddt_all = jnp.concatenate(ddt, axis=0)

    def few(q):
        sel = lax.dynamic_index_in_dim(dsp_near, q, 2, keepdims=False).reshape(LEN, 2 * cols)
        dts = lax.dynamic_slice_in_dim(ddt_all, jnp.where(q == mine, 0, heads), heads, 1)
        return jnp.concatenate([sel, dts], axis=1)

    both = jnp.concatenate([few(mine), few(1 - mine)], axis=1)
    g_few = weight_grad(normed, both)
    width = 2 * cols + heads
    g_few = reduce_pair(jnp.stack([g_few[:, :width], g_few[:, width:]]))
    grad_w_bc = g_few[:, : 2 * cols].reshape(dim, 2, cols)
    grad_w_dt = g_few[:, 2 * cols :]

    acc = sum(accs).reshape(2, 6, 8, lanes).sum(axis=2)
    gg = sum(ggs).reshape(2, 1, lanes)
    acc_dt = sum(accs_dt).reshape(2, 8, 128).sum(axis=1)[:, :docl].reshape(2, 2, heads)
    acc_dt = jnp.pad(acc_dt.transpose(1, 0, 2).reshape(2, 1, -1), ((0, 0), (0, 0), (0, lanes - docl)))
    vec = jnp.concatenate([acc, gg, acc_dt], axis=1)
    acc_bc = sum(accs_bc).reshape(5, 8, 2 * NS).sum(axis=1)

    def rows_sum(v):
        bit = 1
        while bit < nrows:
            v = v + cross(v, bit)
            bit *= 2
        return v

    vec = rows_sum(vec[0] + swap(vec[1]))
    acc_bc = rows_sum(acc_bc + swap(acc_bc)).reshape(5, 2, NS)
    acc_bc = lax.dynamic_slice_in_dim(acc_bc, me * cols, cols, 2)

    s_all = jnp.concatenate(scales)
    out_near = mixer * s_all[:, None]
    o_own = lax.dynamic_slice_in_dim(out_near, mine * local_dim, local_dim, 1)
    o_far = swap(
        lax.dynamic_slice_in_dim(out_near, (1 - mine) * local_dim, local_dim, 1).astype(bf16)
    )
    r_own = r_wide[:, 0]
    m_own = jnp.concatenate(mts)
    r_far = swap(r_own)
    m_far = swap(m_own)
    d_own = jnp.concatenate(near, axis=0)
    d_far = jnp.concatenate(far, axis=0)
    x_near = lax.dynamic_slice_in_dim(hidden_in, me * local_dim, local_dim, 1).astype(f32)
    gain = lax.dynamic_slice_in_dim(norm_gain, me * local_dim, local_dim, 0)
    outs, grads, gain_sum = [], [], 0.0
    for q in range(2):
        sel = mine == q
        x = x_near[q * LEN : (q + 1) * LEN]
        cot = cotangent[q * LEN : (q + 1) * LEN].astype(f32)
        outs.append((x + jnp.where(sel, o_own, o_far.astype(f32))).astype(bf16))
        d = jnp.where(sel, d_own, d_far.astype(f32))
        r = jnp.where(sel, r_own, r_far)[:, None]
        m = jnp.where(sel, m_own, m_far)[:, None]
        grads.append(cot + r * (d * gain) - x * (r * r) * (m / dim))
        gain_sum = gain_sum + jnp.sum(d * x * r, axis=0)
    return (
        jnp.concatenate(outs, axis=0),
        jnp.concatenate(grads, axis=0),
        rows_sum(gain_sum),
        grad_w_zx,
        grad_w_dt,
        grad_w_bc,
        vec[:4],
        vec[4],
        acc_bc[:4],
        acc_bc[4],
        vec[7, heads : 2 * heads],
        vec[7, :heads],
        vec[5].reshape(heads, HD).sum(axis=1),
        vec[6],
        grad_w_out,
    )


def solution(mesh):
    placed = (
        P("rows", None),
        P("rows"),
        P("rows", "state"),
        P(),
        P(None, None, "state"),
        P(None, "state"),
        P(None, None, "state"),
        P(None, "state"),
        P("state"),
        P(None, None, "state"),
        P(None, "state"),
        P("state"),
        P("state"),
        P("state"),
        P("state"),
        P("state", None),
    )
    return jax.shard_map(
        shards,
        mesh=mesh,
        in_specs=placed,
        out_specs=(
            P("rows", "state"),
            P("rows", "state"),
            P("state"),
            P(None, None, "state"),
            P(None, "state"),
            P(None, None, "state"),
            P(None, "state"),
            P("state"),
            P(None, None, "state"),
            P(None, "state"),
            P("state"),
            P("state"),
            P("state"),
            P("state"),
            P("state", None),
        ),
        check_vma=False,
    )
```

```python
import functools

import jax
import jax.numpy as jnp
from jax import lax
from jax.experimental import pallas as pl
from jax.experimental.pallas import tpu as pltpu
from jax.sharding import Mesh
from jax.sharding import PartitionSpec as P

LEN = 2048
BLK = 256
NBLK = LEN // BLK
CHUNKS = 2
CT = LEN // CHUNKS
CB = CT // BLK
HD = 64
NS = 128
EPSILON = 1e-05
HIGHEST = lax.Precision.HIGHEST
f32 = jnp.float32
bf16 = jnp.bfloat16
COST = 1
CHEAP = 1 << 16
VMEM_LIMIT = 56 * 1024 * 1024


def nn(a, b, **kw):
    return lax.dot_general(a, b, (((1,), (0,)), ((), ())), preferred_element_type=f32, **kw)


def nt(a, b):
    return lax.dot_general(a, b, (((1,), (1,)), ((), ())), preferred_element_type=f32)


def tn(a, b):
    return lax.dot_general(a, b, (((0,), (0,)), ((), ())), preferred_element_type=f32)


def iota(shape, dim):
    return lax.broadcasted_iota(jnp.int32, shape, dim)


def sigmoid(v):
    return 1.0 / (1.0 + jnp.exp(-v))


def fold(v):
    return v.reshape(v.shape[0] // 8, 8, v.shape[1]).sum(axis=0)


def expand(cols, off, heads):
    low = iota((cols.shape[0], 128), 1) < HD
    pieces = []
    for p in range(heads // 2):
        a = cols[:, off + 2 * p : off + 2 * p + 1]
        b = cols[:, off + 2 * p + 1 : off + 2 * p + 2]
        pieces.append(jnp.where(low, a, b))
    return jnp.concatenate(pieces, axis=1)


def quad_masks(rows):
    head = iota((rows, 4 * HD), 1) // HD
    return [head == h for h in range(4)]


def stacked(v, masks):
    zero = jnp.zeros_like(v)
    return jnp.concatenate([jnp.where(m, v, zero) for m in masks], axis=0)


def segment_sums(v, off):
    n = v.shape[1]
    pick = (iota((n, 128), 1) == iota((n, 128), 0) // HD + off).astype(bf16)
    high = v.astype(bf16)
    rest = (v - high.astype(f32)).astype(bf16)
    return nn(high, pick) + nn(rest, pick)


def conv_tile(step, x1, kern, msk, buf, start=None):
    @pl.when(step == 0)
    def _():
        buf[0:8, :] = jnp.zeros((8, buf.shape[1]), f32) if start is None else start[...]

    buf[8 : 8 + BLK, :] = x1
    acc = kern[4:5, :] + kern[3:4, :] * x1
    for k in range(1, 4):
        acc = acc + kern[3 - k : 4 - k, :] * (buf[8 - k : 8 - k + BLK, :] * msk[:, k : k + 1])
    buf[0:8, :] = x1[BLK - 8 :, :]
    return acc


def project_tile(n, w, kern, msk, z, xp, a, xs, buf, start=None):
    lanes = w.shape[1] // 2
    p = nn(n, w[...])
    z[...] = p[:, :lanes].astype(bf16)
    x1 = p[:, lanes:]
    xp[...] = x1.astype(bf16)
    acc = conv_tile(pl.program_id(0), x1, kern, msk, buf, start)
    a[...] = acc.astype(bf16)
    xs[...] = (acc * sigmoid(acc)).astype(bf16)


def first_kernel(which, hid, gain, w, kern, msk, start, normed, r, z, xp, a, xs, tail, buf):
    x = hid[...].astype(f32)
    rr = lax.rsqrt(jnp.mean(x * x, axis=1, keepdims=True) + EPSILON)
    n = (x * rr * gain[...]).astype(bf16)
    normed[...] = n
    r[...] = jnp.broadcast_to(rr, (BLK, 128))
    project_tile(n, w, kern, msk, z, xp, a, xs, buf, start)
    tail[...] = buf[0:8, :]


def second_kernel(normed, w, kern, msk, z, xp, a, xs, buf):
    project_tile(normed[...], w, kern, msk, z, xp, a, xs, buf)


def states_kernel(docl, normed, ws, kern, dtp, msk, bcp, bca, bc, dtr, dt, cum, cumt, buf):
    q = nt(normed[...], ws[...])
    x1 = q[:, : 2 * NS]
    bcp[...] = x1
    acc = conv_tile(pl.program_id(0), x1, kern, msk, buf)
    bca[...] = acc
    bc[...] = (acc * sigmoid(acc)).astype(bf16)
    d = q[:, 2 * NS :]
    dtr[...] = d
    v = d + dtp[0:1, :]
    e = jnp.exp(-jnp.abs(v))
    small = e * (1.0 - e * (0.5 - e * (1.0 / 3.0 - 0.25 * e)))
    step = jnp.maximum(v, 0.0) + jnp.where(e < 0.01, small, jnp.log(1.0 + e))
    lane = iota((BLK, 128), 1)
    step = jnp.where(lane < docl, step, 0.0)
    dt[...] = step
    ext = jnp.where(lane == docl, msk[:, 0:1], step * dtp[1:2, :])
    tri = (iota((BLK, BLK), 0) >= iota((BLK, BLK), 1)).astype(f32)
    c = nn(tri, ext, precision=HIGHEST)
    cum[...] = c
    cumt[...] = c.T


def block_scalars(docl, cum):
    lane = iota((BLK, 128), 1)
    doc = cum[:, docl : docl + 1]
    doc_last = cum[BLK - 1 : BLK, docl : docl + 1]
    rates = jnp.where(lane < docl, cum, 0.0)
    last = rates[BLK - 1 : BLK, :]
    lead = jnp.exp(rates) * (doc == 0.0).astype(f32)
    trail = jnp.exp(last - rates) * (doc == doc_last).astype(f32)
    retain = jnp.exp(last) * (doc_last == 0.0).astype(f32)
    return lead, trail, retain


def scan_kernel(docl, off, xs, z, bc, dt, cum, cumt, prm, y, gw, sin, pw, state):
    lanes = xs.shape[1]
    heads = lanes // HD

    @pl.when(pl.program_id(0) == 0)
    def _():
        state[...] = jnp.zeros_like(state)

    s_in = state[...]
    sin[0] = s_in
    b = bc[:, :NS]
    c = bc[:, NS:]
    cumv = cum[...]
    lead, trail, retain = block_scalars(docl, cumv)
    within = (cumv[:, docl : docl + 1] == cumt[docl : docl + 1, :]) & (
        iota((BLK, BLK), 0) >= iota((BLK, BLK), 1)
    )
    bias = jnp.where(within, 0.0, -1e30)
    g = nt(c, b)
    xf = xs[...].astype(f32)
    u = xf * expand(dt[...], off, heads)
    ub = u.astype(bf16)
    masks = quad_masks(BLK)
    parts = []
    for q in range(heads // 4):
        mixes = []
        for h in range(off + 4 * q, off + 4 * q + 4):
            decay = jnp.exp((cumv[:, h : h + 1] - cumt[h : h + 1, :]) + bias)
            mixes.append((decay * g).astype(bf16))
        uq = ub[:, q * 256 : q * 256 + 256]
        parts.append(nn(jnp.concatenate(mixes, axis=1), stacked(uq, masks)))
    yv = jnp.concatenate(parts, axis=1)
    yv = yv + nn(c, s_in.astype(bf16)) * expand(lead, off, heads) + prm[6:7, :] * xf
    y[...] = yv
    ut = (u * expand(trail, off, heads)).astype(bf16)
    state[...] = s_in * expand(retain, off, heads) + tn(b, ut)
    zz = z[...].astype(f32)
    gated = yv * zz * sigmoid(zz)
    gw[...] = (gated * prm[5:6, :]).astype(bf16)
    pw[...] = jnp.broadcast_to(jnp.sum(gated * gated, axis=1, keepdims=True), (BLK, 128))


def out_kernel(ga, gb, wa, wb, o):
    o[...] = (nn(ga[...], wa[...]) + nn(gb[...], wb[...])).astype(bf16)


def dyn_kernel(c, wa, wb, ga, gb, da, db, qs):
    cv = c[...]
    a = nt(cv, wa[...])
    b = nt(cv, wb[...])
    da[...] = a.astype(bf16)
    db[...] = b.astype(bf16)
    q = jnp.sum(a * ga[...].astype(f32), axis=1, keepdims=True)
    q = q + jnp.sum(b * gb[...].astype(f32), axis=1, keepdims=True)
    qs[...] = jnp.broadcast_to(q, (BLK, 128))


def gate_kernel(sq, da, db, ya, yb, za, zb, prma, prmb, dz, dy, yn, mt, gg):
    lanes = da.shape[1]
    s = sq[:, 0:1]
    kq = sq[:, 1:2]

    @pl.when(pl.program_id(0) == 0)
    def _():
        gg[...] = jnp.zeros_like(gg)

    total = jnp.zeros((BLK, 1), f32)
    for half, (dref, yref, zref, prm) in enumerate(((da, ya, za, prma), (db, yb, zb, prmb))):
        at = slice(half * lanes, half * lanes + lanes)
        dn = dref[...].astype(f32)
        y = yref[...]
        z = zref[...].astype(f32)
        gn = prm[5:6, :]
        sg = sigmoid(z)
        act = z * sg
        g = y * act
        gs = g * s
        yn[:, at] = (gs * gn).astype(bf16)
        gg[:, at] += fold(dn * gs)
        dg = s * (dn * gn) - g * kq
        dy[:, at] = (dg * act).astype(bf16)
        low = (dg * y * (sg * (1.0 + z * (1.0 - sg)))).astype(bf16)
        dz[:, at] = low
        total = total + jnp.sum(low.astype(f32) * z, axis=1, keepdims=True)
    mt[...] = jnp.broadcast_to(total, (BLK, 128))


def conv_back(da, xp, kern, buf, mbuf):
    dx = kern[3:4, :] * da
    taps = [None, None, None, fold(xp * da)]
    for k in range(1, 4):
        sh = buf[k : k + BLK, :] * mbuf[k : k + BLK, k : k + 1]
        dx = dx + kern[3 - k : 4 - k, :] * sh
        taps[3 - k] = fold(xp * sh)
    return dx, taps


def back_kernel(
    docl,
    dy, bc, dt, cum, cumt, dtr, msk, dtp,
    ya, yb, xsa, xsb, aa, ab, xpa, xpb, sia, sib, prma, prmb,
    ds_in, cda_in, cm_in,
    dxp, ddt, dbc, mt, acc, accs, ds, cda, cm,
    buf, mbuf,
):
    lanes = xsa.shape[1]
    heads = lanes // HD
    step = pl.program_id(0)

    @pl.when(step == 0)
    def _():
        ds[...] = ds_in[...]
        buf[:, 0:8, :] = cda_in[...]
        mbuf[0:8, :] = cm_in[...]
        acc[...] = jnp.zeros_like(acc)
        accs[...] = jnp.zeros_like(accs)

    mbuf[BLK : BLK + 8, :] = mbuf[0:8, :]
    mbuf[0:BLK, :] = msk[...]
    b = bc[:, :NS]
    c = bc[:, NS:]
    cumv = cum[...]
    lead, trail, retain = block_scalars(docl, cumv)
    within = (cumv[:, docl : docl + 1] == cumt[docl : docl + 1, :]) & (
        iota((BLK, BLK), 0) <= iota((BLK, BLK), 1)
    )
    bias = jnp.where(within, 0.0, -1e30)
    gt = nt(b, c)
    masks = quad_masks(BLK)
    dgt = jnp.zeros((BLK, BLK), f32)
    d_c = jnp.zeros((BLK, NS), f32)
    d_b = jnp.zeros((BLK, NS), f32)
    r1 = jnp.zeros((BLK, 128), f32)
    r2 = jnp.zeros((BLK, 128), f32)
    r3 = jnp.zeros((BLK, 128), f32)
    held = jnp.zeros((8, 128), f32)
    total = jnp.zeros((BLK, 1), f32)
    refs = ((ya, xsa, aa, xpa, sia, prma), (yb, xsb, ab, xpb, sib, prmb))
    for half, (yr, xsr, ar, xpr, sir, prm) in enumerate(refs):
        off = half * heads
        at = slice(half * lanes, half * lanes + lanes)
        dyb = dy[:, at]
        dyf = dyb.astype(f32)
        skip = prm[6:7, :]
        xf = xsr[...].astype(f32)
        dte = expand(dt[...], off, heads)
        u = xf * dte
        ub = u.astype(bf16)
        ubf = ub.astype(f32)
        s_in = sir[0]
        d_state = ds[half]
        dsb = d_state.astype(bf16)
        te = expand(trail, off, heads)
        tb = te * nn(b, dsb)
        parts = []
        for q in range(heads // 4):
            uq = ub[:, q * 256 : q * 256 + 256]
            dq = dyb[:, q * 256 : q * 256 + 256]
            dmt = nt(stacked(uq, masks), dq)
            mixes = []
            for i in range(4):
                h = off + 4 * q + i
                decay = jnp.exp((cumt[h : h + 1, :] - cumv[:, h : h + 1]) + bias)
                mixes.append((decay * gt).astype(bf16))
                dgt = dgt + dmt[i * BLK : i * BLK + BLK, :] * decay
            parts.append(nn(jnp.concatenate(mixes, axis=1), stacked(dq, masks)))
        du = jnp.concatenate(parts, axis=1) + tb
        ldy = (expand(lead, off, heads) * dyf).astype(bf16)
        d_c = d_c + nt(ldy, s_in.astype(bf16))
        d_b = d_b + nt((te * u).astype(bf16), dsb)
        ds[half] = d_state * expand(retain, off, heads) + tn(c, ldy)
        r1 = r1 + segment_sums(dyf * (yr[...] - skip * xf) - ubf * du, off)
        r2 = r2 + segment_sums(ubf * tb, off)
        r3 = r3 + segment_sums(xf * du, off)
        held = held + segment_sums(fold(d_state * s_in), off)
        a = ar[...].astype(f32)
        sa = sigmoid(a)
        da = (dte * du + skip * dyf) * (sa * (1.0 + a * (1.0 - sa)))
        buf[half, BLK : BLK + 8, :] = buf[half, 0:8, :]
        buf[half, 0:BLK, :] = da
        xp = xpr[...].astype(f32)
        dx, taps = conv_back(da, xp, prm, buf.at[half], mbuf)
        low = dx.astype(bf16)
        dxp[:, at] = low
        total = total + jnp.sum(low.astype(f32) * xp, axis=1, keepdims=True)
        for k in range(4):
            acc[half, 8 * k : 8 * k + 8, :] += taps[k]
        acc[half, 32:40, :] += fold(da)
        acc[half, 40:48, :] += fold(dyf * xf)
    dgb = dgt.astype(bf16)
    dbc[:, :NS] = (d_b + nn(dgb, c)).astype(bf16)
    dbc[:, NS:] = (d_c + tn(dgb, b)).astype(bf16)
    at_last = jnp.sum(r2, axis=0, keepdims=True) + retain * jnp.sum(held, axis=0, keepdims=True)
    dcum = r1 + jnp.where(iota((BLK, 128), 0) == BLK - 1, at_last, 0.0)
    later = (iota((BLK, BLK), 1) >= iota((BLK, BLK), 0)).astype(f32)
    drate = nn(later, dcum, precision=HIGHEST)
    rate = dtp[1:2, :]
    lane = iota((BLK, 128), 1)
    draw = jnp.where(lane < docl, (r3 + rate * drate) * sigmoid(dtr[...] + dtp[0:1, :]), 0.0)
    low = draw.astype(bf16)
    ddt[...] = low
    accs[0:8, :] += fold(drate * dt[...]) * rate
    accs[8:16, :] += fold(draw)
    total = total + jnp.sum(low.astype(f32) * dtr[...], axis=1, keepdims=True)
    mt[...] = jnp.broadcast_to(total, (BLK, 128))
    cda[...] = buf[:, 0:8, :]
    cm[...] = mbuf[0:8, :]


def states_back_kernel(dbc, bca, bcp, msk, kern, cda_in, cm_in, dsp, mt, acc, cda, cm, buf, mbuf):
    @pl.when(pl.program_id(0) == 0)
    def _():
        buf[0:8, :] = cda_in[...]
        mbuf[0:8, :] = cm_in[...]
        acc[...] = jnp.zeros_like(acc)

    mbuf[BLK : BLK + 8, :] = mbuf[0:8, :]
    mbuf[0:BLK, :] = msk[...]
    a = bca[...]
    sa = sigmoid(a)
    da = dbc[...] * (sa * (1.0 + a * (1.0 - sa)))
    buf[BLK : BLK + 8, :] = buf[0:8, :]
    buf[0:BLK, :] = da
    xp = bcp[...]
    dx, taps = conv_back(da, xp, kern, buf, mbuf)
    low = dx.astype(bf16)
    dsp[...] = low
    mt[...] = jnp.broadcast_to(jnp.sum(low.astype(f32) * xp, axis=1, keepdims=True), (BLK, 128))
    for k in range(4):
        acc[8 * k : 8 * k + 8, :] += taps[k]
    acc[32:40, :] += fold(da)
    cda[...] = buf[0:8, :]
    cm[...] = mbuf[0:8, :]


def dn_kernel(dz, dxp, ddt, wa, wb, wdt, o):
    n = wa.shape[1] // 2
    v = nt(dz[:, :n], wa[:, :n]) + nt(dxp[:, :n], wa[:, n:])
    v = v + nt(dz[:, n:], wb[:, :n]) + nt(dxp[:, n:], wb[:, n:])
    o[...] = (v + nt(ddt[...], wdt[...])).astype(bf16)


def weight_kernel(count, tiles, extra, core, *refs):
    lhs, rhs, more, (keep, give) = refs[:count], refs[count : 2 * count], refs[2 * count : -2], refs[-2:]
    v = tn(lhs[0][...], rhs[0][...])
    for k in range(1, count):
        v = v + tn(lhs[k][...], rhs[k][...])
    if extra:
        part = lhs[0].shape[0]
        w = tn(lhs[0][...], more[0][:part, :])
        for k in range(1, count):
            w = w + tn(lhs[k][...], more[0][k * part : (k + 1) * part, :])
        n, m = v.shape[1] // 2, w.shape[1] // 2
        v = jnp.concatenate([v[:, :n], w[:, :m], v[:, n:], w[:, m:]], axis=1)
    step = pl.program_id(0)

    @pl.when(step < tiles)
    def _():
        keep[...] = v

    @pl.when(step >= tiles)
    def _():
        give[...] = v


def join_kernel(core, za, zb, xa, xb, o):
    first = pl.program_id(0) * 2 // pl.num_programs(0) == core[0]
    rows, lanes = za.shape
    parts = lanes // 128

    def put(z, x):
        for k in range(parts):
            at = slice(k * 128, k * 128 + 128)
            o[pl.ds(2 * k, rows, stride=2 * parts), :] = z[:, at].astype(f32)
            o[pl.ds(2 * k + 1, rows, stride=2 * parts), :] = x[:, at].astype(f32)

    @pl.when(first)
    def _():
        put(za, xa)

    @pl.when(jnp.logical_not(first))
    def _():
        put(zb, xb)


def tile(width, first=0):
    return pl.BlockSpec((BLK, width), lambda i, *_: (first + i, 0))


def back_tile(width, last):
    return pl.BlockSpec((BLK, width), lambda i, *_: (last - i, 0))


def whole(*shape):
    zeros = (0,) * len(shape)
    return pl.BlockSpec(shape, lambda i, *_: zeros)


def sds(shape, dtype):
    return jax.ShapeDtypeStruct(shape, dtype)


def call(
    kernel, grid, in_specs, out_specs, out_shape, scratch=(), flops=0, moved=0, prefetch=0, after=(), into=()
):
    first = prefetch + len(in_specs)
    extra = len(after) + len(into)

    def body(*refs):
        kernel(*refs[:first], *refs[first + extra :])

    fn = pl.pallas_call(
        body,
        grid_spec=pltpu.PrefetchScalarGridSpec(
            num_scalar_prefetch=prefetch,
            grid=(grid,),
            in_specs=list(in_specs) + [pl.BlockSpec(memory_space=pl.ANY)] * extra,
            out_specs=out_specs,
            scratch_shapes=list(scratch),
        ),
        out_shape=out_shape,
        input_output_aliases={first + len(after) + k: k for k in range(len(into))},
        compiler_params=pltpu.CompilerParams(
            dimension_semantics=("arbitrary",), vmem_limit_bytes=VMEM_LIMIT
        ),
        cost_estimate=pl.CostEstimate(flops=flops // COST, bytes_accessed=moved // COST, transcendentals=0),
    )
    return lambda *args: fn(*args, *after, *into)


def three(v):
    high = lax.optimization_barrier(v.astype(bf16))
    rest = v - high.astype(f32)
    mid = lax.optimization_barrier(rest.astype(bf16))
    return high, mid, (rest - mid.astype(f32)).astype(bf16)


def shards(
    hidden_in, starts, cotangent, norm_gain, w_zx, w_dt, w_bc, conv_x_w, conv_x_b,
    conv_bc_w, conv_bc_b, dt_bias, a_log, d_skip, gnorm_w, w_out,
):
    order = []

    def ordered(*args, after=(), **kw):
        def run(*operands):
            outs = call(*args, after=tuple(after) + tuple(order[-1:]), **kw)(*operands)
            order.append(jax.tree.leaves(outs)[-1])
            return outs

        return run

    groups = lax.axis_size("zline")
    parts = 2 * groups
    nrows = lax.axis_size("rows")
    zpos = lax.axis_index("zline")
    mine = lax.axis_index("pair")
    me = 2 * zpos + mine
    core = lax.axis_index("rows") % 2
    dim = hidden_in.shape[1]
    local_dim = cotangent.shape[1]
    lanes = w_zx.shape[2]
    heads = w_dt.shape[1]
    inner = lanes * parts
    docl = 2 * heads
    wide = dim // groups

    def swap(v):
        return lax.ppermute(v, "pair", [(0, 1), (1, 0)])

    def cross(v, bit):
        return lax.ppermute(v, "rows", [(i, i ^ bit) for i in range(nrows)])

    def line_sum(v):
        bit = 1
        while bit < groups:
            v = v + lax.ppermute(v, "zline", [(i, i ^ bit) for i in range(groups)])
            bit *= 2
        return v

    def rows_of(v, start, size):
        return lax.dynamic_slice_in_dim(v, start, size, 0)

    def zero_after(v):
        return (v.reshape(-1)[0].astype(f32) > 1e38).astype(jnp.int32)

    def late(v, after):
        return v + zero_after(after).astype(v.dtype)

    def half_of_partner(own, after):
        half = own.shape[0] // 2
        return swap(rows_of(own, core * half + zero_after(after), half))

    def with_other_half(got, after):
        other = cross(got, 1)
        first = core + zero_after(after) == 0
        return jnp.concatenate([jnp.where(first, got, other), jnp.where(first, other, got)], axis=0)

    w_a = w_zx.reshape(dim, 2 * lanes)
    o_a = w_out
    small = jnp.stack([dt_bias, a_log, d_skip]).reshape(-1)
    prm_a = jnp.concatenate(
        [
            conv_x_w,
            conv_x_b[None],
            gnorm_w[None],
            jnp.repeat(d_skip, HD)[None],
            jnp.pad(small, (0, lanes - small.shape[0]))[None],
        ],
        axis=0,
    )
    prm_b = swap(prm_a)
    small_b = prm_b[7, : 3 * heads].reshape(3, heads)
    wdt_a = w_dt.T
    wdt_b = swap(wdt_a)
    bias_all = jnp.concatenate([dt_bias, small_b[0]])
    rate_all = -jnp.exp(jnp.concatenate([a_log, small_b[1]]))
    dtp = jnp.pad(jnp.stack([bias_all, rate_all]), ((0, 6), (0, 128 - docl)))
    taps = jnp.concatenate([conv_bc_w, conv_bc_b[None]], axis=0).transpose(1, 2, 0)
    high, mid, low = three(taps)
    pack = jnp.concatenate([w_bc.transpose(1, 2, 0), high, mid, low], axis=2)
    pack = jnp.pad(pack, ((0, 0), (0, 0), (0, 128 - 15)))

    def grow(v, axis, bit, here):
        got = lax.ppermute(v, axis, [(i, i ^ bit) for i in range(lax.axis_size(axis))])
        return jnp.concatenate([jnp.where(here, got, v), jnp.where(here, v, got)], axis=1)

    pack = grow(pack, "pair", 1, mine == 1)
    is0 = mine == 0
    c_pair = [None] * CHUNKS

    def cotangent_of(j, follow, after=None):
        c_mine = rows_of(cotangent, mine * LEN + j * CT, CT)
        c_got = swap(rows_of(cotangent, (1 - mine) * LEN + j * CT + zero_after(follow), CT))
        low = is0 if after is None else mine + zero_after(after) == 0
        return c_got, jnp.concatenate(
            [jnp.where(low, c_mine, c_got), jnp.where(low, c_got, c_mine)], axis=1
        )

    c_got, c_pair[CHUNKS - 1] = cotangent_of(CHUNKS - 1, pack)
    w_got = half_of_partner(w_a, pack)
    o_got = half_of_partner(w_out, w_got)
    early = pack
    turned = [
        lax.ppermute(pack, "zline", [(i, (i + k) % groups) for i in range(groups)])
        for k in range(groups - 1, 0, -1)
    ]
    pack = jnp.concatenate((turned + [pack]) * 2, axis=1)
    size = 2 * w_bc.shape[2]
    pack = lax.dynamic_slice_in_dim(pack, (groups - 1 - zpos) * size, groups * size, 1)
    pack = pack.reshape(2 * NS, dim + 128)
    wbc = pack[:, :dim]
    taps = pack[:, dim : dim + 15].astype(f32).reshape(2 * NS, 3, 5).sum(axis=1)
    kern_bc = jnp.pad(taps.T, ((0, 3), (0, 0)))
    wdt = jnp.concatenate([wdt_a, wdt_b, jnp.zeros((128 - docl, dim), bf16)], axis=0)
    wst = jnp.concatenate([wbc, wdt], axis=0)

    st = rows_of(starts, mine * LEN, LEN).astype(f32)
    open1 = jnp.where(jnp.arange(LEN) == 0, 0.0, 1.0 - st)
    open2 = open1 * jnp.concatenate([jnp.zeros((1,), f32), open1[:-1]])
    open3 = open2 * jnp.concatenate([jnp.zeros((2,), f32), open1[:-2]])
    msk = jnp.pad(jnp.stack([st, open1, open2, open3], axis=1), ((0, 0), (0, 124)))
    which = mine.astype(jnp.int32).reshape(1)

    tl = (BLK, lanes)
    proj_out = [tile(lanes), tile(lanes), tile(lanes), tile(lanes)]
    proj_shape = [sds((LEN, lanes), bf16)] * 4
    pf = 2 * LEN * dim * 2 * lanes

    def first_step(part, start, after, into=()):
        at = part * NBLK // 2
        return ordered(
            first_kernel,
            NBLK // 2,
            [
                pl.BlockSpec((BLK, dim), lambda i, which: (which[0] * NBLK + at + i, 0)),
                whole(1, dim),
                whole(dim, 2 * lanes),
                whole(8, lanes),
                tile(128, at),
                whole(8, lanes),
            ],
            [tile(dim, at), tile(128, at)] + [tile(lanes, at)] * 4 + [whole(8, lanes)],
            [sds((LEN, dim), bf16), sds((LEN, 128), f32)] + proj_shape + [sds((8, lanes), f32)],
            [pltpu.VMEM((BLK + 8, lanes), f32)],
            flops=pf // 2,
            moved=20 << 20,
            prefetch=1,
            after=after,
            into=into,
        )(which, hidden_in, norm_gain.reshape(1, dim), w_a, prm_a, msk, start)

    *begun, tail = first_step(0, jnp.zeros((8, lanes), f32), (early,))
    normed, r_wide, z_a, xp_a, a_a, xs_a, tail = first_step(1, tail, tuple(turned), begun)
    bcp, bca, bc, dtr, dt, cum, cumt = ordered(
        functools.partial(states_kernel, docl),
        NBLK,
        [tile(dim), whole(2 * NS + 128, dim), whole(8, 2 * NS), whole(8, 128), tile(128)],
        [tile(2 * NS)] * 3 + [tile(128)] * 3 + [pl.BlockSpec((128, BLK), lambda i: (0, i))],
        [sds((LEN, 2 * NS), f32)] * 2
        + [sds((LEN, 2 * NS), bf16)]
        + [sds((LEN, 128), f32)] * 3
        + [sds((128, LEN), f32)],
        [pltpu.VMEM((BLK + 8, 2 * NS), f32)],
        flops=2 * LEN * dim * 512,
        moved=18 << 20,
        after=(c_pair[CHUNKS - 1],),
    )(normed, wst, kern_bc, dtp, msk)

    def scan(off, xs, z, prm, after=()):
        return ordered(
            functools.partial(scan_kernel, docl, off),
            NBLK,
            [
                tile(lanes), tile(lanes), tile(2 * NS), tile(128), tile(128),
                pl.BlockSpec((128, BLK), lambda i: (0, i)), whole(8, lanes),
            ],
            [tile(lanes), tile(lanes), pl.BlockSpec((1, NS, lanes), lambda i: (i, 0, 0)), tile(128)],
            [
                sds((LEN, lanes), f32),
                sds((LEN, lanes), bf16),
                sds((NBLK, NS, lanes), f32),
                sds((LEN, 128), f32),
            ],
            [pltpu.VMEM((NS, lanes), f32)],
            flops=10 << 30,
            moved=20 << 20,
            after=after,
        )(xs, z, bc, dt, cum, cumt, prm)

    y_a, gw_a, sin_a, pw_a = scan(0, xs_a, z_a, prm_a)
    for j in reversed(range(CHUNKS - 1)):
        c_pair[j] = cotangent_of(j, cumt, pw_a)[1]
    w_b = with_other_half(w_got, pw_a)
    z_b, xp_b, a_b, xs_b = ordered(
        second_kernel,
        NBLK,
        [tile(dim), whole(dim, 2 * lanes), whole(8, lanes), tile(128)],
        proj_out,
        proj_shape,
        [pltpu.VMEM((BLK + 8, lanes), f32)],
        flops=pf,
        moved=28 << 20,
    )(normed, w_b, prm_b, msk)
    y_b, gw_b, sin_b, pw_b = scan(heads, xs_b, z_b, prm_b)
    o_b = with_other_half(o_got, pw_b)

    class LineSum:
        def __init__(self, v):
            self.v = v
            self.left = groups - 1
            self.up = self.down = None

        def own(self, j):
            return lax.dynamic_slice_in_dim(self.v, jnp.clip(j, 0, groups - 1) * wide, wide, 1)

        def step(self, after=None):
            d = self.left
            if d == 0:
                return
            late = 0 if after is None else zero_after(after)
            send_u, send_d = self.own(zpos + d + late), self.own(zpos - d - late)
            if self.up is not None:
                send_u = (send_u.astype(f32) + self.up.astype(f32)).astype(bf16)
                send_d = (send_d.astype(f32) + self.down.astype(f32)).astype(bf16)
            self.up = lax.ppermute(send_u, "zline", [(i, i + 1) for i in range(groups - d)])
            self.down = lax.ppermute(send_d, "zline", [(i, i - 1) for i in range(d, groups)])
            self.left = d - 1

        def result(self):
            while self.left:
                self.step()
            return self.own(zpos).astype(f32) + self.up.astype(f32) + self.down.astype(f32)

    c_all = [None] * CHUNKS
    for j in reversed(range(CHUNKS)):
        c_all[j] = lax.all_gather(c_pair[j], "zline", axis=1, tiled=True)

    power = pw_a[:, 0] + pw_b[:, 0]
    wdt_t = wdt.T
    wbc_near = lax.dynamic_slice_in_dim(wbc, zpos * wide, wide, 1)

    def dyn_step(j, after=()):
        return ordered(
            dyn_kernel,
            CB,
            [tile(dim), whole(lanes, dim), whole(lanes, dim), tile(lanes, j * CB), tile(lanes, j * CB)],
            [tile(lanes), tile(lanes), tile(128)],
            [sds((CT, lanes), bf16)] * 2 + [sds((CT, 128), f32)],
            flops=4 * CT * lanes * dim,
            moved=12 << 20,
            after=after,
        )(c_all[j], o_a, o_b, gw_a, gw_b)

    def scales_of(j, qs):
        sums = line_sum(jnp.concatenate([power[j * CT : (j + 1) * CT], qs[:, 0]]))
        s = lax.rsqrt(sums[:CT] / inner + EPSILON)
        kq = s * s * s * (sums[CT:] / inner)
        return s, jnp.pad(jnp.stack([s, kq], axis=1), ((0, 0), (0, 126)))

    def gate_step(j, sq, d_a, d_b, after=()):
        return ordered(
            gate_kernel,
            CB,
            [tile(128)] + [tile(lanes)] * 2 + [tile(lanes, j * CB)] * 4 + [whole(8, lanes)] * 2,
            [tile(2 * lanes)] * 3 + [tile(128), whole(8, 2 * lanes)],
            [sds((CT, 2 * lanes), bf16)] * 3 + [sds((CT, 128), f32), sds((8, 2 * lanes), f32)],
            flops=4000 * CT * lanes,
            moved=20 << 20,
            after=after,
        )(sq, d_a, d_b, y_a, y_b, z_a, z_b, prm_a, prm_b)

    def back_step(j, dy, ds, cda, cm, after=()):
        last = j * CB + CB - 1

        def bt(width):
            return back_tile(width, last)

        def loc(width):
            return back_tile(width, CB - 1)

        cols = pl.BlockSpec((128, BLK), lambda i: (0, last - i))
        sins = pl.BlockSpec((1, NS, lanes), lambda i: (last - i, 0, 0))
        return ordered(
            functools.partial(back_kernel, docl),
            CB,
            [
                loc(2 * lanes), bt(2 * NS), bt(128), bt(128), cols, bt(128), bt(128), whole(8, 128),
                bt(lanes), bt(lanes), bt(lanes), bt(lanes), bt(lanes), bt(lanes), bt(lanes), bt(lanes),
                sins, sins, whole(8, lanes), whole(8, lanes),
                whole(2, NS, lanes), whole(2, 8, lanes), whole(8, 128),
            ],
            [
                loc(2 * lanes), loc(128), loc(2 * NS), loc(128), whole(2, 48, lanes), whole(16, 128),
                whole(2, NS, lanes), whole(2, 8, lanes), whole(8, 128),
            ],
            [
                sds((CT, 2 * lanes), bf16), sds((CT, 128), bf16), sds((CT, 2 * NS), bf16),
                sds((CT, 128), f32), sds((2, 48, lanes), f32), sds((16, 128), f32),
                sds((2, NS, lanes), f32), sds((2, 8, lanes), f32), sds((8, 128), f32),
            ],
            [pltpu.VMEM((2, BLK + 8, lanes), f32), pltpu.VMEM((BLK + 8, 128), f32)],
            flops=(80 << 30) // CHUNKS,
            moved=(80 << 20) // CHUNKS,
            after=after,
        )(
            dy, bc, dt, cum, cumt, dtr, msk, dtp,
            y_a, y_b, xs_a, xs_b, a_a, a_b, xp_a, xp_b, sin_a, sin_b, prm_a, prm_b,
            ds, cda, cm,
        )

    def states_sum(v, *after):
        bit = 1
        after = list(after)
        while bit < groups:
            if after:
                v = late(v, after.pop(0))
            got = lax.ppermute(v.astype(bf16), "zline", [(i, i ^ bit) for i in range(groups)])
            v = v.astype(f32) + got.astype(f32)
            bit *= 2
        return v

    def states_step(j, dbc, sda, scm, after=()):
        last = j * CB + CB - 1

        def bt(width):
            return back_tile(width, last)

        def loc(width):
            return back_tile(width, CB - 1)

        return ordered(
            states_back_kernel,
            CB,
            [loc(2 * NS), bt(2 * NS), bt(2 * NS), bt(128), whole(8, 2 * NS), whole(8, 2 * NS), whole(8, 128)],
            [loc(2 * NS), loc(128), whole(40, 2 * NS), whole(8, 2 * NS), whole(8, 128)],
            [
                sds((CT, 2 * NS), bf16), sds((CT, 128), f32), sds((40, 2 * NS), f32),
                sds((8, 2 * NS), f32), sds((8, 128), f32),
            ],
            [pltpu.VMEM((BLK + 8, 2 * NS), f32), pltpu.VMEM((BLK + 8, 128), f32)],
            flops=CHEAP,
            moved=CHEAP,
            after=after,
        )(dbc, bca, bcp, msk, kern_bc, sda, scm)

    def dn_step(dz, dxp, ddt, after=()):
        return ordered(
            dn_kernel,
            4,
            [
                whole(CT, 2 * lanes), whole(CT, 2 * lanes), whole(CT, 128),
                pl.BlockSpec((dim // 4, 2 * lanes), lambda i: (i, 0)),
                pl.BlockSpec((dim // 4, 2 * lanes), lambda i: (i, 0)),
                pl.BlockSpec((dim // 4, 128), lambda i: (i, 0)),
            ],
            pl.BlockSpec((CT, dim // 4), lambda i: (0, i)),
            sds((CT, dim), bf16),
            flops=8 * CT * lanes * dim,
            moved=16 << 20,
            after=after,
        )(dz, dxp, ddt, w_a, w_b, wdt_t)

    def near_sum(dn):
        return lax.psum_scatter(dn, "zline", scatter_dimension=1, tiled=True)

    def near_step(total, dsp):
        total = total.astype(f32) + jnp.dot(dsp, wbc_near, preferred_element_type=f32)
        keep = lax.dynamic_slice_in_dim(total, mine * local_dim, local_dim, 1)
        give = lax.dynamic_slice_in_dim(total, (1 - mine) * local_dim, local_dim, 1)
        return keep, swap(give.astype(bf16))

    core_at = core.astype(jnp.int32).reshape(1)

    def weight_grad(lhs, rhs, more=None):
        count = len(rhs)
        n, m = lhs[0].shape[1], rhs[0].shape[1]
        part = LEN // count
        more = [] if more is None else [more]
        full = m + sum(v.shape[1] for v in more)
        size = min(256, n // 4)
        tiles = n // size // 2

        def order(i, core):
            return jnp.where(i < tiles, i + core[0] * tiles, i - core[0] * tiles)

        return ordered(
            functools.partial(weight_kernel, count, tiles, len(more)),
            2 * tiles,
            [
                pl.BlockSpec(
                    (part, size),
                    lambda i, core, at=0 if v.shape[0] == part else k: (at, order(i, core)),
                )
                for k, v in enumerate(lhs)
            ]
            + [whole(part, m)] * count
            + [whole(*v.shape) for v in more],
            [
                pl.BlockSpec((size, full), lambda i, core: (jnp.minimum(i, tiles - 1), 0)),
                pl.BlockSpec((size, full), lambda i, core: (jnp.maximum(i - tiles, 0), 0)),
            ],
            [sds((n // 2, full), f32)] * 2,
            flops=CHEAP,
            moved=CHEAP,
            prefetch=1,
        )(core_at, *lhs, *rhs, *more)

    dz, dy, yn, mtg, scales = ([None] * CHUNKS for _ in range(5))
    dxp, ddt, dsp, near, far, dns = ([None] * CHUNKS for _ in range(6))
    ggs, accs, accs_dt, accs_bc = [], [], [], []
    carry = (jnp.zeros((2, NS, lanes), f32), jnp.zeros((2, 8, lanes), f32), jnp.zeros((8, 128), f32))
    state_carry = (jnp.zeros((8, 2 * NS), f32), jnp.zeros((8, 128), f32))

    def out_step(j):
        return ordered(
            out_kernel,
            CB,
            [tile(lanes, j * CB)] * 2 + [whole(lanes, dim)] * 2,
            tile(dim),
            sds((CT, dim), bf16),
            flops=4 * CT * lanes * dim,
            moved=10 << 20,
        )(gw_a, gw_b, o_a, o_b)

    top = CHUNKS - 1
    d_a, d_b, qs = dyn_step(top)
    scales[top], sq = scales_of(top, qs)
    mixing = LineSum(out_step(top))
    mixing.step(after=sq)

    dz[1], dy[1], yn[1], mtg[1], gg = gate_step(1, sq, d_a, d_b)
    ggs.append(gg)
    dxp[1], ddt[1], dbc_1, mtb_1, acc, acc_dt, *carry = back_step(1, dy[1], *carry)
    accs.append(acc)
    accs_dt.append(acc_dt)
    dns[1] = dn_step(dz[1], dxp[1], ddt[1], after=(mixing.up, mixing.down))
    total_1 = near_sum(dns[1])
    d_a, d_b, qs = dyn_step(0)
    scales[0], sq = scales_of(0, qs)
    partial_0 = out_step(0)
    dz[0], dy[0], yn[0], mtg[0], gg = gate_step(0, sq, d_a, d_b)
    ggs.append(gg)
    mixing.step(after=sq)
    g_out = weight_grad(c_all, yn)
    g_z = weight_grad([normed] * CHUNKS, dz)
    mixing_2 = (mixing.up, mixing.down)
    mixing.step(after=g_z[0])
    dxp[0], ddt[0], dbc_0, mtb_0, acc, acc_dt, *carry = back_step(
        0, dy[0], *carry, after=mixing_2
    )
    accs.append(acc)
    accs_dt.append(acc_dt)
    dns[0] = dn_step(dz[0], dxp[0], ddt[0], after=(total_1,))
    total_0 = near_sum(dns[0])
    mixed_0 = near_sum(partial_0)
    g_x = weight_grad([normed] * CHUNKS, dxp)
    summed_1 = states_sum(dbc_1, dbc_0, g_x[0])
    summed_0 = states_sum(dbc_0, dbc_0, g_x[0])
    dsp[1], mtc_1, acc_bc, *state_carry = states_step(1, summed_1, *state_carry)
    accs_bc.append(acc_bc)
    dsp[0], mtc_0, acc_bc, *state_carry = states_step(0, summed_0, *state_carry)
    accs_bc.append(acc_bc)

    cols = w_bc.shape[2]
    dsp_near = lax.dynamic_slice_in_dim(
        jnp.concatenate(dsp, axis=0).reshape(LEN, 2, NS), zpos * 2 * cols, 2 * cols, 2
    ).reshape(LEN, 2, 2, cols)
    ddt_all = jnp.concatenate(ddt, axis=0)
    width = 2 * cols + heads

    def few(q):
        sel = lax.dynamic_index_in_dim(dsp_near, q, 2, keepdims=False).reshape(LEN, 2 * cols)
        dts = lax.dynamic_slice_in_dim(ddt_all, jnp.where(q == mine, 0, heads), heads, 1)
        return jnp.concatenate([sel, dts, jnp.zeros((LEN, 128 - width), bf16)], axis=1)

    fewer = jnp.concatenate([few(mine), few(1 - mine)], axis=1)
    g_few = weight_grad([normed], [fewer])
    near[1], far[1] = near_step(total_1, dsp[1])
    near[0], far[0] = near_step(total_0, dsp[0])
    local_sum = jnp.concatenate([mtg[j][:, 0] + m[:, 0] for j, m in ((0, mtb_0), (1, mtb_1))])
    mean_sum = line_sum(local_sum) + jnp.concatenate([mtc_0[:, 0], mtc_1[:, 0]])
    mixer = jnp.concatenate([mixed_0.astype(f32), mixing.result()], axis=0)

    def bit_of(bit):
        return lax.axis_index("rows") // bit % 2

    def reduce_pair(keep, give):
        n = keep.shape[1] // 2
        v = keep + cross(give, 1)
        v = v[:, :n] + swap(v[:, n:].astype(bf16)).astype(f32)
        bit = 2
        while bit < nrows:
            size = v.shape[0] // 2
            up = bit_of(bit)
            give = rows_of(v, (1 - up) * size, size)
            v = rows_of(v, up * size, size) + cross(give.astype(bf16), bit).astype(f32)
            bit *= 2
        v = lax.reduce_precision(v, 8, 7).astype(bf16)
        while bit > 2:
            bit //= 2
            got = cross(v, bit)
            low = bit_of(bit) == 0
            v = jnp.concatenate([jnp.where(low, v, got), jnp.where(low, got, v)], axis=0)
        return v

    def both_cores(v):
        got = cross(v, 1)
        first = core == 0
        return jnp.concatenate([jnp.where(first, v, got), jnp.where(first, got, v)], axis=0)

    g_x, g_z, g_out, g_few = (reduce_pair(*g) for g in (g_x, g_z, g_out, g_few))
    grad_w_out = both_cores(g_out).T.astype(f32)
    g_few = both_cores(g_few).astype(f32)
    grad_w_bc = g_few[:, : 2 * cols].reshape(dim, 2, cols)
    grad_w_dt = g_few[:, 2 * cols : width]
    x_far, z_far = cross(g_x, 1), cross(g_z, 1)
    steps = 8
    size = dim // steps
    at = pl.BlockSpec((size, lanes), lambda i, core: (i % (steps // 2), 0))
    grad_w_zx = ordered(
        join_kernel,
        steps,
        [at] * 4,
        pl.BlockSpec((size * 2 * lanes // 128, 128), lambda i, core: (i, 0)),
        sds((dim * 2 * lanes // 128, 128), f32),
        moved=24 << 20,
        prefetch=1,
    )(core_at, g_z, z_far, g_x, x_far)
    grad_w_zx = grad_w_zx.reshape(dim, lanes // 128, 2, 128).transpose(0, 2, 1, 3)
    grad_w_zx = grad_w_zx.reshape(dim, 2, lanes)

    acc = sum(accs).reshape(2, 6, 8, lanes).sum(axis=2)
    gg = sum(ggs).sum(axis=0).reshape(2, 1, lanes)
    acc_dt = sum(accs_dt).reshape(2, 8, 128).sum(axis=1)[:, :docl].reshape(2, 2, heads)
    acc_dt = jnp.pad(acc_dt.transpose(1, 0, 2).reshape(2, 1, -1), ((0, 0), (0, 0), (0, lanes - docl)))
    vec = jnp.concatenate([acc, gg, acc_dt], axis=1)
    acc_bc = sum(accs_bc).reshape(5, 8, 2 * NS).sum(axis=1)

    def rows_sum(v):
        bit = 1
        while bit < nrows:
            v = v + cross(v, bit)
            bit *= 2
        return v

    vec = rows_sum(vec[0] + swap(vec[1]))
    acc_bc = rows_sum(acc_bc + swap(acc_bc)).reshape(5, 2, NS)
    acc_bc = lax.dynamic_slice_in_dim(acc_bc, me * cols, cols, 2)

    s_all = jnp.concatenate(scales)
    out_near = mixer * s_all[:, None]
    o_own = lax.dynamic_slice_in_dim(out_near, mine * local_dim, local_dim, 1)
    o_far = swap(
        lax.dynamic_slice_in_dim(out_near, (1 - mine) * local_dim, local_dim, 1).astype(bf16)
    )
    r_own = r_wide[:, 0]
    m_own = mean_sum
    r_far = swap(r_own)
    m_far = swap(m_own)
    d_own = jnp.concatenate(near, axis=0)
    d_far = jnp.concatenate(far, axis=0)
    x_near = lax.dynamic_slice_in_dim(hidden_in, me * local_dim, local_dim, 1).astype(f32)
    gain = lax.dynamic_slice_in_dim(norm_gain, me * local_dim, local_dim, 0)
    outs, grads, gain_sum = [], [], 0.0
    for q in range(2):
        sel = mine == q
        x = x_near[q * LEN : (q + 1) * LEN]
        cot = cotangent[q * LEN : (q + 1) * LEN].astype(f32)
        outs.append((x + jnp.where(sel, o_own, o_far.astype(f32))).astype(bf16))
        d = jnp.where(sel, d_own, d_far.astype(f32))
        r = jnp.where(sel, r_own, r_far)[:, None]
        m = jnp.where(sel, m_own, m_far)[:, None]
        grads.append(cot + r * (d * gain) - x * (r * r) * (m / dim))
        gain_sum = gain_sum + jnp.sum(d * x * r, axis=0)
    return (
        jnp.concatenate(outs, axis=0),
        jnp.concatenate(grads, axis=0),
        rows_sum(gain_sum),
        grad_w_zx,
        grad_w_dt,
        grad_w_bc,
        vec[:4],
        vec[4],
        acc_bc[:4],
        acc_bc[4],
        vec[7, heads : 2 * heads],
        vec[7, :heads],
        vec[5].reshape(heads, HD).sum(axis=1),
        vec[6],
        grad_w_out,
    )


STATE = ("zline", "pair")


def solution(mesh):
    placed = (
        P("rows", None),
        P("rows"),
        P("rows", STATE),
        P(),
        P(None, None, STATE),
        P(None, STATE),
        P(None, None, STATE),
        P(None, STATE),
        P(STATE),
        P(None, None, STATE),
        P(None, STATE),
        P(STATE),
        P(STATE),
        P(STATE),
        P(STATE),
        P(STATE, None),
    )
    rows, parts = mesh.devices.shape
    split = Mesh(mesh.devices.reshape(rows, parts // 2, 2), ("rows", "zline", "pair"))
    return jax.shard_map(
        shards,
        mesh=split,
        in_specs=placed,
        out_specs=(
            P("rows", STATE),
            P("rows", STATE),
            P(STATE),
            P(None, None, STATE),
            P(None, STATE),
            P(None, None, STATE),
            P(None, STATE),
            P(STATE),
            P(None, None, STATE),
            P(None, STATE),
            P(STATE),
            P(STATE),
            P(STATE),
            P(STATE),
            P(STATE, None),
        ),
        check_vma=False,
    )
```

```python
import functools

import jax
import jax.numpy as jnp
from jax import lax
from jax.experimental import pallas as pl
from jax.experimental.pallas import tpu as pltpu
from jax.sharding import Mesh
from jax.sharding import PartitionSpec as P

LEN = 2048
BLK = 256
NBLK = LEN // BLK
CHUNKS = 2
CT = LEN // CHUNKS
CB = CT // BLK
HD = 64
NS = 128
EPSILON = 1e-05
HIGHEST = lax.Precision.HIGHEST
f32 = jnp.float32
bf16 = jnp.bfloat16
COST = 1
CHEAP = 1 << 16
VMEM_LIMIT = 56 * 1024 * 1024


def nn(a, b, **kw):
    return lax.dot_general(a, b, (((1,), (0,)), ((), ())), preferred_element_type=f32, **kw)


def nt(a, b):
    return lax.dot_general(a, b, (((1,), (1,)), ((), ())), preferred_element_type=f32)


def tn(a, b):
    return lax.dot_general(a, b, (((0,), (0,)), ((), ())), preferred_element_type=f32)


def iota(shape, dim):
    return lax.broadcasted_iota(jnp.int32, shape, dim)


def sigmoid(v):
    return 1.0 / (1.0 + jnp.exp(-v))


def fold(v):
    return v.reshape(v.shape[0] // 8, 8, v.shape[1]).sum(axis=0)


def expand(cols, off, heads):
    low = iota((cols.shape[0], 128), 1) < HD
    pieces = []
    for p in range(heads // 2):
        a = cols[:, off + 2 * p : off + 2 * p + 1]
        b = cols[:, off + 2 * p + 1 : off + 2 * p + 2]
        pieces.append(jnp.where(low, a, b))
    return jnp.concatenate(pieces, axis=1)


def quad_masks(rows):
    head = iota((rows, 4 * HD), 1) // HD
    return [head == h for h in range(4)]


def stacked(v, masks):
    zero = jnp.zeros_like(v)
    return jnp.concatenate([jnp.where(m, v, zero) for m in masks], axis=0)


def segment_sums(v, off):
    n = v.shape[1]
    pick = (iota((n, 128), 1) == iota((n, 128), 0) // HD + off).astype(bf16)
    high = v.astype(bf16)
    rest = (v - high.astype(f32)).astype(bf16)
    return nn(high, pick) + nn(rest, pick)


def conv_tile(step, x1, kern, msk, buf, start=None):
    @pl.when(step == 0)
    def _():
        buf[0:8, :] = jnp.zeros((8, buf.shape[1]), f32) if start is None else start[...]

    buf[8 : 8 + BLK, :] = x1
    acc = kern[4:5, :] + kern[3:4, :] * x1
    for k in range(1, 4):
        acc = acc + kern[3 - k : 4 - k, :] * (buf[8 - k : 8 - k + BLK, :] * msk[:, k : k + 1])
    buf[0:8, :] = x1[BLK - 8 :, :]
    return acc


def project_tile(n, w, kern, msk, z, xp, a, xs, buf, start=None):
    lanes = w.shape[1] // 2
    p = nn(n, w[...])
    z[...] = p[:, :lanes].astype(bf16)
    x1 = p[:, lanes:]
    xp[...] = x1.astype(bf16)
    acc = conv_tile(pl.program_id(0), x1, kern, msk, buf, start)
    a[...] = acc.astype(bf16)
    xs[...] = (acc * sigmoid(acc)).astype(bf16)


def first_kernel(which, hid, gain, w, kern, msk, start, normed, r, z, xp, a, xs, tail, buf):
    x = hid[...].astype(f32)
    rr = lax.rsqrt(jnp.mean(x * x, axis=1, keepdims=True) + EPSILON)
    n = (x * rr * gain[...]).astype(bf16)
    normed[...] = n
    r[...] = jnp.broadcast_to(rr, (BLK, 128))
    project_tile(n, w, kern, msk, z, xp, a, xs, buf, start)
    tail[...] = buf[0:8, :]


def second_kernel(normed, w, kern, msk, start, z, xp, a, xs, tail, buf):
    project_tile(normed[...], w, kern, msk, z, xp, a, xs, buf, start)
    tail[...] = buf[0:8, :]


def states_kernel(docl, normed, ws, kern, dtp, msk, bcp, bca, bc, dtr, dt, cum, cumt, buf):
    q = nt(normed[...], ws[...])
    x1 = q[:, : 2 * NS]
    bcp[...] = x1
    acc = conv_tile(pl.program_id(0), x1, kern, msk, buf)
    bca[...] = acc
    bc[...] = (acc * sigmoid(acc)).astype(bf16)
    d = q[:, 2 * NS :]
    dtr[...] = d
    v = d + dtp[0:1, :]
    e = jnp.exp(-jnp.abs(v))
    small = e * (1.0 - e * (0.5 - e * (1.0 / 3.0 - 0.25 * e)))
    step = jnp.maximum(v, 0.0) + jnp.where(e < 0.01, small, jnp.log(1.0 + e))
    lane = iota((BLK, 128), 1)
    step = jnp.where(lane < docl, step, 0.0)
    dt[...] = step
    ext = jnp.where(lane == docl, msk[:, 0:1], step * dtp[1:2, :])
    tri = (iota((BLK, BLK), 0) >= iota((BLK, BLK), 1)).astype(f32)
    c = nn(tri, ext, precision=HIGHEST)
    cum[...] = c
    cumt[...] = c.T


def block_scalars(docl, cum):
    lane = iota((BLK, 128), 1)
    doc = cum[:, docl : docl + 1]
    doc_last = cum[BLK - 1 : BLK, docl : docl + 1]
    rates = jnp.where(lane < docl, cum, 0.0)
    last = rates[BLK - 1 : BLK, :]
    lead = jnp.exp(rates) * (doc == 0.0).astype(f32)
    trail = jnp.exp(last - rates) * (doc == doc_last).astype(f32)
    retain = jnp.exp(last) * (doc_last == 0.0).astype(f32)
    return lead, trail, retain


def scan_kernel(docl, off, xs, z, bc, dt, cum, cumt, prm, start, y, gw, sin, pw, state):
    lanes = xs.shape[1]
    heads = lanes // HD

    @pl.when(pl.program_id(0) == 0)
    def _():
        state[...] = start[...]

    s_in = state[...]
    sin[0] = s_in
    b = bc[:, :NS]
    c = bc[:, NS:]
    cumv = cum[...]
    lead, trail, retain = block_scalars(docl, cumv)
    within = (cumv[:, docl : docl + 1] == cumt[docl : docl + 1, :]) & (
        iota((BLK, BLK), 0) >= iota((BLK, BLK), 1)
    )
    bias = jnp.where(within, 0.0, -1e30)
    g = nt(c, b)
    xf = xs[...].astype(f32)
    u = xf * expand(dt[...], off, heads)
    ub = u.astype(bf16)
    masks = quad_masks(BLK)
    parts = []
    for q in range(heads // 4):
        mixes = []
        for h in range(off + 4 * q, off + 4 * q + 4):
            decay = jnp.exp((cumv[:, h : h + 1] - cumt[h : h + 1, :]) + bias)
            mixes.append((decay * g).astype(bf16))
        uq = ub[:, q * 256 : q * 256 + 256]
        parts.append(nn(jnp.concatenate(mixes, axis=1), stacked(uq, masks)))
    yv = jnp.concatenate(parts, axis=1)
    yv = yv + nn(c, s_in.astype(bf16)) * expand(lead, off, heads) + prm[6:7, :] * xf
    y[...] = yv
    ut = (u * expand(trail, off, heads)).astype(bf16)
    state[...] = s_in * expand(retain, off, heads) + tn(b, ut)
    zz = z[...].astype(f32)
    gated = yv * zz * sigmoid(zz)
    gw[...] = (gated * prm[5:6, :]).astype(bf16)
    pw[...] = jnp.broadcast_to(jnp.sum(gated * gated, axis=1, keepdims=True), (BLK, 128))


def out_kernel(ga, gb, wa, wb, o):
    o[...] = (nn(ga[...], wa[...]) + nn(gb[...], wb[...])).astype(bf16)


def dyn_kernel(c, wa, wb, ga, gb, da, db, qs):
    cv = c[...]
    a = nt(cv, wa[...])
    b = nt(cv, wb[...])
    da[...] = a.astype(bf16)
    db[...] = b.astype(bf16)
    q = jnp.sum(a * ga[...].astype(f32), axis=1, keepdims=True)
    q = q + jnp.sum(b * gb[...].astype(f32), axis=1, keepdims=True)
    qs[...] = jnp.broadcast_to(q, (BLK, 128))


def gate_kernel(sq, da, db, ya, yb, za, zb, prma, prmb, dz, dy, yn, mt, gg):
    lanes = da.shape[1]
    s = sq[:, 0:1]
    kq = sq[:, 1:2]

    @pl.when(pl.program_id(0) == 0)
    def _():
        gg[...] = jnp.zeros_like(gg)

    total = jnp.zeros((BLK, 1), f32)
    for half, (dref, yref, zref, prm) in enumerate(((da, ya, za, prma), (db, yb, zb, prmb))):
        at = slice(half * lanes, half * lanes + lanes)
        dn = dref[...].astype(f32)
        y = yref[...]
        z = zref[...].astype(f32)
        gn = prm[5:6, :]
        sg = sigmoid(z)
        act = z * sg
        g = y * act
        gs = g * s
        yn[:, at] = (gs * gn).astype(bf16)
        gg[:, at] += fold(dn * gs)
        dg = s * (dn * gn) - g * kq
        dy[:, at] = (dg * act).astype(bf16)
        low = (dg * y * (sg * (1.0 + z * (1.0 - sg)))).astype(bf16)
        dz[:, at] = low
        total = total + jnp.sum(low.astype(f32) * z, axis=1, keepdims=True)
    mt[...] = jnp.broadcast_to(total, (BLK, 128))


def conv_back(da, xp, kern, buf, mbuf):
    dx = kern[3:4, :] * da
    taps = [None, None, None, fold(xp * da)]
    for k in range(1, 4):
        sh = buf[k : k + BLK, :] * mbuf[k : k + BLK, k : k + 1]
        dx = dx + kern[3 - k : 4 - k, :] * sh
        taps[3 - k] = fold(xp * sh)
    return dx, taps


def back_kernel(
    docl,
    dy, bc, dt, cum, cumt, dtr, msk, dtp,
    ya, yb, xsa, xsb, aa, ab, xpa, xpb, sia, sib, prma, prmb,
    ds_in, cda_in, cm_in,
    dxp, ddt, dbc, mt, acc, accs, ds, cda, cm,
    buf, mbuf,
):
    lanes = xsa.shape[1]
    heads = lanes // HD
    step = pl.program_id(0)

    @pl.when(step == 0)
    def _():
        ds[...] = ds_in[...]
        buf[:, 0:8, :] = cda_in[...]
        mbuf[0:8, :] = cm_in[...]
        acc[...] = jnp.zeros_like(acc)
        accs[...] = jnp.zeros_like(accs)

    mbuf[BLK : BLK + 8, :] = mbuf[0:8, :]
    mbuf[0:BLK, :] = msk[...]
    b = bc[:, :NS]
    c = bc[:, NS:]
    cumv = cum[...]
    lead, trail, retain = block_scalars(docl, cumv)
    within = (cumv[:, docl : docl + 1] == cumt[docl : docl + 1, :]) & (
        iota((BLK, BLK), 0) <= iota((BLK, BLK), 1)
    )
    bias = jnp.where(within, 0.0, -1e30)
    gt = nt(b, c)
    masks = quad_masks(BLK)
    dgt = jnp.zeros((BLK, BLK), f32)
    d_c = jnp.zeros((BLK, NS), f32)
    d_b = jnp.zeros((BLK, NS), f32)
    r1 = jnp.zeros((BLK, 128), f32)
    r2 = jnp.zeros((BLK, 128), f32)
    r3 = jnp.zeros((BLK, 128), f32)
    held = jnp.zeros((8, 128), f32)
    total = jnp.zeros((BLK, 1), f32)
    refs = ((ya, xsa, aa, xpa, sia, prma), (yb, xsb, ab, xpb, sib, prmb))
    for half, (yr, xsr, ar, xpr, sir, prm) in enumerate(refs):
        off = half * heads
        at = slice(half * lanes, half * lanes + lanes)
        dyb = dy[:, at]
        dyf = dyb.astype(f32)
        skip = prm[6:7, :]
        xf = xsr[...].astype(f32)
        dte = expand(dt[...], off, heads)
        u = xf * dte
        ub = u.astype(bf16)
        ubf = ub.astype(f32)
        s_in = sir[0]
        d_state = ds[half]
        dsb = d_state.astype(bf16)
        te = expand(trail, off, heads)
        tb = te * nn(b, dsb)
        parts = []
        for q in range(heads // 4):
            uq = ub[:, q * 256 : q * 256 + 256]
            dq = dyb[:, q * 256 : q * 256 + 256]
            dmt = nt(stacked(uq, masks), dq)
            mixes = []
            for i in range(4):
                h = off + 4 * q + i
                decay = jnp.exp((cumt[h : h + 1, :] - cumv[:, h : h + 1]) + bias)
                mixes.append((decay * gt).astype(bf16))
                dgt = dgt + dmt[i * BLK : i * BLK + BLK, :] * decay
            parts.append(nn(jnp.concatenate(mixes, axis=1), stacked(dq, masks)))
        du = jnp.concatenate(parts, axis=1) + tb
        ldy = (expand(lead, off, heads) * dyf).astype(bf16)
        d_c = d_c + nt(ldy, s_in.astype(bf16))
        d_b = d_b + nt((te * u).astype(bf16), dsb)
        ds[half] = d_state * expand(retain, off, heads) + tn(c, ldy)
        r1 = r1 + segment_sums(dyf * (yr[...] - skip * xf) - ubf * du, off)
        r2 = r2 + segment_sums(ubf * tb, off)
        r3 = r3 + segment_sums(xf * du, off)
        held = held + segment_sums(fold(d_state * s_in), off)
        a = ar[...].astype(f32)
        sa = sigmoid(a)
        da = (dte * du + skip * dyf) * (sa * (1.0 + a * (1.0 - sa)))
        buf[half, BLK : BLK + 8, :] = buf[half, 0:8, :]
        buf[half, 0:BLK, :] = da
        xp = xpr[...].astype(f32)
        dx, taps = conv_back(da, xp, prm, buf.at[half], mbuf)
        low = dx.astype(bf16)
        dxp[:, at] = low
        total = total + jnp.sum(low.astype(f32) * xp, axis=1, keepdims=True)
        for k in range(4):
            acc[half, 8 * k : 8 * k + 8, :] += taps[k]
        acc[half, 32:40, :] += fold(da)
        acc[half, 40:48, :] += fold(dyf * xf)
    dgb = dgt.astype(bf16)
    dbc[:, :NS] = (d_b + nn(dgb, c)).astype(bf16)
    dbc[:, NS:] = (d_c + tn(dgb, b)).astype(bf16)
    at_last = jnp.sum(r2, axis=0, keepdims=True) + retain * jnp.sum(held, axis=0, keepdims=True)
    dcum = r1 + jnp.where(iota((BLK, 128), 0) == BLK - 1, at_last, 0.0)
    later = (iota((BLK, BLK), 1) >= iota((BLK, BLK), 0)).astype(f32)
    drate = nn(later, dcum, precision=HIGHEST)
    rate = dtp[1:2, :]
    lane = iota((BLK, 128), 1)
    draw = jnp.where(lane < docl, (r3 + rate * drate) * sigmoid(dtr[...] + dtp[0:1, :]), 0.0)
    low = draw.astype(bf16)
    ddt[...] = low
    accs[0:8, :] += fold(drate * dt[...]) * rate
    accs[8:16, :] += fold(draw)
    total = total + jnp.sum(low.astype(f32) * dtr[...], axis=1, keepdims=True)
    mt[...] = jnp.broadcast_to(total, (BLK, 128))
    cda[...] = buf[:, 0:8, :]
    cm[...] = mbuf[0:8, :]


def states_back_kernel(dbc, bca, bcp, msk, kern, cda_in, cm_in, dsp, mt, acc, cda, cm, buf, mbuf):
    @pl.when(pl.program_id(0) == 0)
    def _():
        buf[0:8, :] = cda_in[...]
        mbuf[0:8, :] = cm_in[...]
        acc[...] = jnp.zeros_like(acc)

    mbuf[BLK : BLK + 8, :] = mbuf[0:8, :]
    mbuf[0:BLK, :] = msk[...]
    a = bca[...]
    sa = sigmoid(a)
    da = dbc[...].astype(f32) * (sa * (1.0 + a * (1.0 - sa)))
    buf[BLK : BLK + 8, :] = buf[0:8, :]
    buf[0:BLK, :] = da
    xp = bcp[...]
    dx, taps = conv_back(da, xp, kern, buf, mbuf)
    low = dx.astype(bf16)
    dsp[...] = low
    mt[...] = jnp.broadcast_to(jnp.sum(low.astype(f32) * xp, axis=1, keepdims=True), (BLK, 128))
    for k in range(4):
        acc[8 * k : 8 * k + 8, :] += taps[k]
    acc[32:40, :] += fold(da)
    cda[...] = buf[0:8, :]
    cm[...] = mbuf[0:8, :]


def dn_kernel(dz, dxp, ddt, dbc, wa, wb, wdt, o):
    n = wa.shape[1] // 2
    wide = wa.shape[0]
    v = nt(dz[:, :n], wa[:, :n]) + nt(dxp[:, :n], wa[:, n:])
    v = v + nt(dz[:, n:], wb[:, :n]) + nt(dxp[:, n:], wb[:, n:])
    o[:, :wide] = (v + nt(ddt[...], wdt[...])).astype(bf16)
    cols = NS // pl.num_programs(0)
    row, lane = iota((2 * NS, 128), 0), iota((2 * NS, 128), 1)
    source = lane // cols * NS + pl.program_id(0) * cols + lane % cols
    pick = ((row == source) & (lane < 2 * cols)).astype(bf16)
    o[:, wide:] = nn(dbc[...], pick).astype(bf16)


def weight_kernel(count, tiles, extra, core, *refs):
    lhs, rhs, more, (keep, give) = refs[:count], refs[count : 2 * count], refs[2 * count : -2], refs[-2:]
    v = tn(lhs[0][...], rhs[0][...])
    for k in range(1, count):
        v = v + tn(lhs[k][...], rhs[k][...])
    if extra:
        part = lhs[0].shape[0]
        w = tn(lhs[0][...], more[0][:part, :])
        for k in range(1, count):
            w = w + tn(lhs[k][...], more[0][k * part : (k + 1) * part, :])
        n, m = v.shape[1] // 2, w.shape[1] // 2
        v = jnp.concatenate([v[:, :n], w[:, :m], v[:, n:], w[:, m:]], axis=1)
    step = pl.program_id(0)

    @pl.when(step < tiles)
    def _():
        keep[...] = v

    @pl.when(step >= tiles)
    def _():
        give[...] = v


def few_kernel(lhs, rhs, o):
    o[...] = tn(rhs[...], lhs[...])


def join_kernel(core, za, zb, xa, xb, o):
    first = pl.program_id(0) * 2 // pl.num_programs(0) == core[0]
    rows, lanes = za.shape
    parts = lanes // 128

    def put(z, x):
        for k in range(parts):
            at = slice(k * 128, k * 128 + 128)
            o[pl.ds(2 * k, rows, stride=2 * parts), :] = z[:, at].astype(f32)
            o[pl.ds(2 * k + 1, rows, stride=2 * parts), :] = x[:, at].astype(f32)

    @pl.when(first)
    def _():
        put(za, xa)

    @pl.when(jnp.logical_not(first))
    def _():
        put(zb, xb)


def tile(width, first=0):
    return pl.BlockSpec((BLK, width), lambda i, *_: (first + i, 0))


def back_tile(width, last):
    return pl.BlockSpec((BLK, width), lambda i, *_: (last - i, 0))


def whole(*shape):
    zeros = (0,) * len(shape)
    return pl.BlockSpec(shape, lambda i, *_: zeros)


def sds(shape, dtype):
    return jax.ShapeDtypeStruct(shape, dtype)


def call(
    kernel, grid, in_specs, out_specs, out_shape, scratch=(), flops=0, moved=0, prefetch=0, after=(), into=()
):
    first = prefetch + len(in_specs)
    extra = len(after) + len(into)

    def body(*refs):
        kernel(*refs[:first], *refs[first + extra :])

    fn = pl.pallas_call(
        body,
        grid_spec=pltpu.PrefetchScalarGridSpec(
            num_scalar_prefetch=prefetch,
            grid=(grid,),
            in_specs=list(in_specs) + [pl.BlockSpec(memory_space=pl.ANY)] * extra,
            out_specs=out_specs,
            scratch_shapes=list(scratch),
        ),
        out_shape=out_shape,
        input_output_aliases={first + len(after) + k: k for k in range(len(into))},
        compiler_params=pltpu.CompilerParams(
            dimension_semantics=("arbitrary",), vmem_limit_bytes=VMEM_LIMIT
        ),
        cost_estimate=pl.CostEstimate(flops=flops // COST, bytes_accessed=moved // COST, transcendentals=0),
    )
    return lambda *args: fn(*args, *after, *into)


def three(v):
    high = lax.optimization_barrier(v.astype(bf16))
    rest = v - high.astype(f32)
    mid = lax.optimization_barrier(rest.astype(bf16))
    return high, mid, (rest - mid.astype(f32)).astype(bf16)


def shards(
    hidden_in, starts, cotangent, norm_gain, w_zx, w_dt, w_bc, conv_x_w, conv_x_b,
    conv_bc_w, conv_bc_b, dt_bias, a_log, d_skip, gnorm_w, w_out,
):
    order = []

    def ordered(*args, after=(), **kw):
        def run(*operands):
            outs = call(*args, after=tuple(after) + tuple(order[-1:]), **kw)(*operands)
            order.append(jax.tree.leaves(outs)[-1])
            return outs

        return run

    groups = lax.axis_size("zline")
    parts = 2 * groups
    nrows = lax.axis_size("rows")
    zpos = lax.axis_index("zline")
    mine = lax.axis_index("pair")
    me = 2 * zpos + mine
    core = lax.axis_index("rows") % 2
    dim = hidden_in.shape[1]
    local_dim = cotangent.shape[1]
    lanes = w_zx.shape[2]
    heads = w_dt.shape[1]
    inner = lanes * parts
    docl = 2 * heads
    wide = dim // groups

    def swap(v):
        return lax.ppermute(v, "pair", [(0, 1), (1, 0)])

    def cross(v, bit):
        return lax.ppermute(v, "rows", [(i, i ^ bit) for i in range(nrows)])

    def line_sum(v):
        bit = 1
        while bit < groups:
            v = v + lax.ppermute(v, "zline", [(i, i ^ bit) for i in range(groups)])
            bit *= 2
        return v

    def rows_of(v, start, size):
        return lax.dynamic_slice_in_dim(v, start, size, 0)

    def zero_after(v):
        return (v.reshape(-1)[0].astype(f32) > 1e38).astype(jnp.int32)

    def late(v, after):
        return v + zero_after(after).astype(v.dtype)

    def half_of_partner(own, after=None):
        half = own.shape[0] // 2
        at = core * half if after is None else core * half + zero_after(after)
        return swap(rows_of(own, at, half))

    def with_other_half(got, after):
        other = cross(got, 1)
        first = core + zero_after(after) == 0
        return jnp.concatenate([jnp.where(first, got, other), jnp.where(first, other, got)], axis=0)

    w_a = w_zx.reshape(dim, 2 * lanes)
    o_a = w_out
    small = jnp.stack([dt_bias, a_log, d_skip]).reshape(-1)
    prm_a = jnp.concatenate(
        [
            conv_x_w,
            conv_x_b[None],
            gnorm_w[None],
            jnp.repeat(d_skip, HD)[None],
            jnp.pad(small, (0, lanes - small.shape[0]))[None],
        ],
        axis=0,
    )
    prm_b = swap(prm_a)
    small_b = prm_b[7, : 3 * heads].reshape(3, heads)
    wdt_a = w_dt.T
    wdt_b = swap(wdt_a)
    bias_all = jnp.concatenate([dt_bias, small_b[0]])
    rate_all = -jnp.exp(jnp.concatenate([a_log, small_b[1]]))
    dtp = jnp.pad(jnp.stack([bias_all, rate_all]), ((0, 6), (0, 128 - docl)))
    taps = jnp.concatenate([conv_bc_w, conv_bc_b[None]], axis=0).transpose(1, 2, 0)
    high, mid, low = three(taps)
    pack = jnp.concatenate([w_bc.transpose(1, 2, 0), high, mid, low], axis=2)
    pack = jnp.pad(pack, ((0, 0), (0, 0), (0, 128 - 15)))

    pack = lax.all_gather(pack, ("zline", "pair"), axis=1, tiled=True)
    is0 = mine == 0
    w_half = rows_of(w_a, core * (dim // 2), dim // 2)
    w_got = swap(w_half)
    c_got = swap(rows_of(cotangent, (1 - mine) * LEN + zero_after(w_got), LEN))
    o_got = half_of_partner(w_out, w_got)
    c_mine = rows_of(cotangent, mine * LEN, LEN)
    c_mine = lax.all_gather(c_mine, "zline", axis=1, tiled=True)
    pack = pack.reshape(2 * NS, dim + 128)
    wbc = pack[:, :dim]
    taps = pack[:, dim : dim + 15].astype(f32).reshape(2 * NS, 3, 5).sum(axis=1)
    kern_bc = jnp.pad(taps.T, ((0, 3), (0, 0)))
    wdt = jnp.concatenate([wdt_a, wdt_b, jnp.zeros((128 - docl, dim), bf16)], axis=0)
    wst = jnp.concatenate([wbc, wdt], axis=0)

    st = rows_of(starts, mine * LEN, LEN).astype(f32)
    open1 = jnp.where(jnp.arange(LEN) == 0, 0.0, 1.0 - st)
    open2 = open1 * jnp.concatenate([jnp.zeros((1,), f32), open1[:-1]])
    open3 = open2 * jnp.concatenate([jnp.zeros((2,), f32), open1[:-2]])
    msk = jnp.pad(jnp.stack([st, open1, open2, open3], axis=1), ((0, 0), (0, 124)))
    which = mine.astype(jnp.int32).reshape(1)

    tl = (BLK, lanes)
    proj_out = [tile(lanes), tile(lanes), tile(lanes), tile(lanes)]
    proj_shape = [sds((LEN, lanes), bf16)] * 4
    pf = 2 * LEN * dim * 2 * lanes

    normed, r_wide, z_a, xp_a, a_a, xs_a, tail = ordered(
        first_kernel,
        NBLK,
        [
            pl.BlockSpec((BLK, dim), lambda i, which: (which[0] * NBLK + i, 0)),
            whole(1, dim),
            whole(dim, 2 * lanes),
            whole(8, lanes),
            tile(128),
            whole(8, lanes),
        ],
        [tile(dim), tile(128)] + [tile(lanes)] * 4 + [whole(8, lanes)],
        [sds((LEN, dim), bf16), sds((LEN, 128), f32)] + proj_shape + [sds((8, lanes), f32)],
        [pltpu.VMEM((BLK + 8, lanes), f32)],
        flops=pf,
        moved=40 << 20,
        prefetch=1,
    )(which, hidden_in, norm_gain.reshape(1, dim), w_a, prm_a, msk, jnp.zeros((8, lanes), f32))
    bcp, bca, bc, dtr, dt, cum, cumt = ordered(
        functools.partial(states_kernel, docl),
        NBLK,
        [tile(dim), whole(2 * NS + 128, dim), whole(8, 2 * NS), whole(8, 128), tile(128)],
        [tile(2 * NS)] * 3 + [tile(128)] * 3 + [pl.BlockSpec((128, BLK), lambda i: (0, i))],
        [sds((LEN, 2 * NS), f32)] * 2
        + [sds((LEN, 2 * NS), bf16)]
        + [sds((LEN, 128), f32)] * 3
        + [sds((128, LEN), f32)],
        [pltpu.VMEM((BLK + 8, 2 * NS), f32)],
        flops=2 * LEN * dim * 512,
        moved=18 << 20,
        after=(w_got,),
    )(normed, wst, kern_bc, dtp, msk)

    def line_scatter(v, axis=1):
        return lax.psum_scatter(v, "zline", scatter_dimension=axis, tiled=True)

    no_tail = jnp.zeros((8, lanes), f32)
    no_state = jnp.zeros((NS, lanes), f32)

    def scan(off, xs, z, prm, start=no_state, at=0, blocks=NBLK, into=()):
        return ordered(
            functools.partial(scan_kernel, docl, off),
            blocks,
            [
                tile(lanes, at), tile(lanes, at), tile(2 * NS, at), tile(128, at), tile(128, at),
                pl.BlockSpec((128, BLK), lambda i: (0, at + i)), whole(8, lanes), whole(NS, lanes),
            ],
            [
                tile(lanes, at), tile(lanes, at),
                pl.BlockSpec((1, NS, lanes), lambda i: (at + i, 0, 0)), tile(128, at), whole(NS, lanes),
            ],
            [
                sds((LEN, lanes), f32),
                sds((LEN, lanes), bf16),
                sds((NBLK, NS, lanes), f32),
                sds((LEN, 128), f32),
                sds((NS, lanes), f32),
            ],
            flops=(10 << 30) * blocks // NBLK,
            moved=(20 << 20) * blocks // NBLK,
            into=into,
        )(xs, z, bc, dt, cum, cumt, prm, start)

    def second_step(start, at, blocks, into):
        return ordered(
            second_kernel,
            blocks,
            [tile(dim, at), whole(dim, 2 * lanes), whole(8, lanes), tile(128, at), whole(8, lanes)],
            [tile(lanes, at)] * 4 + [whole(8, lanes)],
            proj_shape + [sds((8, lanes), f32)],
            [pltpu.VMEM((BLK + 8, lanes), f32)],
            flops=pf * blocks // NBLK,
            moved=(28 << 20) * blocks // NBLK,
            into=into,
        )(normed, w_b, prm_b, msk, start)

    def out_step(j):
        return ordered(
            out_kernel,
            CB,
            [tile(lanes, j * CB)] * 2 + [whole(lanes, dim)] * 2,
            tile(dim),
            sds((CT, dim), bf16),
            flops=4 * CT * lanes * dim,
            moved=10 << 20,
        )(gw_a, gw_b, o_a, o_b)

    y_a, gw_a, sin_a, pw_a, _ = scan(0, xs_a, z_a, prm_a)
    w_b = with_other_half(w_got, pw_a)
    c_got = lax.all_gather(late(c_got, pw_a), "zline", axis=1, tiled=True)
    half = NBLK // 2
    *begun, tail = second_step(no_tail, 0, half, ())
    *done, state = scan(heads, begun[3], begun[0], prm_b, no_state, 0, half)
    o_b = with_other_half(late(o_got, tail), state)
    gw_b = done[1]
    mixed_0 = line_scatter(out_step(0))
    z_b, xp_b, a_b, xs_b, _ = second_step(tail, half, half, begun)
    y_b, gw_b, sin_b, pw_b, _ = scan(heads, xs_b, z_b, prm_b, state, half, half, done)

    c_all = [None] * CHUNKS
    for j in reversed(range(CHUNKS)):
        mine_j, got_j = (v[j * CT : (j + 1) * CT] for v in (c_mine, c_got))
        c_all[j] = jnp.concatenate(
            [jnp.where(is0, mine_j, got_j), jnp.where(is0, got_j, mine_j)], axis=1
        )

    def reordered(w):
        return jnp.concatenate(
            [
                w[:, (2 * z + q) * local_dim : (2 * z + q + 1) * local_dim]
                for q in range(2)
                for z in range(groups)
            ],
            axis=1,
        )

    p_a, p_b = reordered(o_a), reordered(o_b)

    power = pw_a[:, 0] + pw_b[:, 0]
    wdt_t = wdt.T
    cols = w_bc.shape[2]

    def group_columns(v, group):
        v = v.reshape(-1, 2, NS)
        return lax.dynamic_slice_in_dim(v, group * 2 * cols, 2 * cols, 2).reshape(-1, 4 * cols)

    def near_columns(v):
        return jnp.pad(group_columns(v, zpos), ((0, 0), (0, 128 - 4 * cols)))

    bca_near, bcp_near, kern_near = near_columns(bca), near_columns(bcp), near_columns(kern_bc)
    wbc_near = lax.dynamic_slice_in_dim(wbc, zpos * wide, wide, 1).T
    wbc_near = jnp.concatenate(
        [group_columns(wbc_near, (zpos + groups - k) % groups) for k in range(groups)], axis=1
    ).T

    def dyn_step(j, after=()):
        return ordered(
            dyn_kernel,
            CB,
            [tile(dim), whole(lanes, dim), whole(lanes, dim), tile(lanes, j * CB), tile(lanes, j * CB)],
            [tile(lanes), tile(lanes), tile(128)],
            [sds((CT, lanes), bf16)] * 2 + [sds((CT, 128), f32)],
            flops=4 * CT * lanes * dim,
            moved=12 << 20,
            after=after,
        )(c_all[j], p_a, p_b, gw_a, gw_b)

    def scales_of(j, qs):
        sums = line_sum(jnp.concatenate([power[j * CT : (j + 1) * CT], qs[:, 0]]))
        s = lax.rsqrt(sums[:CT] / inner + EPSILON)
        kq = s * s * s * (sums[CT:] / inner)
        return s, jnp.pad(jnp.stack([s, kq], axis=1), ((0, 0), (0, 126)))

    def gate_step(j, sq, d_a, d_b, after=()):
        return ordered(
            gate_kernel,
            CB,
            [tile(128)] + [tile(lanes)] * 2 + [tile(lanes, j * CB)] * 4 + [whole(8, lanes)] * 2,
            [tile(2 * lanes)] * 3 + [tile(128), whole(8, 2 * lanes)],
            [sds((CT, 2 * lanes), bf16)] * 3 + [sds((CT, 128), f32), sds((8, 2 * lanes), f32)],
            flops=4000 * CT * lanes,
            moved=20 << 20,
            after=after,
        )(sq, d_a, d_b, y_a, y_b, z_a, z_b, prm_a, prm_b)

    def back_step(j, dy, ds, cda, cm, after=()):
        last = j * CB + CB - 1

        def bt(width):
            return back_tile(width, last)

        def loc(width):
            return back_tile(width, CB - 1)

        cols = pl.BlockSpec((128, BLK), lambda i: (0, last - i))
        sins = pl.BlockSpec((1, NS, lanes), lambda i: (last - i, 0, 0))
        return ordered(
            functools.partial(back_kernel, docl),
            CB,
            [
                loc(2 * lanes), bt(2 * NS), bt(128), bt(128), cols, bt(128), bt(128), whole(8, 128),
                bt(lanes), bt(lanes), bt(lanes), bt(lanes), bt(lanes), bt(lanes), bt(lanes), bt(lanes),
                sins, sins, whole(8, lanes), whole(8, lanes),
                whole(2, NS, lanes), whole(2, 8, lanes), whole(8, 128),
            ],
            [
                loc(2 * lanes), loc(128), loc(2 * NS), loc(128), whole(2, 48, lanes), whole(16, 128),
                whole(2, NS, lanes), whole(2, 8, lanes), whole(8, 128),
            ],
            [
                sds((CT, 2 * lanes), bf16), sds((CT, 128), bf16), sds((CT, 2 * NS), bf16),
                sds((CT, 128), f32), sds((2, 48, lanes), f32), sds((16, 128), f32),
                sds((2, NS, lanes), f32), sds((2, 8, lanes), f32), sds((8, 128), f32),
            ],
            [pltpu.VMEM((2, BLK + 8, lanes), f32), pltpu.VMEM((BLK + 8, 128), f32)],
            flops=(80 << 30) // CHUNKS,
            moved=(80 << 20) // CHUNKS,
            after=after,
        )(
            dy, bc, dt, cum, cumt, dtr, msk, dtp,
            y_a, y_b, xs_a, xs_b, a_a, a_b, xp_a, xp_b, sin_a, sin_b, prm_a, prm_b,
            ds, cda, cm,
        )

    def states_step(j, dbc, sda, scm):
        last = j * CB + CB - 1

        def bt(width):
            return back_tile(width, last)

        def loc(width):
            return back_tile(width, CB - 1)

        return ordered(
            states_back_kernel,
            CB,
            [
                pl.BlockSpec((BLK, 128), lambda i: (CB - 1 - i, wide // 128)),
                bt(128), bt(128), bt(128), whole(8, 128), whole(8, 128), whole(8, 128),
            ],
            [loc(128), loc(128), whole(40, 128), whole(8, 128), whole(8, 128)],
            [
                sds((CT, 128), bf16), sds((CT, 128), f32), sds((40, 128), f32),
                sds((8, 128), f32), sds((8, 128), f32),
            ],
            [pltpu.VMEM((BLK + 8, 128), f32), pltpu.VMEM((BLK + 8, 128), f32)],
            flops=CHEAP,
            moved=CHEAP,
        )(dbc, bca_near, bcp_near, msk, kern_near, sda, scm)

    def dn_step(dz, dxp, ddt, dbc, after=()):
        return ordered(
            dn_kernel,
            groups,
            [
                whole(CT, 2 * lanes), whole(CT, 2 * lanes), whole(CT, 128), whole(CT, 2 * NS),
                pl.BlockSpec((wide, 2 * lanes), lambda i: (i, 0)),
                pl.BlockSpec((wide, 2 * lanes), lambda i: (i, 0)),
                pl.BlockSpec((wide, 128), lambda i: (i, 0)),
            ],
            pl.BlockSpec((CT, wide + 128), lambda i: (i, 0)),
            sds((groups * CT, wide + 128), bf16),
            flops=8 * CT * lanes * dim,
            moved=16 << 20,
            after=after,
        )(dz, dxp, ddt, dbc, w_a, w_b, wdt_t)

    def near_step(total, dsp):
        mine_first = [dsp[:, : 4 * cols]] + [
            lax.ppermute(dsp[:, : 4 * cols], "zline", [(i, (i + k) % groups) for i in range(groups)])
            for k in range(1, groups)
        ]
        total = total[:, :wide].astype(f32) + nn(jnp.concatenate(mine_first, axis=1), wbc_near)
        keep = lax.dynamic_slice_in_dim(total, mine * local_dim, local_dim, 1)
        give = lax.dynamic_slice_in_dim(total, (1 - mine) * local_dim, local_dim, 1)
        return keep, swap(give.astype(bf16))

    core_at = core.astype(jnp.int32).reshape(1)

    def weight_grad(lhs, rhs, more=None, after=()):
        count = len(rhs)
        n, m = lhs[0].shape[1], rhs[0].shape[1]
        part = LEN // count
        more = [] if more is None else [more]
        full = m + sum(v.shape[1] for v in more)
        size = min(256, n // 4)
        tiles = n // size // 2

        def order(i, core):
            return jnp.where(i < tiles, i + core[0] * tiles, i - core[0] * tiles)

        return ordered(
            functools.partial(weight_kernel, count, tiles, len(more)),
            2 * tiles,
            [
                pl.BlockSpec(
                    (part, size),
                    lambda i, core, at=0 if v.shape[0] == part else k: (at, order(i, core)),
                )
                for k, v in enumerate(lhs)
            ]
            + [whole(part, m)] * count
            + [whole(*v.shape) for v in more],
            [
                pl.BlockSpec((size, full), lambda i, core: (jnp.minimum(i, tiles - 1), 0)),
                pl.BlockSpec((size, full), lambda i, core: (jnp.maximum(i - tiles, 0), 0)),
            ],
            [sds((n // 2, full), f32)] * 2,
            flops=CHEAP,
            moved=CHEAP,
            prefetch=1,
            after=after,
        )(core_at, *lhs, *rhs, *more)

    def bit_of(bit):
        return lax.axis_index("rows") // bit % 2

    def core_sum(keep, give):
        return keep + cross(give, 1)

    def pair_sum(v):
        n = v.shape[1] // 2
        return v[:, :n] + swap(v[:, n:].astype(bf16)).astype(f32)

    dz, dy, yn, mtg, scales = ([None] * CHUNKS for _ in range(5))
    dxp, ddt, dsp, near, far, dns = ([None] * CHUNKS for _ in range(6))
    ggs, accs, accs_dt, accs_bc = [], [], [], []
    carry = (jnp.zeros((2, NS, lanes), f32), jnp.zeros((2, 8, lanes), f32), jnp.zeros((8, 128), f32))
    state_carry = (jnp.zeros((8, 128), f32), jnp.zeros((8, 128), f32))

    top = CHUNKS - 1
    d_a, d_b, qs = dyn_step(top)
    scales[top], sq = scales_of(top, qs)

    dz[1], dy[1], yn[1], mtg[1], gg = gate_step(1, sq, d_a, d_b)
    ggs.append(gg)
    dxp[1], ddt[1], dbc_1, mtb_1, acc, acc_dt, *carry = back_step(1, dy[1], *carry)
    accs.append(acc)
    accs_dt.append(acc_dt)
    dns[1] = dn_step(dz[1], dxp[1], ddt[1], dbc_1, after=(mixed_0,))
    total_1 = line_scatter(dns[1], 0)
    d_a, d_b, qs = dyn_step(0)
    scales[0], sq = scales_of(0, qs)
    mixed_1 = line_scatter(out_step(1))
    dz[0], dy[0], yn[0], mtg[0], gg = gate_step(0, sq, d_a, d_b)
    ggs.append(gg)
    g_out = weight_grad(c_all, yn)
    g_z = weight_grad([normed] * CHUNKS, dz)
    dxp[0], ddt[0], dbc_0, mtb_0, acc, acc_dt, *carry = back_step(0, dy[0], *carry)
    accs.append(acc)
    accs_dt.append(acc_dt)
    dsp[1], mtc_1, acc_bc, *state_carry = states_step(1, total_1, *state_carry)
    accs_bc.append(acc_bc)
    out_sum, z_sum = core_sum(*g_out), core_sum(*g_z)
    g_x = weight_grad([normed] * CHUNKS, dxp, after=(out_sum, z_sum))
    x_sum = core_sum(*g_x)
    out_sum = pair_sum(out_sum)
    dns[0] = dn_step(dz[0], dxp[0], ddt[0], dbc_0, after=(out_sum,))
    total_0 = line_scatter(dns[0], 0)
    dsp[0], mtc_0, acc_bc, *state_carry = states_step(0, total_0, *state_carry)
    accs_bc.append(acc_bc)

    dsp_near = jnp.concatenate(dsp, axis=0)[:, : 4 * cols].reshape(LEN, 2, 2, cols)
    ddt_all = jnp.concatenate(ddt, axis=0)
    width = 2 * cols + heads

    def few(q):
        sel = lax.dynamic_index_in_dim(dsp_near, q, 2, keepdims=False).reshape(LEN, 2 * cols)
        dts = lax.dynamic_slice_in_dim(ddt_all, jnp.where(q == mine, 0, heads), heads, 1)
        return jnp.concatenate([sel, dts, jnp.zeros((LEN, 128 - width), bf16)], axis=1)

    fewer = jnp.concatenate([few(mine), few(1 - mine)], axis=1)
    g_few = ordered(
        few_kernel,
        8,
        [pl.BlockSpec((LEN, dim // 8), lambda i: (0, i)), whole(LEN, fewer.shape[1])],
        pl.BlockSpec((fewer.shape[1], dim // 8), lambda i: (0, i)),
        sds((fewer.shape[1], dim), f32),
        flops=CHEAP,
        moved=CHEAP,
    )(normed, fewer)
    near[1], far[1] = near_step(total_1, dsp[1])
    near[0], far[0] = near_step(total_0, dsp[0])
    local_sum = [
        mtg[j][:, 0] + m[:, 0] + n[:, 0] for j, m, n in ((0, mtb_0, mtc_0), (1, mtb_1, mtc_1))
    ]
    mean_sum = line_sum(jnp.concatenate(local_sum))
    mixer = jnp.concatenate([mixed_0, mixed_1], axis=0).astype(f32)

    def reduce_rows(v):
        bit = 2
        while bit < nrows:
            size = v.shape[0] // 2
            up = bit_of(bit)
            give = rows_of(v, (1 - up) * size, size)
            v = rows_of(v, up * size, size) + cross(give.astype(bf16), bit).astype(f32)
            bit *= 2
        v = lax.reduce_precision(v, 8, 7).astype(bf16)
        while bit > 2:
            bit //= 2
            got = cross(v, bit)
            low = bit_of(bit) == 0
            v = jnp.concatenate([jnp.where(low, v, got), jnp.where(low, got, v)], axis=0)
        return v

    def both_cores(v):
        got = cross(v, 1)
        first = core == 0
        return jnp.concatenate([jnp.where(first, v, got), jnp.where(first, got, v)], axis=0)

    def rows_sum(v):
        bit = 1
        while bit < nrows:
            v = v + cross(v, bit)
            bit *= 2
        return v

    g_x, g_z, g_out = (reduce_rows(v) for v in (pair_sum(x_sum), pair_sum(z_sum), out_sum))
    g_few = rows_sum(g_few[:width] + swap(g_few[128 : 128 + width].astype(bf16)).astype(f32))
    g_out = both_cores(g_out)
    grad_w_out = jnp.concatenate(
        [
            g_out[(q * groups + z) * local_dim : (q * groups + z + 1) * local_dim]
            for z in range(groups)
            for q in range(2)
        ],
        axis=0,
    ).T.astype(f32)
    grad_w_bc = g_few[: 2 * cols].reshape(2, cols, dim).transpose(2, 0, 1)
    grad_w_dt = g_few[2 * cols :].T
    x_far, z_far = cross(g_x, 1), cross(g_z, 1)
    steps = 8
    size = dim // steps
    at = pl.BlockSpec((size, lanes), lambda i, core: (i % (steps // 2), 0))
    grad_w_zx = ordered(
        join_kernel,
        steps,
        [at] * 4,
        pl.BlockSpec((size * 2 * lanes // 128, 128), lambda i, core: (i, 0)),
        sds((dim * 2 * lanes // 128, 128), f32),
        moved=24 << 20,
        prefetch=1,
    )(core_at, g_z, z_far, g_x, x_far)
    grad_w_zx = grad_w_zx.reshape(dim, lanes // 128, 2, 128).transpose(0, 2, 1, 3)
    grad_w_zx = grad_w_zx.reshape(dim, 2, lanes)

    acc = sum(accs).reshape(2, 6, 8, lanes).sum(axis=2)
    gg = sum(ggs).sum(axis=0).reshape(2, 1, lanes)
    acc_dt = sum(accs_dt).reshape(2, 8, 128).sum(axis=1)[:, :docl].reshape(2, 2, heads)
    acc_dt = jnp.pad(acc_dt.transpose(1, 0, 2).reshape(2, 1, -1), ((0, 0), (0, 0), (0, lanes - docl)))
    vec = jnp.concatenate([acc, gg, acc_dt], axis=1)
    acc_bc = sum(accs_bc).reshape(5, 8, 128).sum(axis=1)[:, : 4 * cols]

    vec = rows_sum(vec[0] + swap(vec[1]))
    acc_bc = rows_sum(acc_bc + swap(acc_bc)).reshape(5, 2, 2, cols)
    acc_bc = lax.dynamic_index_in_dim(acc_bc, mine, 2, keepdims=False)

    s_all = jnp.concatenate(scales)
    out_near = mixer * s_all[:, None]
    o_own = lax.dynamic_slice_in_dim(out_near, mine * local_dim, local_dim, 1)
    o_far = swap(
        lax.dynamic_slice_in_dim(out_near, (1 - mine) * local_dim, local_dim, 1).astype(bf16)
    )
    r_own = r_wide[:, 0]
    m_own = mean_sum
    r_far = swap(r_own)
    m_far = swap(m_own)
    d_own = jnp.concatenate(near, axis=0)
    d_far = jnp.concatenate(far, axis=0)
    x_near = lax.dynamic_slice_in_dim(hidden_in, me * local_dim, local_dim, 1).astype(f32)
    gain = lax.dynamic_slice_in_dim(norm_gain, me * local_dim, local_dim, 0)
    outs, grads, gain_sum = [], [], 0.0
    for q in range(2):
        sel = mine == q
        x = x_near[q * LEN : (q + 1) * LEN]
        cot = cotangent[q * LEN : (q + 1) * LEN].astype(f32)
        outs.append((x + jnp.where(sel, o_own, o_far.astype(f32))).astype(bf16))
        d = jnp.where(sel, d_own, d_far.astype(f32))
        r = jnp.where(sel, r_own, r_far)[:, None]
        m = jnp.where(sel, m_own, m_far)[:, None]
        grads.append(cot + r * (d * gain) - x * (r * r) * (m / dim))
        gain_sum = gain_sum + jnp.sum(d * x * r, axis=0)
    return (
        jnp.concatenate(outs, axis=0),
        jnp.concatenate(grads, axis=0),
        rows_sum(gain_sum),
        grad_w_zx,
        grad_w_dt,
        grad_w_bc,
        vec[:4],
        vec[4],
        acc_bc[:4],
        acc_bc[4],
        vec[7, heads : 2 * heads],
        vec[7, :heads],
        vec[5].reshape(heads, HD).sum(axis=1),
        vec[6],
        grad_w_out,
    )


STATE = ("zline", "pair")


def solution(mesh):
    placed = (
        P("rows", None),
        P("rows"),
        P("rows", STATE),
        P(),
        P(None, None, STATE),
        P(None, STATE),
        P(None, None, STATE),
        P(None, STATE),
        P(STATE),
        P(None, None, STATE),
        P(None, STATE),
        P(STATE),
        P(STATE),
        P(STATE),
        P(STATE),
        P(STATE, None),
    )
    rows, parts = mesh.devices.shape
    split = Mesh(mesh.devices.reshape(rows, parts // 2, 2), ("rows", "zline", "pair"))
    return jax.shard_map(
        shards,
        mesh=split,
        in_specs=placed,
        out_specs=(
            P("rows", STATE),
            P("rows", STATE),
            P(STATE),
            P(None, None, STATE),
            P(None, STATE),
            P(None, None, STATE),
            P(None, STATE),
            P(STATE),
            P(None, None, STATE),
            P(None, STATE),
            P(STATE),
            P(STATE),
            P(STATE),
            P(STATE),
            P(STATE, None),
        ),
        check_vma=False,
    )
```

```python
import functools

import jax
import jax.numpy as jnp
from jax import lax
from jax.experimental import pallas as pl
from jax.experimental.pallas import tpu as pltpu
from jax.sharding import Mesh
from jax.sharding import PartitionSpec as P

LEN = 2048
BLK = 256
NBLK = LEN // BLK
CHUNKS = 2
CT = LEN // CHUNKS
CB = CT // BLK
HD = 64
NS = 128
EPSILON = 1e-05
HIGHEST = lax.Precision.HIGHEST
f32 = jnp.float32
bf16 = jnp.bfloat16
COST = 1
CHEAP = 1 << 16
VMEM_LIMIT = 56 * 1024 * 1024


def nn(a, b, **kw):
    return lax.dot_general(a, b, (((1,), (0,)), ((), ())), preferred_element_type=f32, **kw)


def nt(a, b):
    return lax.dot_general(a, b, (((1,), (1,)), ((), ())), preferred_element_type=f32)


def tn(a, b):
    return lax.dot_general(a, b, (((0,), (0,)), ((), ())), preferred_element_type=f32)


def iota(shape, dim):
    return lax.broadcasted_iota(jnp.int32, shape, dim)


def sigmoid(v):
    return 1.0 / (1.0 + jnp.exp(-v))


def fold(v):
    return v.reshape(v.shape[0] // 8, 8, v.shape[1]).sum(axis=0)


def expand(cols, off, heads):
    low = iota((cols.shape[0], 128), 1) < HD
    pieces = []
    for p in range(heads // 2):
        a = cols[:, off + 2 * p : off + 2 * p + 1]
        b = cols[:, off + 2 * p + 1 : off + 2 * p + 2]
        pieces.append(jnp.where(low, a, b))
    return jnp.concatenate(pieces, axis=1)


def quad_masks(rows):
    head = iota((rows, 4 * HD), 1) // HD
    return [head == h for h in range(4)]


def stacked(v, masks):
    zero = jnp.zeros_like(v)
    return jnp.concatenate([jnp.where(m, v, zero) for m in masks], axis=0)


def segment_sums(v, off):
    n = v.shape[1]
    pick = (iota((n, 128), 1) == iota((n, 128), 0) // HD + off).astype(bf16)
    high = v.astype(bf16)
    rest = (v - high.astype(f32)).astype(bf16)
    return nn(high, pick) + nn(rest, pick)


def conv_tile(step, x1, kern, msk, buf, start=None):
    @pl.when(step == 0)
    def _():
        buf[0:8, :] = jnp.zeros((8, buf.shape[1]), f32) if start is None else start[...]

    buf[8 : 8 + BLK, :] = x1
    acc = kern[4:5, :] + kern[3:4, :] * x1
    for k in range(1, 4):
        acc = acc + kern[3 - k : 4 - k, :] * (buf[8 - k : 8 - k + BLK, :] * msk[:, k : k + 1])
    buf[0:8, :] = x1[BLK - 8 :, :]
    return acc


def project_tile(n, w, kern, msk, z, xp, a, xs, buf, start=None):
    lanes = w.shape[1] // 2
    p = nn(n, w[...])
    z[...] = p[:, :lanes].astype(bf16)
    x1 = p[:, lanes:]
    xp[...] = x1.astype(bf16)
    acc = conv_tile(pl.program_id(0), x1, kern, msk, buf, start)
    a[...] = acc.astype(bf16)
    xs[...] = (acc * sigmoid(acc)).astype(bf16)


def first_kernel(which, hid, gain, w, kern, msk, start, normed, r, z, xp, a, xs, tail, buf):
    x = hid[...].astype(f32)
    rr = lax.rsqrt(jnp.mean(x * x, axis=1, keepdims=True) + EPSILON)
    n = (x * rr * gain[...]).astype(bf16)
    normed[...] = n
    r[...] = jnp.broadcast_to(rr, (BLK, 128))
    project_tile(n, w, kern, msk, z, xp, a, xs, buf, start)
    tail[...] = buf[0:8, :]


def second_kernel(normed, w, kern, msk, start, z, xp, a, xs, tail, buf):
    project_tile(normed[...], w, kern, msk, z, xp, a, xs, buf, start)
    tail[...] = buf[0:8, :]


def states_kernel(docl, normed, ws, kern, dtp, msk, bcp, bca, bc, dtr, dt, cum, cumt, buf):
    q = nt(normed[...], ws[...])
    x1 = q[:, : 2 * NS]
    bcp[...] = x1
    acc = conv_tile(pl.program_id(0), x1, kern, msk, buf)
    bca[...] = acc
    bc[...] = (acc * sigmoid(acc)).astype(bf16)
    d = q[:, 2 * NS :]
    dtr[...] = d
    v = d + dtp[0:1, :]
    e = jnp.exp(-jnp.abs(v))
    small = e * (1.0 - e * (0.5 - e * (1.0 / 3.0 - 0.25 * e)))
    step = jnp.maximum(v, 0.0) + jnp.where(e < 0.01, small, jnp.log(1.0 + e))
    lane = iota((BLK, 128), 1)
    step = jnp.where(lane < docl, step, 0.0)
    dt[...] = step
    ext = jnp.where(lane == docl, msk[:, 0:1], step * dtp[1:2, :])
    tri = (iota((BLK, BLK), 0) >= iota((BLK, BLK), 1)).astype(f32)
    c = nn(tri, ext, precision=HIGHEST)
    cum[...] = c
    cumt[...] = c.T


def block_scalars(docl, cum):
    lane = iota((BLK, 128), 1)
    doc = cum[:, docl : docl + 1]
    doc_last = cum[BLK - 1 : BLK, docl : docl + 1]
    rates = jnp.where(lane < docl, cum, 0.0)
    last = rates[BLK - 1 : BLK, :]
    lead = jnp.exp(rates) * (doc == 0.0).astype(f32)
    trail = jnp.exp(last - rates) * (doc == doc_last).astype(f32)
    retain = jnp.exp(last) * (doc_last == 0.0).astype(f32)
    return lead, trail, retain


def scan_kernel(docl, off, xs, z, bc, dt, cum, cumt, prm, start, y, gw, sin, pw, state):
    lanes = xs.shape[1]
    heads = lanes // HD

    @pl.when(pl.program_id(0) == 0)
    def _():
        state[...] = start[...]

    s_in = state[...]
    sin[0] = s_in
    b = bc[:, :NS]
    c = bc[:, NS:]
    cumv = cum[...]
    lead, trail, retain = block_scalars(docl, cumv)
    within = (cumv[:, docl : docl + 1] == cumt[docl : docl + 1, :]) & (
        iota((BLK, BLK), 0) >= iota((BLK, BLK), 1)
    )
    bias = jnp.where(within, 0.0, -1e30)
    g = nt(c, b)
    xf = xs[...].astype(f32)
    u = xf * expand(dt[...], off, heads)
    ub = u.astype(bf16)
    masks = quad_masks(BLK)
    parts = []
    for q in range(heads // 4):
        mixes = []
        for h in range(off + 4 * q, off + 4 * q + 4):
            decay = jnp.exp((cumv[:, h : h + 1] - cumt[h : h + 1, :]) + bias)
            mixes.append((decay * g).astype(bf16))
        uq = ub[:, q * 256 : q * 256 + 256]
        parts.append(nn(jnp.concatenate(mixes, axis=1), stacked(uq, masks)))
    yv = jnp.concatenate(parts, axis=1)
    yv = yv + nn(c, s_in.astype(bf16)) * expand(lead, off, heads) + prm[6:7, :] * xf
    y[...] = yv
    ut = (u * expand(trail, off, heads)).astype(bf16)
    state[...] = s_in * expand(retain, off, heads) + tn(b, ut)
    zz = z[...].astype(f32)
    gated = yv * zz * sigmoid(zz)
    gw[...] = (gated * prm[5:6, :]).astype(bf16)
    pw[...] = jnp.broadcast_to(jnp.sum(gated * gated, axis=1, keepdims=True), (BLK, 128))


def out_kernel(ga, gb, wa, wb, o):
    o[...] = (nn(ga[...], wa[...]) + nn(gb[...], wb[...])).astype(bf16)


def dyn_kernel(c, wa, wb, ga, gb, da, db, qs):
    cv = c[...]
    a = nt(cv, wa[...])
    b = nt(cv, wb[...])
    da[...] = a.astype(bf16)
    db[...] = b.astype(bf16)
    q = jnp.sum(a * ga[...].astype(f32), axis=1, keepdims=True)
    q = q + jnp.sum(b * gb[...].astype(f32), axis=1, keepdims=True)
    qs[...] = jnp.broadcast_to(q, (BLK, 128))


def gate_kernel(sq, da, db, ya, yb, za, zb, prma, prmb, dz, dy, yn, mt, gg):
    lanes = da.shape[1]
    s = sq[:, 0:1]
    kq = sq[:, 1:2]

    @pl.when(pl.program_id(0) == 0)
    def _():
        gg[...] = jnp.zeros_like(gg)

    total = jnp.zeros((BLK, 1), f32)
    for half, (dref, yref, zref, prm) in enumerate(((da, ya, za, prma), (db, yb, zb, prmb))):
        at = slice(half * lanes, half * lanes + lanes)
        dn = dref[...].astype(f32)
        y = yref[...]
        z = zref[...].astype(f32)
        gn = prm[5:6, :]
        sg = sigmoid(z)
        act = z * sg
        g = y * act
        gs = g * s
        yn[:, at] = (gs * gn).astype(bf16)
        gg[:, at] += fold(dn * gs)
        dg = s * (dn * gn) - g * kq
        dy[:, at] = (dg * act).astype(bf16)
        low = (dg * y * (sg * (1.0 + z * (1.0 - sg)))).astype(bf16)
        dz[:, at] = low
        total = total + jnp.sum(low.astype(f32) * z, axis=1, keepdims=True)
    mt[...] = jnp.broadcast_to(total, (BLK, 128))


def conv_back(da, xp, kern, buf, mbuf):
    dx = kern[3:4, :] * da
    taps = [None, None, None, fold(xp * da)]
    for k in range(1, 4):
        sh = buf[k : k + BLK, :] * mbuf[k : k + BLK, k : k + 1]
        dx = dx + kern[3 - k : 4 - k, :] * sh
        taps[3 - k] = fold(xp * sh)
    return dx, taps


def back_kernel(
    docl,
    dy, bc, dt, cum, cumt, dtr, msk, dtp,
    ya, yb, xsa, xsb, aa, ab, xpa, xpb, sia, sib, prma, prmb,
    ds_in, cda_in, cm_in,
    dxp, ddt, dbc, mt, acc, accs, ds, cda, cm,
    buf, mbuf,
):
    lanes = xsa.shape[1]
    heads = lanes // HD
    step = pl.program_id(0)

    @pl.when(step == 0)
    def _():
        ds[...] = ds_in[...]
        buf[:, 0:8, :] = cda_in[...]
        mbuf[0:8, :] = cm_in[...]
        acc[...] = jnp.zeros_like(acc)
        accs[...] = jnp.zeros_like(accs)

    mbuf[BLK : BLK + 8, :] = mbuf[0:8, :]
    mbuf[0:BLK, :] = msk[...]
    b = bc[:, :NS]
    c = bc[:, NS:]
    cumv = cum[...]
    lead, trail, retain = block_scalars(docl, cumv)
    within = (cumv[:, docl : docl + 1] == cumt[docl : docl + 1, :]) & (
        iota((BLK, BLK), 0) <= iota((BLK, BLK), 1)
    )
    bias = jnp.where(within, 0.0, -1e30)
    gt = nt(b, c)
    masks = quad_masks(BLK)
    dgt = jnp.zeros((BLK, BLK), f32)
    d_c = jnp.zeros((BLK, NS), f32)
    d_b = jnp.zeros((BLK, NS), f32)
    r1 = jnp.zeros((BLK, 128), f32)
    r2 = jnp.zeros((BLK, 128), f32)
    r3 = jnp.zeros((BLK, 128), f32)
    held = jnp.zeros((8, 128), f32)
    total = jnp.zeros((BLK, 1), f32)
    refs = ((ya, xsa, aa, xpa, sia, prma), (yb, xsb, ab, xpb, sib, prmb))
    for half, (yr, xsr, ar, xpr, sir, prm) in enumerate(refs):
        off = half * heads
        at = slice(half * lanes, half * lanes + lanes)
        dyb = dy[:, at]
        dyf = dyb.astype(f32)
        skip = prm[6:7, :]
        xf = xsr[...].astype(f32)
        dte = expand(dt[...], off, heads)
        u = xf * dte
        ub = u.astype(bf16)
        ubf = ub.astype(f32)
        s_in = sir[0]
        d_state = ds[half]
        dsb = d_state.astype(bf16)
        te = expand(trail, off, heads)
        tb = te * nn(b, dsb)
        parts = []
        for q in range(heads // 4):
            uq = ub[:, q * 256 : q * 256 + 256]
            dq = dyb[:, q * 256 : q * 256 + 256]
            dmt = nt(stacked(uq, masks), dq)
            mixes = []
            for i in range(4):
                h = off + 4 * q + i
                decay = jnp.exp((cumt[h : h + 1, :] - cumv[:, h : h + 1]) + bias)
                mixes.append((decay * gt).astype(bf16))
                dgt = dgt + dmt[i * BLK : i * BLK + BLK, :] * decay
            parts.append(nn(jnp.concatenate(mixes, axis=1), stacked(dq, masks)))
        du = jnp.concatenate(parts, axis=1) + tb
        ldy = (expand(lead, off, heads) * dyf).astype(bf16)
        d_c = d_c + nt(ldy, s_in.astype(bf16))
        d_b = d_b + nt((te * u).astype(bf16), dsb)
        ds[half] = d_state * expand(retain, off, heads) + tn(c, ldy)
        r1 = r1 + segment_sums(dyf * (yr[...] - skip * xf) - ubf * du, off)
        r2 = r2 + segment_sums(ubf * tb, off)
        r3 = r3 + segment_sums(xf * du, off)
        held = held + segment_sums(fold(d_state * s_in), off)
        a = ar[...].astype(f32)
        sa = sigmoid(a)
        da = (dte * du + skip * dyf) * (sa * (1.0 + a * (1.0 - sa)))
        buf[half, BLK : BLK + 8, :] = buf[half, 0:8, :]
        buf[half, 0:BLK, :] = da
        xp = xpr[...].astype(f32)
        dx, taps = conv_back(da, xp, prm, buf.at[half], mbuf)
        low = dx.astype(bf16)
        dxp[:, at] = low
        total = total + jnp.sum(low.astype(f32) * xp, axis=1, keepdims=True)
        for k in range(4):
            acc[half, 8 * k : 8 * k + 8, :] += taps[k]
        acc[half, 32:40, :] += fold(da)
        acc[half, 40:48, :] += fold(dyf * xf)
    dgb = dgt.astype(bf16)
    dbc[:, :NS] = (d_b + nn(dgb, c)).astype(bf16)
    dbc[:, NS:] = (d_c + tn(dgb, b)).astype(bf16)
    at_last = jnp.sum(r2, axis=0, keepdims=True) + retain * jnp.sum(held, axis=0, keepdims=True)
    dcum = r1 + jnp.where(iota((BLK, 128), 0) == BLK - 1, at_last, 0.0)
    later = (iota((BLK, BLK), 1) >= iota((BLK, BLK), 0)).astype(f32)
    drate = nn(later, dcum, precision=HIGHEST)
    rate = dtp[1:2, :]
    lane = iota((BLK, 128), 1)
    draw = jnp.where(lane < docl, (r3 + rate * drate) * sigmoid(dtr[...] + dtp[0:1, :]), 0.0)
    low = draw.astype(bf16)
    ddt[...] = low
    accs[0:8, :] += fold(drate * dt[...]) * rate
    accs[8:16, :] += fold(draw)
    total = total + jnp.sum(low.astype(f32) * dtr[...], axis=1, keepdims=True)
    mt[...] = jnp.broadcast_to(total, (BLK, 128))
    cda[...] = buf[:, 0:8, :]
    cm[...] = mbuf[0:8, :]


def states_back_kernel(dbc, bca, bcp, msk, kern, cda_in, cm_in, dsp, mt, acc, cda, cm, buf, mbuf):
    @pl.when(pl.program_id(0) == 0)
    def _():
        buf[0:8, :] = cda_in[...]
        mbuf[0:8, :] = cm_in[...]
        acc[...] = jnp.zeros_like(acc)

    mbuf[BLK : BLK + 8, :] = mbuf[0:8, :]
    mbuf[0:BLK, :] = msk[...]
    a = bca[...]
    sa = sigmoid(a)
    da = dbc[...].astype(f32) * (sa * (1.0 + a * (1.0 - sa)))
    buf[BLK : BLK + 8, :] = buf[0:8, :]
    buf[0:BLK, :] = da
    xp = bcp[...]
    dx, taps = conv_back(da, xp, kern, buf, mbuf)
    low = dx.astype(bf16)
    dsp[...] = low
    mt[...] = jnp.broadcast_to(jnp.sum(low.astype(f32) * xp, axis=1, keepdims=True), (BLK, 128))
    for k in range(4):
        acc[8 * k : 8 * k + 8, :] += taps[k]
    acc[32:40, :] += fold(da)
    cda[...] = buf[0:8, :]
    cm[...] = mbuf[0:8, :]


def dn_kernel(dz, dxp, ddt, dbc, wa, wb, wdt, o):
    n = wa.shape[1] // 2
    wide = wa.shape[0]
    v = nt(dz[:, :n], wa[:, :n]) + nt(dxp[:, :n], wa[:, n:])
    v = v + nt(dz[:, n:], wb[:, :n]) + nt(dxp[:, n:], wb[:, n:])
    o[:, :wide] = (v + nt(ddt[...], wdt[...])).astype(bf16)
    cols = NS // pl.num_programs(0)
    row, lane = iota((2 * NS, 128), 0), iota((2 * NS, 128), 1)
    source = lane // cols * NS + pl.program_id(0) * cols + lane % cols
    pick = ((row == source) & (lane < 2 * cols)).astype(bf16)
    o[:, wide:] = nn(dbc[...], pick).astype(bf16)


def weight_kernel(count, tiles, extra, core, *refs):
    lhs, rhs, more, (keep, give) = refs[:count], refs[count : 2 * count], refs[2 * count : -2], refs[-2:]
    v = tn(lhs[0][...], rhs[0][...])
    for k in range(1, count):
        v = v + tn(lhs[k][...], rhs[k][...])
    if extra:
        part = lhs[0].shape[0]
        w = tn(lhs[0][...], more[0][:part, :])
        for k in range(1, count):
            w = w + tn(lhs[k][...], more[0][k * part : (k + 1) * part, :])
        n, m = v.shape[1] // 2, w.shape[1] // 2
        v = jnp.concatenate([v[:, :n], w[:, :m], v[:, n:], w[:, m:]], axis=1)
    step = pl.program_id(0)

    @pl.when(step < tiles)
    def _():
        keep[...] = v

    @pl.when(step >= tiles)
    def _():
        give[...] = v


def few_kernel(cols, heads, mine, lhs, dsp_0, dsp_1, ddt_0, ddt_1, o, few):
    @pl.when(pl.program_id(0) == 0)
    def _():
        row, lane = iota((128, 256), 0), iota((128, 256), 1)
        side, c = lane // 128, lane % 128
        pair = jnp.where(side == 0, mine[0], 1 - mine[0])
        state = (row == c // cols * 2 * cols + pair * cols + c % cols) & (c < 2 * cols)
        step = (row == side * heads + c - 2 * cols) & (c >= 2 * cols) & (c < 2 * cols + heads)
        for k, (dsp, ddt) in enumerate(((dsp_0, ddt_0), (dsp_1, ddt_1))):
            v = nn(dsp[...], state.astype(bf16)) + nn(ddt[...], step.astype(bf16))
            few[k * CT : k * CT + CT, :] = v.astype(bf16)

    o[...] = tn(few[...], lhs[...])


def join_kernel(core, za, zb, xa, xb, o):
    first = pl.program_id(0) * 2 // pl.num_programs(0) == core[0]
    rows, lanes = za.shape
    parts = lanes // 128

    def put(z, x):
        for k in range(parts):
            at = slice(k * 128, k * 128 + 128)
            o[pl.ds(2 * k, rows, stride=2 * parts), :] = z[:, at].astype(f32)
            o[pl.ds(2 * k + 1, rows, stride=2 * parts), :] = x[:, at].astype(f32)

    @pl.when(first)
    def _():
        put(za, xa)

    @pl.when(jnp.logical_not(first))
    def _():
        put(zb, xb)


def tile(width, first=0):
    return pl.BlockSpec((BLK, width), lambda i, *_: (first + i, 0))


def back_tile(width, last):
    return pl.BlockSpec((BLK, width), lambda i, *_: (last - i, 0))


def whole(*shape):
    zeros = (0,) * len(shape)
    return pl.BlockSpec(shape, lambda i, *_: zeros)


def sds(shape, dtype):
    return jax.ShapeDtypeStruct(shape, dtype)


def call(
    kernel, grid, in_specs, out_specs, out_shape, scratch=(), flops=0, moved=0, prefetch=0, after=(), into=()
):
    first = prefetch + len(in_specs)
    extra = len(after) + len(into)

    def body(*refs):
        kernel(*refs[:first], *refs[first + extra :])

    fn = pl.pallas_call(
        body,
        grid_spec=pltpu.PrefetchScalarGridSpec(
            num_scalar_prefetch=prefetch,
            grid=(grid,),
            in_specs=list(in_specs) + [pl.BlockSpec(memory_space=pl.ANY)] * extra,
            out_specs=out_specs,
            scratch_shapes=list(scratch),
        ),
        out_shape=out_shape,
        input_output_aliases={first + len(after) + k: k for k in range(len(into))},
        compiler_params=pltpu.CompilerParams(
            dimension_semantics=("arbitrary",), vmem_limit_bytes=VMEM_LIMIT
        ),
        cost_estimate=pl.CostEstimate(flops=flops // COST, bytes_accessed=moved // COST, transcendentals=0),
    )
    return lambda *args: fn(*args, *after, *into)


def three(v):
    high = lax.optimization_barrier(v.astype(bf16))
    rest = v - high.astype(f32)
    mid = lax.optimization_barrier(rest.astype(bf16))
    return high, mid, (rest - mid.astype(f32)).astype(bf16)


def shards(
    hidden_in, starts, cotangent, norm_gain, w_zx, w_dt, w_bc, conv_x_w, conv_x_b,
    conv_bc_w, conv_bc_b, dt_bias, a_log, d_skip, gnorm_w, w_out,
):
    order = []

    def ordered(*args, after=(), **kw):
        def run(*operands):
            outs = call(*args, after=tuple(after) + tuple(order[-1:]), **kw)(*operands)
            order.append(jax.tree.leaves(outs)[-1])
            return outs

        return run

    groups = lax.axis_size("zline")
    parts = 2 * groups
    nrows = lax.axis_size("rows")
    zpos = lax.axis_index("zline")
    mine = lax.axis_index("pair")
    me = 2 * zpos + mine
    core = lax.axis_index("rows") % 2
    dim = hidden_in.shape[1]
    local_dim = cotangent.shape[1]
    lanes = w_zx.shape[2]
    heads = w_dt.shape[1]
    inner = lanes * parts
    docl = 2 * heads
    wide = dim // groups

    def swap(v):
        return lax.ppermute(v, "pair", [(0, 1), (1, 0)])

    def cross(v, bit):
        return lax.ppermute(v, "rows", [(i, i ^ bit) for i in range(nrows)])

    def line_sum(v):
        bit = 1
        while bit < groups:
            v = v + lax.ppermute(v, "zline", [(i, i ^ bit) for i in range(groups)])
            bit *= 2
        return v

    def rows_of(v, start, size):
        return lax.dynamic_slice_in_dim(v, start, size, 0)

    def zero_after(v):
        return (v.reshape(-1)[0].astype(f32) > 1e38).astype(jnp.int32)

    def late(v, after):
        return v + zero_after(after).astype(v.dtype)

    def half_of_partner(own, after=None):
        half = own.shape[0] // 2
        at = core * half if after is None else core * half + zero_after(after)
        return swap(rows_of(own, at, half))

    def with_other_half(got, after):
        other = cross(got, 1)
        first = core + zero_after(after) == 0
        return jnp.concatenate([jnp.where(first, got, other), jnp.where(first, other, got)], axis=0)

    w_a = w_zx.reshape(dim, 2 * lanes)
    o_a = w_out
    small = jnp.stack([dt_bias, a_log, d_skip]).reshape(-1)
    prm_a = jnp.concatenate(
        [
            conv_x_w,
            conv_x_b[None],
            gnorm_w[None],
            jnp.repeat(d_skip, HD)[None],
            jnp.pad(small, (0, lanes - small.shape[0]))[None],
        ],
        axis=0,
    )
    prm_b = swap(prm_a)
    small_b = prm_b[7, : 3 * heads].reshape(3, heads)
    wdt_a = w_dt.T
    wdt_b = swap(wdt_a)
    bias_all = jnp.concatenate([dt_bias, small_b[0]])
    rate_all = -jnp.exp(jnp.concatenate([a_log, small_b[1]]))
    dtp = jnp.pad(jnp.stack([bias_all, rate_all]), ((0, 6), (0, 128 - docl)))
    taps = jnp.concatenate([conv_bc_w, conv_bc_b[None]], axis=0).transpose(1, 2, 0)
    high, mid, low = three(taps)
    pack = jnp.concatenate([w_bc.transpose(1, 2, 0), high, mid, low], axis=2)
    pack = jnp.pad(pack, ((0, 0), (0, 0), (0, 128 - 15)))

    pack = lax.all_gather(pack, ("zline", "pair"), axis=1, tiled=True)
    is0 = mine == 0
    c_got = swap(rows_of(cotangent, (1 - mine) * LEN, LEN))
    w_got = half_of_partner(w_a)
    o_got = half_of_partner(w_out)
    c_mine = rows_of(cotangent, mine * LEN, LEN)
    c_mine = lax.all_gather(c_mine, "zline", axis=1, tiled=True)
    pack = pack.reshape(2 * NS, dim + 128)
    wbc = pack[:, :dim]
    taps = pack[:, dim : dim + 15].astype(f32).reshape(2 * NS, 3, 5).sum(axis=1)
    kern_bc = jnp.pad(taps.T, ((0, 3), (0, 0)))
    wdt = jnp.concatenate([wdt_a, wdt_b, jnp.zeros((128 - docl, dim), bf16)], axis=0)
    wst = jnp.concatenate([wbc, wdt], axis=0)

    st = rows_of(starts, mine * LEN, LEN).astype(f32)
    open1 = jnp.where(jnp.arange(LEN) == 0, 0.0, 1.0 - st)
    open2 = open1 * jnp.concatenate([jnp.zeros((1,), f32), open1[:-1]])
    open3 = open2 * jnp.concatenate([jnp.zeros((2,), f32), open1[:-2]])
    msk = jnp.pad(jnp.stack([st, open1, open2, open3], axis=1), ((0, 0), (0, 124)))
    which = mine.astype(jnp.int32).reshape(1)

    tl = (BLK, lanes)
    proj_out = [tile(lanes), tile(lanes), tile(lanes), tile(lanes)]
    proj_shape = [sds((LEN, lanes), bf16)] * 4
    pf = 2 * LEN * dim * 2 * lanes

    normed, r_wide, z_a, xp_a, a_a, xs_a, tail = ordered(
        first_kernel,
        NBLK,
        [
            pl.BlockSpec((BLK, dim), lambda i, which: (which[0] * NBLK + i, 0)),
            whole(1, dim),
            whole(dim, 2 * lanes),
            whole(8, lanes),
            tile(128),
            whole(8, lanes),
        ],
        [tile(dim), tile(128)] + [tile(lanes)] * 4 + [whole(8, lanes)],
        [sds((LEN, dim), bf16), sds((LEN, 128), f32)] + proj_shape + [sds((8, lanes), f32)],
        [pltpu.VMEM((BLK + 8, lanes), f32)],
        flops=pf,
        moved=40 << 20,
        prefetch=1,
        after=(prm_b, wdt_b),
    )(which, hidden_in, norm_gain.reshape(1, dim), w_a, prm_a, msk, jnp.zeros((8, lanes), f32))
    bcp, bca, bc, dtr, dt, cum, cumt = ordered(
        functools.partial(states_kernel, docl),
        NBLK,
        [tile(dim), whole(2 * NS + 128, dim), whole(8, 2 * NS), whole(8, 128), tile(128)],
        [tile(2 * NS)] * 3 + [tile(128)] * 3 + [pl.BlockSpec((128, BLK), lambda i: (0, i))],
        [sds((LEN, 2 * NS), f32)] * 2
        + [sds((LEN, 2 * NS), bf16)]
        + [sds((LEN, 128), f32)] * 3
        + [sds((128, LEN), f32)],
        [pltpu.VMEM((BLK + 8, 2 * NS), f32)],
        flops=2 * LEN * dim * 512,
        moved=18 << 20,
    )(normed, wst, kern_bc, dtp, msk)

    def line_scatter(v, axis=1):
        return lax.psum_scatter(v, "zline", scatter_dimension=axis, tiled=True)

    no_tail = jnp.zeros((8, lanes), f32)
    no_state = jnp.zeros((NS, lanes), f32)

    def scan(off, xs, z, prm, start=no_state, at=0, blocks=NBLK, into=(), after=()):
        return ordered(
            functools.partial(scan_kernel, docl, off),
            blocks,
            [
                tile(lanes, at), tile(lanes, at), tile(2 * NS, at), tile(128, at), tile(128, at),
                pl.BlockSpec((128, BLK), lambda i: (0, at + i)), whole(8, lanes), whole(NS, lanes),
            ],
            [
                tile(lanes, at), tile(lanes, at),
                pl.BlockSpec((1, NS, lanes), lambda i: (at + i, 0, 0)), tile(128, at), whole(NS, lanes),
            ],
            [
                sds((LEN, lanes), f32),
                sds((LEN, lanes), bf16),
                sds((NBLK, NS, lanes), f32),
                sds((LEN, 128), f32),
                sds((NS, lanes), f32),
            ],
            flops=(10 << 30) * blocks // NBLK,
            moved=(20 << 20) * blocks // NBLK,
            into=into,
            after=after,
        )(xs, z, bc, dt, cum, cumt, prm, start)

    def second_step(start, at, blocks, into):
        return ordered(
            second_kernel,
            blocks,
            [tile(dim, at), whole(dim, 2 * lanes), whole(8, lanes), tile(128, at), whole(8, lanes)],
            [tile(lanes, at)] * 4 + [whole(8, lanes)],
            proj_shape + [sds((8, lanes), f32)],
            [pltpu.VMEM((BLK + 8, lanes), f32)],
            flops=pf * blocks // NBLK,
            moved=(28 << 20) * blocks // NBLK,
            into=into,
        )(normed, w_b, prm_b, msk, start)

    def out_step(j):
        return ordered(
            out_kernel,
            CB,
            [tile(lanes, j * CB)] * 2 + [whole(lanes, dim)] * 2,
            tile(dim),
            sds((CT, dim), bf16),
            flops=4 * CT * lanes * dim,
            moved=10 << 20,
        )(gw_a, gw_b, o_a, o_b)

    y_a, gw_a, sin_a, pw_a, _ = scan(0, xs_a, z_a, prm_a, after=(w_got,))
    w_b = with_other_half(w_got, pw_a)
    c_got = lax.all_gather(late(c_got, pw_a), "zline", axis=1, tiled=True)
    half = NBLK // 2
    *begun, tail = second_step(no_tail, 0, half, ())
    *done, state = scan(heads, begun[3], begun[0], prm_b, no_state, 0, half)
    o_b = with_other_half(late(o_got, tail), state)
    gw_b = done[1]
    mixed_0 = line_scatter(out_step(0))
    z_b, xp_b, a_b, xs_b, _ = second_step(tail, half, half, begun)
    y_b, gw_b, sin_b, pw_b, _ = scan(heads, xs_b, z_b, prm_b, state, half, half, done)

    c_all = [None] * CHUNKS
    for j in reversed(range(CHUNKS)):
        mine_j, got_j = (v[j * CT : (j + 1) * CT] for v in (c_mine, c_got))
        c_all[j] = jnp.concatenate(
            [jnp.where(is0, mine_j, got_j), jnp.where(is0, got_j, mine_j)], axis=1
        )

    def reordered(w):
        return jnp.concatenate(
            [
                w[:, (2 * z + q) * local_dim : (2 * z + q + 1) * local_dim]
                for q in range(2)
                for z in range(groups)
            ],
            axis=1,
        )

    p_a, p_b = reordered(o_a), reordered(o_b)

    power = pw_a[:, 0] + pw_b[:, 0]
    wdt_t = wdt.T
    cols = w_bc.shape[2]

    def group_columns(v, group):
        v = v.reshape(-1, 2, NS)
        return lax.dynamic_slice_in_dim(v, group * 2 * cols, 2 * cols, 2).reshape(-1, 4 * cols)

    def near_columns(v):
        return jnp.pad(group_columns(v, zpos), ((0, 0), (0, 128 - 4 * cols)))

    bca_near, bcp_near, kern_near = near_columns(bca), near_columns(bcp), near_columns(kern_bc)
    wbc_near = lax.dynamic_slice_in_dim(wbc, zpos * wide, wide, 1).T
    wbc_near = jnp.concatenate(
        [group_columns(wbc_near, (zpos + groups - k) % groups) for k in range(groups)], axis=1
    ).T

    def dyn_step(j, after=()):
        return ordered(
            dyn_kernel,
            CB,
            [tile(dim), whole(lanes, dim), whole(lanes, dim), tile(lanes, j * CB), tile(lanes, j * CB)],
            [tile(lanes), tile(lanes), tile(128)],
            [sds((CT, lanes), bf16)] * 2 + [sds((CT, 128), f32)],
            flops=4 * CT * lanes * dim,
            moved=12 << 20,
            after=after,
        )(c_all[j], p_a, p_b, gw_a, gw_b)

    def scales_of(j, qs):
        sums = line_sum(jnp.concatenate([power[j * CT : (j + 1) * CT], qs[:, 0]]))
        s = lax.rsqrt(sums[:CT] / inner + EPSILON)
        kq = s * s * s * (sums[CT:] / inner)
        return s, jnp.pad(jnp.stack([s, kq], axis=1), ((0, 0), (0, 126)))

    def gate_step(j, sq, d_a, d_b, after=()):
        return ordered(
            gate_kernel,
            CB,
            [tile(128)] + [tile(lanes)] * 2 + [tile(lanes, j * CB)] * 4 + [whole(8, lanes)] * 2,
            [tile(2 * lanes)] * 3 + [tile(128), whole(8, 2 * lanes)],
            [sds((CT, 2 * lanes), bf16)] * 3 + [sds((CT, 128), f32), sds((8, 2 * lanes), f32)],
            flops=4000 * CT * lanes,
            moved=20 << 20,
            after=after,
        )(sq, d_a, d_b, y_a, y_b, z_a, z_b, prm_a, prm_b)

    def back_step(j, dy, ds, cda, cm, after=()):
        last = j * CB + CB - 1

        def bt(width):
            return back_tile(width, last)

        def loc(width):
            return back_tile(width, CB - 1)

        cols = pl.BlockSpec((128, BLK), lambda i: (0, last - i))
        sins = pl.BlockSpec((1, NS, lanes), lambda i: (last - i, 0, 0))
        return ordered(
            functools.partial(back_kernel, docl),
            CB,
            [
                loc(2 * lanes), bt(2 * NS), bt(128), bt(128), cols, bt(128), bt(128), whole(8, 128),
                bt(lanes), bt(lanes), bt(lanes), bt(lanes), bt(lanes), bt(lanes), bt(lanes), bt(lanes),
                sins, sins, whole(8, lanes), whole(8, lanes),
                whole(2, NS, lanes), whole(2, 8, lanes), whole(8, 128),
            ],
            [
                loc(2 * lanes), loc(128), loc(2 * NS), loc(128), whole(2, 48, lanes), whole(16, 128),
                whole(2, NS, lanes), whole(2, 8, lanes), whole(8, 128),
            ],
            [
                sds((CT, 2 * lanes), bf16), sds((CT, 128), bf16), sds((CT, 2 * NS), bf16),
                sds((CT, 128), f32), sds((2, 48, lanes), f32), sds((16, 128), f32),
                sds((2, NS, lanes), f32), sds((2, 8, lanes), f32), sds((8, 128), f32),
            ],
            [pltpu.VMEM((2, BLK + 8, lanes), f32), pltpu.VMEM((BLK + 8, 128), f32)],
            flops=(80 << 30) // CHUNKS,
            moved=(80 << 20) // CHUNKS,
            after=after,
        )(
            dy, bc, dt, cum, cumt, dtr, msk, dtp,
            y_a, y_b, xs_a, xs_b, a_a, a_b, xp_a, xp_b, sin_a, sin_b, prm_a, prm_b,
            ds, cda, cm,
        )

    def states_step(j, dbc, sda, scm, after=()):
        last = j * CB + CB - 1

        def bt(width):
            return back_tile(width, last)

        def loc(width):
            return back_tile(width, CB - 1)

        return ordered(
            states_back_kernel,
            CB,
            [
                pl.BlockSpec((BLK, 128), lambda i: (CB - 1 - i, wide // 128)),
                bt(128), bt(128), bt(128), whole(8, 128), whole(8, 128), whole(8, 128),
            ],
            [loc(128), loc(128), whole(40, 128), whole(8, 128), whole(8, 128)],
            [
                sds((CT, 128), bf16), sds((CT, 128), f32), sds((40, 128), f32),
                sds((8, 128), f32), sds((8, 128), f32),
            ],
            [pltpu.VMEM((BLK + 8, 128), f32), pltpu.VMEM((BLK + 8, 128), f32)],
            flops=CHEAP,
            moved=CHEAP,
            after=after,
        )(dbc, bca_near, bcp_near, msk, kern_near, sda, scm)

    def dn_step(dz, dxp, ddt, dbc, after=()):
        return ordered(
            dn_kernel,
            groups,
            [
                whole(CT, 2 * lanes), whole(CT, 2 * lanes), whole(CT, 128), whole(CT, 2 * NS),
                pl.BlockSpec((wide, 2 * lanes), lambda i: (i, 0)),
                pl.BlockSpec((wide, 2 * lanes), lambda i: (i, 0)),
                pl.BlockSpec((wide, 128), lambda i: (i, 0)),
            ],
            pl.BlockSpec((CT, wide + 128), lambda i: (i, 0)),
            sds((groups * CT, wide + 128), bf16),
            flops=8 * CT * lanes * dim,
            moved=16 << 20,
            after=after,
        )(dz, dxp, ddt, dbc, w_a, w_b, wdt_t)

    def near_step(total, dsp, after):
        mine_first = [dsp[:, : 4 * cols]] + [
            lax.ppermute(dsp[:, : 4 * cols], "zline", [(i, (i + k) % groups) for i in range(groups)])
            for k in range(1, groups)
        ]
        total = late(total[:, :wide].astype(f32), after) + nn(jnp.concatenate(mine_first, axis=1), wbc_near)
        keep = lax.dynamic_slice_in_dim(total, mine * local_dim, local_dim, 1)
        give = lax.dynamic_slice_in_dim(total, (1 - mine) * local_dim, local_dim, 1)
        return keep, swap(give.astype(bf16))

    core_at = core.astype(jnp.int32).reshape(1)

    def weight_grad(lhs, rhs, more=None, after=()):
        count = len(rhs)
        n, m = lhs[0].shape[1], rhs[0].shape[1]
        part = LEN // count
        more = [] if more is None else [more]
        full = m + sum(v.shape[1] for v in more)
        size = min(256, n // 4)
        tiles = n // size // 2

        def order(i, core):
            return jnp.where(i < tiles, i + core[0] * tiles, i - core[0] * tiles)

        return ordered(
            functools.partial(weight_kernel, count, tiles, len(more)),
            2 * tiles,
            [
                pl.BlockSpec(
                    (part, size),
                    lambda i, core, at=0 if v.shape[0] == part else k: (at, order(i, core)),
                )
                for k, v in enumerate(lhs)
            ]
            + [whole(part, m)] * count
            + [whole(*v.shape) for v in more],
            [
                pl.BlockSpec((size, full), lambda i, core: (jnp.minimum(i, tiles - 1), 0)),
                pl.BlockSpec((size, full), lambda i, core: (jnp.maximum(i - tiles, 0), 0)),
            ],
            [sds((n // 2, full), f32)] * 2,
            flops=CHEAP,
            moved=CHEAP,
            prefetch=1,
            after=after,
        )(core_at, *lhs, *rhs, *more)

    def bit_of(bit):
        return lax.axis_index("rows") // bit % 2

    def core_sum(keep, give):
        return keep + cross(give, 1)

    def pair_sum(v, after):
        n = v.shape[1] // 2
        return late(v[:, :n], after) + swap(v[:, n:].astype(bf16)).astype(f32)

    def chip_sum(v):
        bit = 2
        while bit < nrows:
            size = v.shape[0] // 2
            up = bit_of(bit)
            give = rows_of(v, (1 - up) * size, size)
            v = rows_of(v, up * size, size) + cross(give.astype(bf16), bit).astype(f32)
            bit *= 2
        return lax.reduce_precision(v, 8, 7).astype(bf16)

    def chip_parts(v):
        bit = nrows
        while bit > 2:
            bit //= 2
            got = cross(v, bit)
            low = bit_of(bit) == 0
            v = jnp.concatenate([jnp.where(low, v, got), jnp.where(low, got, v)], axis=0)
        return v

    dz, dy, yn, mtg, scales = ([None] * CHUNKS for _ in range(5))
    dxp, ddt, dsp, near, far, dns = ([None] * CHUNKS for _ in range(6))
    ggs, accs, accs_dt, accs_bc = [], [], [], []
    carry = (jnp.zeros((2, NS, lanes), f32), jnp.zeros((2, 8, lanes), f32), jnp.zeros((8, 128), f32))
    state_carry = (jnp.zeros((8, 128), f32), jnp.zeros((8, 128), f32))

    top = CHUNKS - 1
    d_a, d_b, qs = dyn_step(top)
    scales[top], sq = scales_of(top, qs)

    dz[1], dy[1], yn[1], mtg[1], gg = gate_step(1, sq, d_a, d_b)
    ggs.append(gg)
    dxp[1], ddt[1], dbc_1, mtb_1, acc, acc_dt, *carry = back_step(1, dy[1], *carry)
    accs.append(acc)
    accs_dt.append(acc_dt)
    dns[1] = dn_step(dz[1], dxp[1], ddt[1], dbc_1, after=(mixed_0,))
    total_1 = line_scatter(dns[1], 0)
    d_a, d_b, qs = dyn_step(0)
    scales[0], sq = scales_of(0, qs)
    mixed_1 = line_scatter(out_step(1))
    dz[0], dy[0], yn[0], mtg[0], gg = gate_step(0, sq, d_a, d_b)
    ggs.append(gg)
    g_out = weight_grad(c_all, yn)
    g_z = weight_grad([normed] * CHUNKS, dz)
    dsp[1], mtc_1, acc_bc, *state_carry = states_step(1, total_1, *state_carry)
    accs_bc.append(acc_bc)
    dxp[0], ddt[0], dbc_0, mtb_0, acc, acc_dt, *carry = back_step(0, dy[0], *carry)
    accs.append(acc)
    accs_dt.append(acc_dt)
    near[1], far[1] = near_step(total_1, dsp[1], dbc_0)
    out_sum, z_sum = core_sum(*g_out), core_sum(*g_z)
    g_x = weight_grad([normed] * CHUNKS, dxp, after=(out_sum, z_sum))
    x_sum = core_sum(*g_x)
    out_sum, z_sum = pair_sum(out_sum, dbc_0), pair_sum(z_sum, dbc_0)
    dns[0] = dn_step(dz[0], dxp[0], ddt[0], dbc_0, after=(out_sum, z_sum, near[1]))
    total_0 = line_scatter(dns[0], 0)
    x_part = chip_sum(pair_sum(x_sum, total_0))
    dsp[0], mtc_0, acc_bc, *state_carry = states_step(0, total_0, *state_carry)
    g_x = chip_parts(x_part)
    accs_bc.append(acc_bc)

    width = 2 * cols + heads
    g_few = ordered(
        functools.partial(few_kernel, cols, heads),
        8,
        [pl.BlockSpec((LEN, dim // 8), lambda i, mine: (0, i))] + [whole(CT, 128)] * 4,
        pl.BlockSpec((256, dim // 8), lambda i, mine: (0, i)),
        sds((256, dim), f32),
        [pltpu.VMEM((LEN, 256), bf16)],
        flops=CHEAP,
        moved=CHEAP,
        prefetch=1,
    )(which, normed, dsp[0], dsp[1], ddt[0], ddt[1])
    near[0], far[0] = near_step(total_0, dsp[0], total_0)
    local_sum = [
        mtg[j][:, 0] + m[:, 0] + n[:, 0] for j, m, n in ((0, mtb_0, mtc_0), (1, mtb_1, mtc_1))
    ]
    mean_sum = line_sum(jnp.concatenate(local_sum))
    mixer = jnp.concatenate([mixed_0, mixed_1], axis=0).astype(f32)

    def both_cores(v):
        got = cross(v, 1)
        first = core == 0
        return jnp.concatenate([jnp.where(first, v, got), jnp.where(first, got, v)], axis=0)

    def rows_sum(v):
        bit = 1
        while bit < nrows:
            v = v + cross(v, bit)
            bit *= 2
        return v

    g_z, g_out = (chip_parts(chip_sum(v)) for v in (z_sum, out_sum))
    g_few = rows_sum(g_few[:width] + swap(g_few[128 : 128 + width].astype(bf16)).astype(f32))
    g_out = both_cores(g_out)
    grad_w_out = jnp.concatenate(
        [
            g_out[(q * groups + z) * local_dim : (q * groups + z + 1) * local_dim]
            for z in range(groups)
            for q in range(2)
        ],
        axis=0,
    ).T.astype(f32)
    grad_w_bc = g_few[: 2 * cols].reshape(2, cols, dim).transpose(2, 0, 1)
    grad_w_dt = g_few[2 * cols :].T
    x_far, z_far = cross(g_x, 1), cross(g_z, 1)
    steps = 8
    size = dim // steps
    at = pl.BlockSpec((size, lanes), lambda i, core: (i % (steps // 2), 0))
    grad_w_zx = ordered(
        join_kernel,
        steps,
        [at] * 4,
        pl.BlockSpec((size * 2 * lanes // 128, 128), lambda i, core: (i, 0)),
        sds((dim * 2 * lanes // 128, 128), f32),
        moved=24 << 20,
        prefetch=1,
    )(core_at, g_z, z_far, g_x, x_far)
    grad_w_zx = grad_w_zx.reshape(dim, lanes // 128, 2, 128).transpose(0, 2, 1, 3)
    grad_w_zx = grad_w_zx.reshape(dim, 2, lanes)

    acc = sum(accs).reshape(2, 6, 8, lanes).sum(axis=2)
    gg = sum(ggs).sum(axis=0).reshape(2, 1, lanes)
    acc_dt = sum(accs_dt).reshape(2, 8, 128).sum(axis=1)[:, :docl].reshape(2, 2, heads)
    acc_dt = jnp.pad(acc_dt.transpose(1, 0, 2).reshape(2, 1, -1), ((0, 0), (0, 0), (0, lanes - docl)))
    vec = jnp.concatenate([acc, gg, acc_dt], axis=1)
    acc_bc = sum(accs_bc).reshape(5, 8, 128).sum(axis=1)[:, : 4 * cols]

    vec = rows_sum(vec[0] + swap(vec[1]))
    acc_bc = rows_sum(acc_bc + swap(acc_bc)).reshape(5, 2, 2, cols)
    acc_bc = lax.dynamic_index_in_dim(acc_bc, mine, 2, keepdims=False)

    s_all = jnp.concatenate(scales)
    out_near = mixer * s_all[:, None]
    o_own = lax.dynamic_slice_in_dim(out_near, mine * local_dim, local_dim, 1)
    o_far = swap(
        lax.dynamic_slice_in_dim(out_near, (1 - mine) * local_dim, local_dim, 1).astype(bf16)
    )
    r_own = r_wide[:, 0]
    m_own = mean_sum
    r_far = swap(r_own)
    m_far = swap(m_own)
    d_own = jnp.concatenate(near, axis=0)
    d_far = jnp.concatenate(far, axis=0)
    x_near = lax.dynamic_slice_in_dim(hidden_in, me * local_dim, local_dim, 1).astype(f32)
    gain = lax.dynamic_slice_in_dim(norm_gain, me * local_dim, local_dim, 0)
    outs, grads, gain_sum = [], [], 0.0
    for q in range(2):
        sel = mine == q
        x = x_near[q * LEN : (q + 1) * LEN]
        cot = cotangent[q * LEN : (q + 1) * LEN].astype(f32)
        outs.append((x + jnp.where(sel, o_own, o_far.astype(f32))).astype(bf16))
        d = jnp.where(sel, d_own, d_far.astype(f32))
        r = jnp.where(sel, r_own, r_far)[:, None]
        m = jnp.where(sel, m_own, m_far)[:, None]
        grads.append(cot + r * (d * gain) - x * (r * r) * (m / dim))
        gain_sum = gain_sum + jnp.sum(d * x * r, axis=0)
    return (
        jnp.concatenate(outs, axis=0),
        jnp.concatenate(grads, axis=0),
        rows_sum(gain_sum),
        grad_w_zx,
        grad_w_dt,
        grad_w_bc,
        vec[:4],
        vec[4],
        acc_bc[:4],
        acc_bc[4],
        vec[7, heads : 2 * heads],
        vec[7, :heads],
        vec[5].reshape(heads, HD).sum(axis=1),
        vec[6],
        grad_w_out,
    )


STATE = ("zline", "pair")


def solution(mesh):
    placed = (
        P("rows", None),
        P("rows"),
        P("rows", STATE),
        P(),
        P(None, None, STATE),
        P(None, STATE),
        P(None, None, STATE),
        P(None, STATE),
        P(STATE),
        P(None, None, STATE),
        P(None, STATE),
        P(STATE),
        P(STATE),
        P(STATE),
        P(STATE),
        P(STATE, None),
    )
    rows, parts = mesh.devices.shape
    split = Mesh(mesh.devices.reshape(rows, parts // 2, 2), ("rows", "zline", "pair"))
    return jax.shard_map(
        shards,
        mesh=split,
        in_specs=placed,
        out_specs=(
            P("rows", STATE),
            P("rows", STATE),
            P(STATE),
            P(None, None, STATE),
            P(None, STATE),
            P(None, None, STATE),
            P(None, STATE),
            P(STATE),
            P(None, None, STATE),
            P(None, STATE),
            P(STATE),
            P(STATE),
            P(STATE),
            P(STATE),
            P(STATE, None),
        ),
        check_vma=False,
    )
```

```python
import functools

import jax
import jax.numpy as jnp
from jax import lax
from jax.experimental import pallas as pl
from jax.experimental.pallas import tpu as pltpu
from jax.sharding import Mesh
from jax.sharding import PartitionSpec as P

LEN = 2048
BLK = 256
NBLK = LEN // BLK
CHUNKS = 2
CT = LEN // CHUNKS
CB = CT // BLK
HD = 64
NS = 128
EPSILON = 1e-05
HIGHEST = lax.Precision.HIGHEST
f32 = jnp.float32
bf16 = jnp.bfloat16
COST = 1
CHEAP = 1 << 16
VMEM_LIMIT = 56 * 1024 * 1024


def nn(a, b, **kw):
    return lax.dot_general(a, b, (((1,), (0,)), ((), ())), preferred_element_type=f32, **kw)


def nt(a, b):
    return lax.dot_general(a, b, (((1,), (1,)), ((), ())), preferred_element_type=f32)


def tn(a, b):
    return lax.dot_general(a, b, (((0,), (0,)), ((), ())), preferred_element_type=f32)


def iota(shape, dim):
    return lax.broadcasted_iota(jnp.int32, shape, dim)


def sigmoid(v):
    return 1.0 / (1.0 + jnp.exp(-v))


def fold(v):
    return v.reshape(v.shape[0] // 8, 8, v.shape[1]).sum(axis=0)


def expand(cols, off, heads):
    low = iota((cols.shape[0], 128), 1) < HD
    pieces = []
    for p in range(heads // 2):
        a = cols[:, off + 2 * p : off + 2 * p + 1]
        b = cols[:, off + 2 * p + 1 : off + 2 * p + 2]
        pieces.append(jnp.where(low, a, b))
    return jnp.concatenate(pieces, axis=1)


def quad_masks(rows):
    head = iota((rows, 4 * HD), 1) // HD
    return [head == h for h in range(4)]


def stacked(v, masks):
    zero = jnp.zeros_like(v)
    return jnp.concatenate([jnp.where(m, v, zero) for m in masks], axis=0)


def segment_sums(v, off):
    n = v.shape[1]
    pick = (iota((n, 128), 1) == iota((n, 128), 0) // HD + off).astype(bf16)
    high = v.astype(bf16)
    rest = (v - high.astype(f32)).astype(bf16)
    return nn(high, pick) + nn(rest, pick)


def conv_tile(step, x1, kern, msk, buf, start=None):
    @pl.when(step == 0)
    def _():
        buf[0:8, :] = jnp.zeros((8, buf.shape[1]), f32) if start is None else start[...]

    buf[8 : 8 + BLK, :] = x1
    acc = kern[4:5, :] + kern[3:4, :] * x1
    for k in range(1, 4):
        acc = acc + kern[3 - k : 4 - k, :] * (buf[8 - k : 8 - k + BLK, :] * msk[:, k : k + 1])
    buf[0:8, :] = x1[BLK - 8 :, :]
    return acc


def project_tile(n, w, kern, msk, z, xp, a, xs, buf, start=None):
    lanes = w.shape[1] // 2
    p = nn(n, w[...])
    z[...] = p[:, :lanes].astype(bf16)
    x1 = p[:, lanes:]
    xp[...] = x1.astype(bf16)
    acc = conv_tile(pl.program_id(0), x1, kern, msk, buf, start)
    a[...] = acc.astype(bf16)
    xs[...] = (acc * sigmoid(acc)).astype(bf16)


def first_kernel(which, hid, gain, w, kern, msk, start, normed, r, z, xp, a, xs, tail, buf):
    x = hid[...].astype(f32)
    rr = lax.rsqrt(jnp.mean(x * x, axis=1, keepdims=True) + EPSILON)
    n = (x * rr * gain[...]).astype(bf16)
    normed[...] = n
    r[...] = jnp.broadcast_to(rr, (BLK, 128))
    project_tile(n, w, kern, msk, z, xp, a, xs, buf, start)
    tail[...] = buf[0:8, :]


def second_kernel(normed, w, kern, msk, start, z, xp, a, xs, tail, buf):
    project_tile(normed[...], w, kern, msk, z, xp, a, xs, buf, start)
    tail[...] = buf[0:8, :]


def states_kernel(docl, normed, ws, kern, dtp, msk, bcp, bca, bc, dtr, dt, cum, cumt, buf):
    q = nt(normed[...], ws[...])
    x1 = q[:, : 2 * NS]
    bcp[...] = x1
    acc = conv_tile(pl.program_id(0), x1, kern, msk, buf)
    bca[...] = acc
    bc[...] = (acc * sigmoid(acc)).astype(bf16)
    d = q[:, 2 * NS :]
    dtr[...] = d
    v = d + dtp[0:1, :]
    e = jnp.exp(-jnp.abs(v))
    small = e * (1.0 - e * (0.5 - e * (1.0 / 3.0 - 0.25 * e)))
    step = jnp.maximum(v, 0.0) + jnp.where(e < 0.01, small, jnp.log(1.0 + e))
    lane = iota((BLK, 128), 1)
    step = jnp.where(lane < docl, step, 0.0)
    dt[...] = step
    ext = jnp.where(lane == docl, msk[:, 0:1], step * dtp[1:2, :])
    tri = (iota((BLK, BLK), 0) >= iota((BLK, BLK), 1)).astype(f32)
    c = nn(tri, ext, precision=HIGHEST)
    cum[...] = c
    cumt[...] = c.T


def block_scalars(docl, cum):
    lane = iota((BLK, 128), 1)
    doc = cum[:, docl : docl + 1]
    doc_last = cum[BLK - 1 : BLK, docl : docl + 1]
    rates = jnp.where(lane < docl, cum, 0.0)
    last = rates[BLK - 1 : BLK, :]
    lead = jnp.exp(rates) * (doc == 0.0).astype(f32)
    trail = jnp.exp(last - rates) * (doc == doc_last).astype(f32)
    retain = jnp.exp(last) * (doc_last == 0.0).astype(f32)
    return lead, trail, retain


def scan_kernel(docl, off, xs, z, bc, dt, cum, cumt, prm, start, y, gw, sin, pw, state):
    lanes = xs.shape[1]
    heads = lanes // HD

    @pl.when(pl.program_id(0) == 0)
    def _():
        state[...] = start[...]

    s_in = state[...]
    sin[0] = s_in
    b = bc[:, :NS]
    c = bc[:, NS:]
    cumv = cum[...]
    lead, trail, retain = block_scalars(docl, cumv)
    within = (cumv[:, docl : docl + 1] == cumt[docl : docl + 1, :]) & (
        iota((BLK, BLK), 0) >= iota((BLK, BLK), 1)
    )
    bias = jnp.where(within, 0.0, -1e30)
    g = nt(c, b)
    xf = xs[...].astype(f32)
    u = xf * expand(dt[...], off, heads)
    ub = u.astype(bf16)
    masks = quad_masks(BLK)
    parts = []
    for q in range(heads // 4):
        mixes = []
        for h in range(off + 4 * q, off + 4 * q + 4):
            decay = jnp.exp((cumv[:, h : h + 1] - cumt[h : h + 1, :]) + bias)
            mixes.append((decay * g).astype(bf16))
        uq = ub[:, q * 256 : q * 256 + 256]
        parts.append(nn(jnp.concatenate(mixes, axis=1), stacked(uq, masks)))
    yv = jnp.concatenate(parts, axis=1)
    yv = yv + nn(c, s_in.astype(bf16)) * expand(lead, off, heads) + prm[6:7, :] * xf
    y[...] = yv
    ut = (u * expand(trail, off, heads)).astype(bf16)
    state[...] = s_in * expand(retain, off, heads) + tn(b, ut)
    zz = z[...].astype(f32)
    gated = yv * zz * sigmoid(zz)
    gw[...] = (gated * prm[5:6, :]).astype(bf16)
    pw[...] = jnp.broadcast_to(jnp.sum(gated * gated, axis=1, keepdims=True), (BLK, 128))


def out_kernel(ga, gb, wa, wb, o):
    o[...] = (nn(ga[...], wa[...]) + nn(gb[...], wb[...])).astype(bf16)


def dyn_kernel(c, wa, wb, ga, gb, da, db, qs):
    cv = c[...]
    a = nt(cv, wa[...])
    b = nt(cv, wb[...])
    da[...] = a.astype(bf16)
    db[...] = b.astype(bf16)
    q = jnp.sum(a * ga[...].astype(f32), axis=1, keepdims=True)
    q = q + jnp.sum(b * gb[...].astype(f32), axis=1, keepdims=True)
    qs[...] = jnp.broadcast_to(q, (BLK, 128))


def gate_kernel(sq, da, db, ya, yb, za, zb, prma, prmb, dz, dy, yn, mt, gg):
    lanes = da.shape[1]
    s = sq[:, 0:1]
    kq = sq[:, 1:2]

    @pl.when(pl.program_id(0) == 0)
    def _():
        gg[...] = jnp.zeros_like(gg)

    total = jnp.zeros((BLK, 1), f32)
    for half, (dref, yref, zref, prm) in enumerate(((da, ya, za, prma), (db, yb, zb, prmb))):
        at = slice(half * lanes, half * lanes + lanes)
        dn = dref[...].astype(f32)
        y = yref[...]
        z = zref[...].astype(f32)
        gn = prm[5:6, :]
        sg = sigmoid(z)
        act = z * sg
        g = y * act
        gs = g * s
        yn[:, at] = (gs * gn).astype(bf16)
        gg[:, at] += fold(dn * gs)
        dg = s * (dn * gn) - g * kq
        dy[:, at] = (dg * act).astype(bf16)
        low = (dg * y * (sg * (1.0 + z * (1.0 - sg)))).astype(bf16)
        dz[:, at] = low
        total = total + jnp.sum(low.astype(f32) * z, axis=1, keepdims=True)
    mt[...] = jnp.broadcast_to(total, (BLK, 128))


def conv_back(da, xp, kern, buf, mbuf):
    dx = kern[3:4, :] * da
    taps = [None, None, None, fold(xp * da)]
    for k in range(1, 4):
        sh = buf[k : k + BLK, :] * mbuf[k : k + BLK, k : k + 1]
        dx = dx + kern[3 - k : 4 - k, :] * sh
        taps[3 - k] = fold(xp * sh)
    return dx, taps


def back_kernel(
    docl,
    dy, bc, dt, cum, cumt, dtr, msk, dtp,
    ya, yb, xsa, xsb, aa, ab, xpa, xpb, sia, sib, prma, prmb,
    ds_in, cda_in, cm_in,
    dxp, ddt, dbc, mt, acc, accs, ds, cda, cm,
    buf, mbuf,
):
    lanes = xsa.shape[1]
    heads = lanes // HD
    step = pl.program_id(0)

    @pl.when(step == 0)
    def _():
        ds[...] = ds_in[...]
        buf[:, 0:8, :] = cda_in[...]
        mbuf[0:8, :] = cm_in[...]
        acc[...] = jnp.zeros_like(acc)
        accs[...] = jnp.zeros_like(accs)

    mbuf[BLK : BLK + 8, :] = mbuf[0:8, :]
    mbuf[0:BLK, :] = msk[...]
    b = bc[:, :NS]
    c = bc[:, NS:]
    cumv = cum[...]
    lead, trail, retain = block_scalars(docl, cumv)
    within = (cumv[:, docl : docl + 1] == cumt[docl : docl + 1, :]) & (
        iota((BLK, BLK), 0) <= iota((BLK, BLK), 1)
    )
    bias = jnp.where(within, 0.0, -1e30)
    gt = nt(b, c)
    masks = quad_masks(BLK)
    dgt = jnp.zeros((BLK, BLK), f32)
    d_c = jnp.zeros((BLK, NS), f32)
    d_b = jnp.zeros((BLK, NS), f32)
    r1 = jnp.zeros((BLK, 128), f32)
    r2 = jnp.zeros((BLK, 128), f32)
    r3 = jnp.zeros((BLK, 128), f32)
    held = jnp.zeros((8, 128), f32)
    total = jnp.zeros((BLK, 1), f32)
    refs = ((ya, xsa, aa, xpa, sia, prma), (yb, xsb, ab, xpb, sib, prmb))
    for half, (yr, xsr, ar, xpr, sir, prm) in enumerate(refs):
        off = half * heads
        at = slice(half * lanes, half * lanes + lanes)
        dyb = dy[:, at]
        dyf = dyb.astype(f32)
        skip = prm[6:7, :]
        xf = xsr[...].astype(f32)
        dte = expand(dt[...], off, heads)
        u = xf * dte
        ub = u.astype(bf16)
        ubf = ub.astype(f32)
        s_in = sir[0]
        d_state = ds[half]
        dsb = d_state.astype(bf16)
        te = expand(trail, off, heads)
        tb = te * nn(b, dsb)
        parts = []
        for q in range(heads // 4):
            uq = ub[:, q * 256 : q * 256 + 256]
            dq = dyb[:, q * 256 : q * 256 + 256]
            dmt = nt(stacked(uq, masks), dq)
            mixes = []
            for i in range(4):
                h = off + 4 * q + i
                decay = jnp.exp((cumt[h : h + 1, :] - cumv[:, h : h + 1]) + bias)
                mixes.append((decay * gt).astype(bf16))
                dgt = dgt + dmt[i * BLK : i * BLK + BLK, :] * decay
            parts.append(nn(jnp.concatenate(mixes, axis=1), stacked(dq, masks)))
        du = jnp.concatenate(parts, axis=1) + tb
        ldy = (expand(lead, off, heads) * dyf).astype(bf16)
        d_c = d_c + nt(ldy, s_in.astype(bf16))
        d_b = d_b + nt((te * u).astype(bf16), dsb)
        ds[half] = d_state * expand(retain, off, heads) + tn(c, ldy)
        r1 = r1 + segment_sums(dyf * (yr[...] - skip * xf) - ubf * du, off)
        r2 = r2 + segment_sums(ubf * tb, off)
        r3 = r3 + segment_sums(xf * du, off)
        held = held + segment_sums(fold(d_state * s_in), off)
        a = ar[...].astype(f32)
        sa = sigmoid(a)
        da = (dte * du + skip * dyf) * (sa * (1.0 + a * (1.0 - sa)))
        buf[half, BLK : BLK + 8, :] = buf[half, 0:8, :]
        buf[half, 0:BLK, :] = da
        xp = xpr[...].astype(f32)
        dx, taps = conv_back(da, xp, prm, buf.at[half], mbuf)
        low = dx.astype(bf16)
        dxp[:, at] = low
        total = total + jnp.sum(low.astype(f32) * xp, axis=1, keepdims=True)
        for k in range(4):
            acc[half, 8 * k : 8 * k + 8, :] += taps[k]
        acc[half, 32:40, :] += fold(da)
        acc[half, 40:48, :] += fold(dyf * xf)
    dgb = dgt.astype(bf16)
    dbc[:, :NS] = (d_b + nn(dgb, c)).astype(bf16)
    dbc[:, NS:] = (d_c + tn(dgb, b)).astype(bf16)
    at_last = jnp.sum(r2, axis=0, keepdims=True) + retain * jnp.sum(held, axis=0, keepdims=True)
    dcum = r1 + jnp.where(iota((BLK, 128), 0) == BLK - 1, at_last, 0.0)
    later = (iota((BLK, BLK), 1) >= iota((BLK, BLK), 0)).astype(f32)
    drate = nn(later, dcum, precision=HIGHEST)
    rate = dtp[1:2, :]
    lane = iota((BLK, 128), 1)
    draw = jnp.where(lane < docl, (r3 + rate * drate) * sigmoid(dtr[...] + dtp[0:1, :]), 0.0)
    low = draw.astype(bf16)
    ddt[...] = low
    accs[0:8, :] += fold(drate * dt[...]) * rate
    accs[8:16, :] += fold(draw)
    total = total + jnp.sum(low.astype(f32) * dtr[...], axis=1, keepdims=True)
    mt[...] = jnp.broadcast_to(total, (BLK, 128))
    cda[...] = buf[:, 0:8, :]
    cm[...] = mbuf[0:8, :]


def states_back_kernel(dbc, bca, bcp, msk, kern, cda_in, cm_in, dsp, mt, acc, cda, cm, buf, mbuf):
    @pl.when(pl.program_id(0) == 0)
    def _():
        buf[0:8, :] = cda_in[...]
        mbuf[0:8, :] = cm_in[...]
        acc[...] = jnp.zeros_like(acc)

    mbuf[BLK : BLK + 8, :] = mbuf[0:8, :]
    mbuf[0:BLK, :] = msk[...]
    a = bca[...]
    sa = sigmoid(a)
    da = dbc[...].astype(f32) * (sa * (1.0 + a * (1.0 - sa)))
    buf[BLK : BLK + 8, :] = buf[0:8, :]
    buf[0:BLK, :] = da
    xp = bcp[...]
    dx, taps = conv_back(da, xp, kern, buf, mbuf)
    low = dx.astype(bf16)
    dsp[...] = low
    mt[...] = jnp.broadcast_to(jnp.sum(low.astype(f32) * xp, axis=1, keepdims=True), (BLK, 128))
    for k in range(4):
        acc[8 * k : 8 * k + 8, :] += taps[k]
    acc[32:40, :] += fold(da)
    cda[...] = buf[0:8, :]
    cm[...] = mbuf[0:8, :]


def dn_kernel(dz, dxp, ddt, dbc, wa, wb, wdt, o):
    n = wa.shape[1] // 2
    wide = wa.shape[0]
    v = nt(dz[:, :n], wa[:, :n]) + nt(dxp[:, :n], wa[:, n:])
    v = v + nt(dz[:, n:], wb[:, :n]) + nt(dxp[:, n:], wb[:, n:])
    o[:, :wide] = (v + nt(ddt[...], wdt[...])).astype(bf16)
    cols = NS // pl.num_programs(0)
    row, lane = iota((2 * NS, 128), 0), iota((2 * NS, 128), 1)
    source = lane // cols * NS + pl.program_id(0) * cols + lane % cols
    pick = ((row == source) & (lane < 2 * cols)).astype(bf16)
    o[:, wide:] = nn(dbc[...], pick).astype(bf16)


def weight_kernel(count, tiles, extra, core, *refs):
    lhs, rhs, more, (keep, give) = refs[:count], refs[count : 2 * count], refs[2 * count : -2], refs[-2:]
    v = tn(lhs[0][...], rhs[0][...])
    for k in range(1, count):
        v = v + tn(lhs[k][...], rhs[k][...])
    if extra:
        part = lhs[0].shape[0]
        w = tn(lhs[0][...], more[0][:part, :])
        for k in range(1, count):
            w = w + tn(lhs[k][...], more[0][k * part : (k + 1) * part, :])
        n, m = v.shape[1] // 2, w.shape[1] // 2
        v = jnp.concatenate([v[:, :n], w[:, :m], v[:, n:], w[:, m:]], axis=1)
    step = pl.program_id(0)

    @pl.when(step < tiles)
    def _():
        keep[...] = v

    @pl.when(step >= tiles)
    def _():
        give[...] = v


def few_kernel(cols, heads, mine, lhs, dsp_0, dsp_1, ddt_0, ddt_1, o, few):
    @pl.when(pl.program_id(0) == 0)
    def _():
        row, lane = iota((128, 256), 0), iota((128, 256), 1)
        side, c = lane // 128, lane % 128
        pair = jnp.where(side == 0, mine[0], 1 - mine[0])
        state = (row == c // cols * 2 * cols + pair * cols + c % cols) & (c < 2 * cols)
        step = (row == side * heads + c - 2 * cols) & (c >= 2 * cols) & (c < 2 * cols + heads)
        for k, (dsp, ddt) in enumerate(((dsp_0, ddt_0), (dsp_1, ddt_1))):
            v = nn(dsp[...], state.astype(bf16)) + nn(ddt[...], step.astype(bf16))
            few[k * CT : k * CT + CT, :] = v.astype(bf16)

    o[...] = tn(few[...], lhs[...])


def join_kernel(core, za, zb, xa, xb, o):
    first = pl.program_id(0) * 2 // pl.num_programs(0) == core[0]
    rows, lanes = za.shape
    parts = lanes // 128

    def put(z, x):
        for k in range(parts):
            at = slice(k * 128, k * 128 + 128)
            o[pl.ds(2 * k, rows, stride=2 * parts), :] = z[:, at].astype(f32)
            o[pl.ds(2 * k + 1, rows, stride=2 * parts), :] = x[:, at].astype(f32)

    @pl.when(first)
    def _():
        put(za, xa)

    @pl.when(jnp.logical_not(first))
    def _():
        put(zb, xb)


def tile(width, first=0):
    return pl.BlockSpec((BLK, width), lambda i, *_: (first + i, 0))


def back_tile(width, last):
    return pl.BlockSpec((BLK, width), lambda i, *_: (last - i, 0))


def whole(*shape):
    zeros = (0,) * len(shape)
    return pl.BlockSpec(shape, lambda i, *_: zeros)


def sds(shape, dtype):
    return jax.ShapeDtypeStruct(shape, dtype)


def call(
    kernel, grid, in_specs, out_specs, out_shape, scratch=(), flops=0, moved=0, prefetch=0, after=(), into=()
):
    first = prefetch + len(in_specs)
    extra = len(after) + len(into)

    def body(*refs):
        kernel(*refs[:first], *refs[first + extra :])

    fn = pl.pallas_call(
        body,
        grid_spec=pltpu.PrefetchScalarGridSpec(
            num_scalar_prefetch=prefetch,
            grid=(grid,),
            in_specs=list(in_specs) + [pl.BlockSpec(memory_space=pl.ANY)] * extra,
            out_specs=out_specs,
            scratch_shapes=list(scratch),
        ),
        out_shape=out_shape,
        input_output_aliases={first + len(after) + k: k for k in range(len(into))},
        compiler_params=pltpu.CompilerParams(
            dimension_semantics=("arbitrary",), vmem_limit_bytes=VMEM_LIMIT
        ),
        cost_estimate=pl.CostEstimate(flops=flops // COST, bytes_accessed=moved // COST, transcendentals=0),
    )
    return lambda *args: fn(*args, *after, *into)


def three(v):
    high = lax.optimization_barrier(v.astype(bf16))
    rest = v - high.astype(f32)
    mid = lax.optimization_barrier(rest.astype(bf16))
    return high, mid, (rest - mid.astype(f32)).astype(bf16)


def shards(
    hidden_in, starts, cotangent, norm_gain, w_zx, w_dt, w_bc, conv_x_w, conv_x_b,
    conv_bc_w, conv_bc_b, dt_bias, a_log, d_skip, gnorm_w, w_out,
):
    order = []

    def ordered(*args, after=(), **kw):
        def run(*operands):
            outs = call(*args, after=tuple(after) + tuple(order[-1:]), **kw)(*operands)
            order.append(jax.tree.leaves(outs)[-1])
            return outs

        return run

    groups = lax.axis_size("zline")
    parts = 2 * groups
    nrows = lax.axis_size("rows")
    zpos = lax.axis_index("zline")
    mine = lax.axis_index("pair")
    me = 2 * zpos + mine
    core = lax.axis_index("rows") % 2
    dim = hidden_in.shape[1]
    local_dim = cotangent.shape[1]
    lanes = w_zx.shape[2]
    heads = w_dt.shape[1]
    inner = lanes * parts
    docl = 2 * heads
    wide = dim // groups

    def swap(v):
        return lax.ppermute(v, "pair", [(0, 1), (1, 0)])

    def cross(v, bit):
        return lax.ppermute(v, "rows", [(i, i ^ bit) for i in range(nrows)])

    def line_sum(v):
        bit = 1
        while bit < groups:
            v = v + lax.ppermute(v, "zline", [(i, i ^ bit) for i in range(groups)])
            bit *= 2
        return v

    def rows_of(v, start, size):
        return lax.dynamic_slice_in_dim(v, start, size, 0)

    def zero_after(v):
        return (v.reshape(-1)[0].astype(f32) > 1e38).astype(jnp.int32)

    def late(v, after):
        return v + zero_after(after).astype(v.dtype)

    def half_of_partner(own, after=None):
        half = own.shape[0] // 2
        at = core * half if after is None else core * half + zero_after(after)
        return swap(rows_of(own, at, half))

    def with_other_half(got, after):
        other = cross(got, 1)
        first = core + zero_after(after) == 0
        return jnp.concatenate([jnp.where(first, got, other), jnp.where(first, other, got)], axis=0)

    w_a = w_zx.reshape(dim, 2 * lanes)
    o_a = w_out
    small = jnp.stack([dt_bias, a_log, d_skip]).reshape(-1)
    prm_a = jnp.concatenate(
        [
            conv_x_w,
            conv_x_b[None],
            gnorm_w[None],
            jnp.repeat(d_skip, HD)[None],
            jnp.pad(small, (0, lanes - small.shape[0]))[None],
        ],
        axis=0,
    )
    prm_b = swap(prm_a)
    small_b = prm_b[7, : 3 * heads].reshape(3, heads)
    wdt_a = w_dt.T
    wdt_b = swap(wdt_a)
    bias_all = jnp.concatenate([dt_bias, small_b[0]])
    rate_all = -jnp.exp(jnp.concatenate([a_log, small_b[1]]))
    dtp = jnp.pad(jnp.stack([bias_all, rate_all]), ((0, 6), (0, 128 - docl)))
    taps = jnp.concatenate([conv_bc_w, conv_bc_b[None]], axis=0).transpose(1, 2, 0)
    high, mid, low = three(taps)
    pack = jnp.concatenate([w_bc.transpose(1, 2, 0), high, mid, low], axis=2)
    pack = jnp.pad(pack, ((0, 0), (0, 0), (0, 128 - 15)))

    pack = lax.all_gather(pack, ("zline", "pair"), axis=1, tiled=True)
    is0 = mine == 0
    c_got = swap(rows_of(cotangent, (1 - mine) * LEN, LEN))
    w_got = half_of_partner(w_a)
    o_got = half_of_partner(w_out)
    c_mine = rows_of(cotangent, mine * LEN, LEN)
    c_mine = lax.all_gather(c_mine, "zline", axis=1, tiled=True)
    pack = pack.reshape(2 * NS, dim + 128)
    wbc = pack[:, :dim]
    taps = pack[:, dim : dim + 15].astype(f32).reshape(2 * NS, 3, 5).sum(axis=1)
    kern_bc = jnp.pad(taps.T, ((0, 3), (0, 0)))
    wdt = jnp.concatenate([wdt_a, wdt_b, jnp.zeros((128 - docl, dim), bf16)], axis=0)
    wst = jnp.concatenate([wbc, wdt], axis=0)

    st = rows_of(starts, mine * LEN, LEN).astype(f32)
    open1 = jnp.where(jnp.arange(LEN) == 0, 0.0, 1.0 - st)
    open2 = open1 * jnp.concatenate([jnp.zeros((1,), f32), open1[:-1]])
    open3 = open2 * jnp.concatenate([jnp.zeros((2,), f32), open1[:-2]])
    msk = jnp.pad(jnp.stack([st, open1, open2, open3], axis=1), ((0, 0), (0, 124)))
    which = mine.astype(jnp.int32).reshape(1)

    tl = (BLK, lanes)
    proj_out = [tile(lanes), tile(lanes), tile(lanes), tile(lanes)]
    proj_shape = [sds((LEN, lanes), bf16)] * 4
    pf = 2 * LEN * dim * 2 * lanes

    normed, r_wide, z_a, xp_a, a_a, xs_a, tail = ordered(
        first_kernel,
        NBLK,
        [
            pl.BlockSpec((BLK, dim), lambda i, which: (which[0] * NBLK + i, 0)),
            whole(1, dim),
            whole(dim, 2 * lanes),
            whole(8, lanes),
            tile(128),
            whole(8, lanes),
        ],
        [tile(dim), tile(128)] + [tile(lanes)] * 4 + [whole(8, lanes)],
        [sds((LEN, dim), bf16), sds((LEN, 128), f32)] + proj_shape + [sds((8, lanes), f32)],
        [pltpu.VMEM((BLK + 8, lanes), f32)],
        flops=pf,
        moved=40 << 20,
        prefetch=1,
        after=(prm_b, wdt_b),
    )(which, hidden_in, norm_gain.reshape(1, dim), w_a, prm_a, msk, jnp.zeros((8, lanes), f32))
    bcp, bca, bc, dtr, dt, cum, cumt = ordered(
        functools.partial(states_kernel, docl),
        NBLK,
        [tile(dim), whole(2 * NS + 128, dim), whole(8, 2 * NS), whole(8, 128), tile(128)],
        [tile(2 * NS)] * 3 + [tile(128)] * 3 + [pl.BlockSpec((128, BLK), lambda i: (0, i))],
        [sds((LEN, 2 * NS), f32)] * 2
        + [sds((LEN, 2 * NS), bf16)]
        + [sds((LEN, 128), f32)] * 3
        + [sds((128, LEN), f32)],
        [pltpu.VMEM((BLK + 8, 2 * NS), f32)],
        flops=2 * LEN * dim * 512,
        moved=18 << 20,
    )(normed, wst, kern_bc, dtp, msk)

    def line_scatter(v, axis=1):
        return lax.psum_scatter(v, "zline", scatter_dimension=axis, tiled=True)

    no_tail = jnp.zeros((8, lanes), f32)
    no_state = jnp.zeros((NS, lanes), f32)

    def scan(off, xs, z, prm, start=no_state, at=0, blocks=NBLK, into=(), after=()):
        return ordered(
            functools.partial(scan_kernel, docl, off),
            blocks,
            [
                tile(lanes, at), tile(lanes, at), tile(2 * NS, at), tile(128, at), tile(128, at),
                pl.BlockSpec((128, BLK), lambda i: (0, at + i)), whole(8, lanes), whole(NS, lanes),
            ],
            [
                tile(lanes, at), tile(lanes, at),
                pl.BlockSpec((1, NS, lanes), lambda i: (at + i, 0, 0)), tile(128, at), whole(NS, lanes),
            ],
            [
                sds((LEN, lanes), f32),
                sds((LEN, lanes), bf16),
                sds((NBLK, NS, lanes), f32),
                sds((LEN, 128), f32),
                sds((NS, lanes), f32),
            ],
            flops=(10 << 30) * blocks // NBLK,
            moved=(20 << 20) * blocks // NBLK,
            into=into,
            after=after,
        )(xs, z, bc, dt, cum, cumt, prm, start)

    def second_step(start, at, blocks, into):
        return ordered(
            second_kernel,
            blocks,
            [tile(dim, at), whole(dim, 2 * lanes), whole(8, lanes), tile(128, at), whole(8, lanes)],
            [tile(lanes, at)] * 4 + [whole(8, lanes)],
            proj_shape + [sds((8, lanes), f32)],
            [pltpu.VMEM((BLK + 8, lanes), f32)],
            flops=pf * blocks // NBLK,
            moved=(28 << 20) * blocks // NBLK,
            into=into,
        )(normed, w_b, prm_b, msk, start)

    def out_step(j):
        return ordered(
            out_kernel,
            CB,
            [tile(lanes, j * CB)] * 2 + [whole(lanes, dim)] * 2,
            tile(dim),
            sds((CT, dim), bf16),
            flops=4 * CT * lanes * dim,
            moved=10 << 20,
        )(gw_a, gw_b, o_a, o_b)

    y_a, gw_a, sin_a, pw_a, _ = scan(0, xs_a, z_a, prm_a, after=(w_got,))
    w_b = with_other_half(w_got, pw_a)
    c_got = lax.all_gather(late(c_got, pw_a), "zline", axis=1, tiled=True)
    half = NBLK // 2
    *begun, tail = second_step(no_tail, 0, half, ())
    *done, state = scan(heads, begun[3], begun[0], prm_b, no_state, 0, half)
    o_b = with_other_half(late(o_got, tail), state)
    gw_b = done[1]
    mixed_0 = line_scatter(out_step(0))
    z_b, xp_b, a_b, xs_b, _ = second_step(tail, half, half, begun)
    y_b, gw_b, sin_b, pw_b, _ = scan(heads, xs_b, z_b, prm_b, state, half, half, done)

    c_all = [None] * CHUNKS
    for j in reversed(range(CHUNKS)):
        mine_j, got_j = (v[j * CT : (j + 1) * CT] for v in (c_mine, c_got))
        c_all[j] = jnp.concatenate(
            [jnp.where(is0, mine_j, got_j), jnp.where(is0, got_j, mine_j)], axis=1
        )

    def reordered(w):
        return jnp.concatenate(
            [
                w[:, (2 * z + q) * local_dim : (2 * z + q + 1) * local_dim]
                for q in range(2)
                for z in range(groups)
            ],
            axis=1,
        )

    p_a, p_b = reordered(o_a), reordered(o_b)

    power = pw_a[:, 0] + pw_b[:, 0]
    wdt_t = wdt.T
    cols = w_bc.shape[2]

    def group_columns(v, group):
        v = v.reshape(-1, 2, NS)
        return lax.dynamic_slice_in_dim(v, group * 2 * cols, 2 * cols, 2).reshape(-1, 4 * cols)

    def near_columns(v):
        return jnp.pad(group_columns(v, zpos), ((0, 0), (0, 128 - 4 * cols)))

    bca_near, bcp_near, kern_near = near_columns(bca), near_columns(bcp), near_columns(kern_bc)
    wbc_near = lax.dynamic_slice_in_dim(wbc, zpos * wide, wide, 1).T
    wbc_near = jnp.concatenate(
        [group_columns(wbc_near, (zpos + groups - k) % groups) for k in range(groups)], axis=1
    ).T

    def dyn_step(j, after=()):
        return ordered(
            dyn_kernel,
            CB,
            [tile(dim), whole(lanes, dim), whole(lanes, dim), tile(lanes, j * CB), tile(lanes, j * CB)],
            [tile(lanes), tile(lanes), tile(128)],
            [sds((CT, lanes), bf16)] * 2 + [sds((CT, 128), f32)],
            flops=4 * CT * lanes * dim,
            moved=12 << 20,
            after=after,
        )(c_all[j], p_a, p_b, gw_a, gw_b)

    def scales_of(j, qs):
        sums = line_sum(jnp.concatenate([power[j * CT : (j + 1) * CT], qs[:, 0]]))
        s = lax.rsqrt(sums[:CT] / inner + EPSILON)
        kq = s * s * s * (sums[CT:] / inner)
        return s, jnp.pad(jnp.stack([s, kq], axis=1), ((0, 0), (0, 126)))

    def gate_step(j, sq, d_a, d_b, after=()):
        return ordered(
            gate_kernel,
            CB,
            [tile(128)] + [tile(lanes)] * 2 + [tile(lanes, j * CB)] * 4 + [whole(8, lanes)] * 2,
            [tile(2 * lanes)] * 3 + [tile(128), whole(8, 2 * lanes)],
            [sds((CT, 2 * lanes), bf16)] * 3 + [sds((CT, 128), f32), sds((8, 2 * lanes), f32)],
            flops=4000 * CT * lanes,
            moved=20 << 20,
            after=after,
        )(sq, d_a, d_b, y_a, y_b, z_a, z_b, prm_a, prm_b)

    def back_step(j, dy, ds, cda, cm, after=()):
        last = j * CB + CB - 1

        def bt(width):
            return back_tile(width, last)

        def loc(width):
            return back_tile(width, CB - 1)

        cols = pl.BlockSpec((128, BLK), lambda i: (0, last - i))
        sins = pl.BlockSpec((1, NS, lanes), lambda i: (last - i, 0, 0))
        return ordered(
            functools.partial(back_kernel, docl),
            CB,
            [
                loc(2 * lanes), bt(2 * NS), bt(128), bt(128), cols, bt(128), bt(128), whole(8, 128),
                bt(lanes), bt(lanes), bt(lanes), bt(lanes), bt(lanes), bt(lanes), bt(lanes), bt(lanes),
                sins, sins, whole(8, lanes), whole(8, lanes),
                whole(2, NS, lanes), whole(2, 8, lanes), whole(8, 128),
            ],
            [
                loc(2 * lanes), loc(128), loc(2 * NS), loc(128), whole(2, 48, lanes), whole(16, 128),
                whole(2, NS, lanes), whole(2, 8, lanes), whole(8, 128),
            ],
            [
                sds((CT, 2 * lanes), bf16), sds((CT, 128), bf16), sds((CT, 2 * NS), bf16),
                sds((CT, 128), f32), sds((2, 48, lanes), f32), sds((16, 128), f32),
                sds((2, NS, lanes), f32), sds((2, 8, lanes), f32), sds((8, 128), f32),
            ],
            [pltpu.VMEM((2, BLK + 8, lanes), f32), pltpu.VMEM((BLK + 8, 128), f32)],
            flops=(80 << 30) // CHUNKS,
            moved=(80 << 20) // CHUNKS,
            after=after,
        )(
            dy, bc, dt, cum, cumt, dtr, msk, dtp,
            y_a, y_b, xs_a, xs_b, a_a, a_b, xp_a, xp_b, sin_a, sin_b, prm_a, prm_b,
            ds, cda, cm,
        )

    def states_step(j, dbc, sda, scm, after=()):
        last = j * CB + CB - 1

        def bt(width):
            return back_tile(width, last)

        def loc(width):
            return back_tile(width, CB - 1)

        return ordered(
            states_back_kernel,
            CB,
            [
                pl.BlockSpec((BLK, 128), lambda i: (CB - 1 - i, wide // 128)),
                bt(128), bt(128), bt(128), whole(8, 128), whole(8, 128), whole(8, 128),
            ],
            [loc(128), loc(128), whole(40, 128), whole(8, 128), whole(8, 128)],
            [
                sds((CT, 128), bf16), sds((CT, 128), f32), sds((40, 128), f32),
                sds((8, 128), f32), sds((8, 128), f32),
            ],
            [pltpu.VMEM((BLK + 8, 128), f32), pltpu.VMEM((BLK + 8, 128), f32)],
            flops=CHEAP,
            moved=CHEAP,
            after=after,
        )(dbc, bca_near, bcp_near, msk, kern_near, sda, scm)

    def dn_step(dz, dxp, ddt, dbc, after=()):
        return ordered(
            dn_kernel,
            groups,
            [
                whole(CT, 2 * lanes), whole(CT, 2 * lanes), whole(CT, 128), whole(CT, 2 * NS),
                pl.BlockSpec((wide, 2 * lanes), lambda i: (i, 0)),
                pl.BlockSpec((wide, 2 * lanes), lambda i: (i, 0)),
                pl.BlockSpec((wide, 128), lambda i: (i, 0)),
            ],
            pl.BlockSpec((CT, wide + 128), lambda i: (i, 0)),
            sds((groups * CT, wide + 128), bf16),
            flops=8 * CT * lanes * dim,
            moved=16 << 20,
            after=after,
        )(dz, dxp, ddt, dbc, w_a, w_b, wdt_t)

    def near_step(total, dsp, after):
        mine_first = [dsp[:, : 4 * cols]] + [
            lax.ppermute(dsp[:, : 4 * cols], "zline", [(i, (i + k) % groups) for i in range(groups)])
            for k in range(1, groups)
        ]
        total = late(total[:, :wide].astype(f32), after) + nn(jnp.concatenate(mine_first, axis=1), wbc_near)
        keep = lax.dynamic_slice_in_dim(total, mine * local_dim, local_dim, 1)
        give = lax.dynamic_slice_in_dim(total, (1 - mine) * local_dim, local_dim, 1)
        return keep, swap(give.astype(bf16))

    core_at = core.astype(jnp.int32).reshape(1)

    def weight_grad(lhs, rhs, more=None, after=()):
        count = len(rhs)
        n, m = lhs[0].shape[1], rhs[0].shape[1]
        part = LEN // count
        more = [] if more is None else [more]
        full = m + sum(v.shape[1] for v in more)
        size = min(256, n // 4)
        tiles = n // size // 2

        def order(i, core):
            return jnp.where(i < tiles, i + core[0] * tiles, i - core[0] * tiles)

        return ordered(
            functools.partial(weight_kernel, count, tiles, len(more)),
            2 * tiles,
            [
                pl.BlockSpec(
                    (part, size),
                    lambda i, core, at=0 if v.shape[0] == part else k: (at, order(i, core)),
                )
                for k, v in enumerate(lhs)
            ]
            + [whole(part, m)] * count
            + [whole(*v.shape) for v in more],
            [
                pl.BlockSpec((size, full), lambda i, core: (jnp.minimum(i, tiles - 1), 0)),
                pl.BlockSpec((size, full), lambda i, core: (jnp.maximum(i - tiles, 0), 0)),
            ],
            [sds((n // 2, full), f32)] * 2,
            flops=CHEAP,
            moved=CHEAP,
            prefetch=1,
            after=after,
        )(core_at, *lhs, *rhs, *more)

    def bit_of(bit):
        return lax.axis_index("rows") // bit % 2

    def core_sum(keep, give):
        return keep + cross(give, 1)

    def pair_sum(v, after):
        n = v.shape[1] // 2
        return late(v[:, :n], after) + swap(v[:, n:].astype(bf16)).astype(f32)

    def chip_sum(v):
        bit = 2
        while bit < nrows:
            size = v.shape[0] // 2
            up = bit_of(bit)
            give = rows_of(v, (1 - up) * size, size)
            v = rows_of(v, up * size, size) + cross(give.astype(bf16), bit).astype(f32)
            bit *= 2
        return lax.reduce_precision(v, 8, 7).astype(bf16)

    def chip_parts(v):
        bit = nrows
        while bit > 2:
            bit //= 2
            got = cross(v, bit)
            low = bit_of(bit) == 0
            v = jnp.concatenate([jnp.where(low, v, got), jnp.where(low, got, v)], axis=0)
        return v

    dz, dy, yn, mtg, scales = ([None] * CHUNKS for _ in range(5))
    dxp, ddt, dsp, near, far, dns = ([None] * CHUNKS for _ in range(6))
    ggs, accs, accs_dt, accs_bc = [], [], [], []
    carry = (jnp.zeros((2, NS, lanes), f32), jnp.zeros((2, 8, lanes), f32), jnp.zeros((8, 128), f32))
    state_carry = (jnp.zeros((8, 128), f32), jnp.zeros((8, 128), f32))

    top = CHUNKS - 1
    d_a, d_b, qs = dyn_step(top)
    scales[top], sq = scales_of(top, qs)
    mixed_1 = line_scatter(out_step(1))

    dz[1], dy[1], yn[1], mtg[1], gg = gate_step(1, sq, d_a, d_b)
    ggs.append(gg)
    dxp[1], ddt[1], dbc_1, mtb_1, acc, acc_dt, *carry = back_step(1, dy[1], *carry)
    accs.append(acc)
    accs_dt.append(acc_dt)
    dns[1] = dn_step(dz[1], dxp[1], ddt[1], dbc_1, after=(mixed_0,))
    total_1 = line_scatter(dns[1], 0)
    d_a, d_b, qs = dyn_step(0)
    scales[0], sq = scales_of(0, qs)
    dz[0], dy[0], yn[0], mtg[0], gg = gate_step(0, sq, d_a, d_b)
    ggs.append(gg)
    g_out = weight_grad(c_all, yn)
    g_z = weight_grad([normed] * CHUNKS, dz)
    dxp[0], ddt[0], dbc_0, mtb_0, acc, acc_dt, *carry = back_step(0, dy[0], *carry)
    accs.append(acc)
    accs_dt.append(acc_dt)
    out_sum, z_sum = core_sum(*g_out), core_sum(*g_z)
    g_x = weight_grad([normed] * CHUNKS, dxp, after=(out_sum, z_sum))
    x_sum = core_sum(*g_x)
    out_sum, z_sum = pair_sum(out_sum, dbc_0), pair_sum(z_sum, dbc_0)
    dns[0] = dn_step(dz[0], dxp[0], ddt[0], dbc_0, after=(out_sum, z_sum))
    total_0 = line_scatter(dns[0], 0)
    x_part = chip_sum(pair_sum(x_sum, total_0))
    dsp[1], mtc_1, acc_bc, *state_carry = states_step(1, total_1, *state_carry)
    accs_bc.append(acc_bc)
    near[1], far[1] = near_step(total_1, dsp[1], dns[0])
    dsp[0], mtc_0, acc_bc, *state_carry = states_step(0, total_0, *state_carry)
    g_x = chip_parts(x_part)
    accs_bc.append(acc_bc)

    width = 2 * cols + heads
    g_few = ordered(
        functools.partial(few_kernel, cols, heads),
        8,
        [pl.BlockSpec((LEN, dim // 8), lambda i, mine: (0, i))] + [whole(CT, 128)] * 4,
        pl.BlockSpec((256, dim // 8), lambda i, mine: (0, i)),
        sds((256, dim), f32),
        [pltpu.VMEM((LEN, 256), bf16)],
        flops=CHEAP,
        moved=CHEAP,
        prefetch=1,
    )(which, normed, dsp[0], dsp[1], ddt[0], ddt[1])
    near[0], far[0] = near_step(total_0, dsp[0], total_0)
    local_sum = [
        mtg[j][:, 0] + m[:, 0] + n[:, 0] for j, m, n in ((0, mtb_0, mtc_0), (1, mtb_1, mtc_1))
    ]
    mean_sum = line_sum(jnp.concatenate(local_sum))
    mixer = jnp.concatenate([mixed_0, mixed_1], axis=0).astype(f32)

    def both_cores(v):
        got = cross(v, 1)
        first = core == 0
        return jnp.concatenate([jnp.where(first, v, got), jnp.where(first, got, v)], axis=0)

    def rows_sum(v):
        bit = 1
        while bit < nrows:
            v = v + cross(v, bit)
            bit *= 2
        return v

    g_z, g_out = (chip_parts(chip_sum(v)) for v in (z_sum, out_sum))
    g_few = rows_sum(g_few[:width] + swap(g_few[128 : 128 + width].astype(bf16)).astype(f32))
    g_out = both_cores(g_out)
    grad_w_out = jnp.concatenate(
        [
            g_out[(q * groups + z) * local_dim : (q * groups + z + 1) * local_dim]
            for z in range(groups)
            for q in range(2)
        ],
        axis=0,
    ).T.astype(f32)
    grad_w_bc = g_few[: 2 * cols].reshape(2, cols, dim).transpose(2, 0, 1)
    grad_w_dt = g_few[2 * cols :].T
    x_far, z_far = cross(g_x, 1), cross(g_z, 1)
    steps = 8
    size = dim // steps
    at = pl.BlockSpec((size, lanes), lambda i, core: (i % (steps // 2), 0))
    grad_w_zx = ordered(
        join_kernel,
        steps,
        [at] * 4,
        pl.BlockSpec((size * 2 * lanes // 128, 128), lambda i, core: (i, 0)),
        sds((dim * 2 * lanes // 128, 128), f32),
        moved=24 << 20,
        prefetch=1,
    )(core_at, g_z, z_far, g_x, x_far)
    grad_w_zx = grad_w_zx.reshape(dim, lanes // 128, 2, 128).transpose(0, 2, 1, 3)
    grad_w_zx = grad_w_zx.reshape(dim, 2, lanes)

    acc = sum(accs).reshape(2, 6, 8, lanes).sum(axis=2)
    gg = sum(ggs).sum(axis=0).reshape(2, 1, lanes)
    acc_dt = sum(accs_dt).reshape(2, 8, 128).sum(axis=1)[:, :docl].reshape(2, 2, heads)
    acc_dt = jnp.pad(acc_dt.transpose(1, 0, 2).reshape(2, 1, -1), ((0, 0), (0, 0), (0, lanes - docl)))
    vec = jnp.concatenate([acc, gg, acc_dt], axis=1)
    acc_bc = sum(accs_bc).reshape(5, 8, 128).sum(axis=1)[:, : 4 * cols]

    vec = rows_sum(vec[0] + swap(vec[1]))
    acc_bc = rows_sum(acc_bc + swap(acc_bc)).reshape(5, 2, 2, cols)
    acc_bc = lax.dynamic_index_in_dim(acc_bc, mine, 2, keepdims=False)

    s_all = jnp.concatenate(scales)
    out_near = mixer * s_all[:, None]
    o_own = lax.dynamic_slice_in_dim(out_near, mine * local_dim, local_dim, 1)
    o_far = swap(
        lax.dynamic_slice_in_dim(out_near, (1 - mine) * local_dim, local_dim, 1).astype(bf16)
    )
    r_own = r_wide[:, 0]
    m_own = mean_sum
    r_far = swap(r_own)
    m_far = swap(m_own)
    d_own = jnp.concatenate(near, axis=0)
    d_far = jnp.concatenate(far, axis=0)
    x_near = lax.dynamic_slice_in_dim(hidden_in, me * local_dim, local_dim, 1).astype(f32)
    gain = lax.dynamic_slice_in_dim(norm_gain, me * local_dim, local_dim, 0)
    outs, grads, gain_sum = [], [], 0.0
    for q in range(2):
        sel = mine == q
        x = x_near[q * LEN : (q + 1) * LEN]
        cot = cotangent[q * LEN : (q + 1) * LEN].astype(f32)
        outs.append((x + jnp.where(sel, o_own, o_far.astype(f32))).astype(bf16))
        d = jnp.where(sel, d_own, d_far.astype(f32))
        r = jnp.where(sel, r_own, r_far)[:, None]
        m = jnp.where(sel, m_own, m_far)[:, None]
        grads.append(cot + r * (d * gain) - x * (r * r) * (m / dim))
        gain_sum = gain_sum + jnp.sum(d * x * r, axis=0)
    return (
        jnp.concatenate(outs, axis=0),
        jnp.concatenate(grads, axis=0),
        rows_sum(gain_sum),
        grad_w_zx,
        grad_w_dt,
        grad_w_bc,
        vec[:4],
        vec[4],
        acc_bc[:4],
        acc_bc[4],
        vec[7, heads : 2 * heads],
        vec[7, :heads],
        vec[5].reshape(heads, HD).sum(axis=1),
        vec[6],
        grad_w_out,
    )


STATE = ("zline", "pair")


def solution(mesh):
    placed = (
        P("rows", None),
        P("rows"),
        P("rows", STATE),
        P(),
        P(None, None, STATE),
        P(None, STATE),
        P(None, None, STATE),
        P(None, STATE),
        P(STATE),
        P(None, None, STATE),
        P(None, STATE),
        P(STATE),
        P(STATE),
        P(STATE),
        P(STATE),
        P(STATE, None),
    )
    rows, parts = mesh.devices.shape
    split = Mesh(mesh.devices.reshape(rows, parts // 2, 2), ("rows", "zline", "pair"))
    return jax.shard_map(
        shards,
        mesh=split,
        in_specs=placed,
        out_specs=(
            P("rows", STATE),
            P("rows", STATE),
            P(STATE),
            P(None, None, STATE),
            P(None, STATE),
            P(None, None, STATE),
            P(None, STATE),
            P(STATE),
            P(None, None, STATE),
            P(None, STATE),
            P(STATE),
            P(STATE),
            P(STATE),
            P(STATE),
            P(STATE, None),
        ),
        check_vma=False,
    )
```
